32 devices in a mesh: groups: 2 (over y), row: 4 (over z), col: 4 (over x, core).
Axes of the slice: x: 2, y: 2, z: 4, core: 2. Of those that a mesh axis runs over, the one named last changes fastest.
Arguments:
- initial_rates: float32 [64, 4608], P('groups', ('row', 'col')), parts along dimension 0, may hold values from -3 to 3
- stimuli: bfloat16 [3, 64, 512], P(None, 'groups'), parts along dimension 1, may hold values from -6 to 6
- cotangent: float32 [3, 64, 4608], P(None, 'groups', ('row', 'col')), parts along dimension 1, may hold values from -0.6 to 0.6
- weight_blocks: bfloat16 [4, 4, 64, 128, 128], P('row', 'col'), may hold values from -0.09375 to 0.09375
- slot_owner: int32 [4, 4, 64], P('row', 'col'), may hold values from 0 to 1
- slot_post: int32 [4, 4, 64], P('row', 'col'), may hold values from 0 to 8
- slot_pre: int32 [4, 4, 64], P('row', 'col'), may hold values from 0 to 8
- cell_type: int32 [4608], P(('row', 'col')), may hold values from 0 to 8191
- type_gain: float32 [8192], replicated, may hold values from 0.5 to 2
- input_map: int32 [4608], P(('row', 'col')), may hold values from 0 to 512
Outputs:
- final_rates: float32 [64, 4608], P('groups', ('row', 'col')), parts along dimension 0
- weight_grads: bfloat16 [4, 4, 128, 128, 128], P('row', 'col', 'groups'), parts along dimension 2
- gain_grads: float32 [16384], P('groups'), parts along dimension 0
The draws below stay inside these ranges and needn't reach their ends.
There are 2 independent parts, one for each index of `groups`. The reference program is written for one: setup_inputs(seed, part) draws one part's arguments, and reference() takes and returns one part's arrays. A program takes and returns all parts, laid end to end along the dimension named above; an argument that names none is the same for every part. Nothing has to cross between parts.
Inputs may be any that keep to these rules, and one draw needn't show every extreme that they name: `slot_owner`: 1: the block belongs to the tile whose row index differs by 2; 0: to the device's own tile. `input_map`: 512 marks a neuron without input.
All inputs are finite; a program needn't handle non-finite values.
Results may differ from the reference program's by a relative error of at most 0.006.
Values may be sent and summed in bfloat16 or wider, within the bound.
No kernel may reach another device: no remote copies, remote signals or barrier semaphores. Data moves between devices by JAX's collectives and lax.ppermute only.
A program may use at most 64 MiB of HBM per device.

```python
import math
import jax
import jax.numpy as jnp
from jax import lax

BLOCK = 128
NL = 288
KS = 64
B = 32
TSTEPS = 3
TYPES = 8192
CH = 512
NEUR = 4608
PB = 9
QB = 9
N_ROW = 4
N_COL = 4


def plant(drawn, key, least, largest):
    extent = drawn.shape
    spot = [jax.random.randint(jax.random.fold_in(key, axis), (), 0, extent[axis]) for axis in range(len(extent))]
    drawn = drawn.at[tuple(spot)].set(least)
    longest = extent.index(max(extent))
    spot[longest] = (spot[longest] + 1) % extent[longest]
    return drawn.at[tuple(spot)].set(largest)


def levels(stream_key, shape, cuts, smallest, top_value):
    def one(axis_at, shards_of):
        steps = jax.random.uniform(jax.random.fold_in(jax.random.fold_in(stream_key, 6), axis_at), (shards_of,), jnp.float32, smallest / len(cuts), top_value / len(cuts))
        return jnp.repeat(jnp.exp(steps), shape[axis_at] // shards_of).reshape((-1,) + (1,) * (len(shape) - axis_at - 1))

    loudness = one(*cuts[0])
    for cut in cuts[1:]:
        loudness = loudness * one(*cut)
    return loudness


def scatter_about(stream_key, dims, spread, bound, pieces=(), kind=jnp.bfloat16):
    level = levels(stream_key, dims, pieces, -0.22, 0.18) if pieces else 1.0
    values = jax.random.normal(stream_key, dims, jnp.float32) * spread * level
    return jnp.minimum(jnp.maximum(values, -bound), bound).astype(kind)


def setup_inputs(seed: int = 0, part: int = 0) -> dict:
    key_of = jax.random.split(jax.random.key(seed), 11)
    own_keys = jax.random.split(jax.random.fold_in(key_of[10], part), 11)
    return {
        "initial_rates": scatter_about(own_keys[0], (B, NEUR), 0.5, 3.0, ((1, 16),), jnp.float32),
        "stimuli": scatter_about(own_keys[1], (TSTEPS, B, CH), 1.0, 6.0),
        "cotangent": scatter_about(own_keys[2], (TSTEPS, B, NEUR), 0.1, 0.6, ((2, 16),), jnp.float32),
        "weight_blocks": scatter_about(key_of[3], (N_ROW, N_COL, KS, BLOCK, BLOCK), (KS * 16384 // NL) ** -0.5, 0.09375, ((0, 4), (1, 4))),
        "slot_owner": plant(jax.random.randint(key_of[4], (N_ROW, N_COL, KS), 0, 2), jax.random.fold_in(key_of[4], 1), 0, 1).astype(jnp.int32),
        "slot_post": plant(jax.random.randint(key_of[5], (N_ROW, N_COL, KS), 0, PB), jax.random.fold_in(key_of[5], 1), 0, PB - 1).astype(jnp.int32),
        "slot_pre": plant(jax.random.randint(key_of[6], (N_ROW, N_COL, KS), 0, QB), jax.random.fold_in(key_of[6], 1), 0, QB - 1).astype(jnp.int32),
        "cell_type": plant(jax.random.randint(key_of[7], (NEUR,), 0, TYPES), jax.random.fold_in(key_of[7], 1), 0, TYPES - 1).astype(jnp.int32),
        "type_gain": jnp.clip(jnp.exp(jax.random.uniform(key_of[8], (TYPES,), jnp.float32, math.log(0.5), math.log(2.0))), 0.5, 2.0),
        "input_map": plant(jax.random.randint(key_of[9], (NEUR,), 0, CH + 1), jax.random.fold_in(key_of[9], 1), 0, CH).astype(jnp.int32),
    }


def reference(initial_rates, stimuli, cotangent, weight_blocks, slot_owner, slot_post, slot_pre, cell_type, type_gain, input_map):
    device_count = N_ROW * N_COL
    block_total = NEUR // BLOCK
    weight_all = weight_blocks.reshape(device_count, KS, BLOCK, BLOCK)
    device_ids = jnp.arange(device_count, dtype=jnp.int32)
    row_ids = device_ids // N_COL
    col_ids = device_ids % N_COL
    owner_rows = jnp.bitwise_xor(row_ids[:, None], slot_owner.reshape(device_count, KS) * (N_ROW // 2))
    global_post = (owner_rows * PB + slot_post.reshape(device_count, KS)).astype(jnp.int32)
    local_pre = slot_pre.reshape(device_count, KS).astype(jnp.int32)
    neuron_gain = type_gain[cell_type]
    padded = jnp.concatenate([stimuli, jnp.zeros((TSTEPS, B, 1), jnp.bfloat16)], axis=2)
    drive = padded[:, :, input_map].astype(jnp.float32)

    def to_sets(values):
        return values.reshape(B, N_ROW, N_COL, NL).transpose(0, 2, 1, 3).reshape(B, N_COL, QB, BLOCK)

    def from_sets(values):
        return values.reshape(B, N_COL, N_ROW, NL).transpose(0, 2, 1, 3).reshape(B, NEUR)

    def forward_currents(lowered):
        presets = to_sets(lowered)

        def one_device(total, inputs):
            weights, post_ids, column, pre_ids = inputs
            picked = presets[:, column][:, pre_ids].astype(jnp.float32)
            product = jnp.einsum('kij,bkj->bki', weights.astype(jnp.float32), picked)
            return total.at[:, post_ids].add(product), None

        total, _ = lax.scan(one_device, jnp.zeros((B, block_total, BLOCK), jnp.float32), (weight_all, global_post, col_ids, local_pre))
        return total.reshape(B, NEUR)

    def backward_currents(delta):
        post_sets = delta.reshape(B, block_total, BLOCK)

        def one_device(total, inputs):
            weights, post_ids, column, pre_ids = inputs
            picked = post_sets[:, post_ids].astype(jnp.float32)
            product = jnp.einsum('kij,bki->bkj', weights.astype(jnp.float32), picked)
            return total.at[:, column, pre_ids].add(product), None

        total, _ = lax.scan(one_device, jnp.zeros((B, N_COL, QB, BLOCK), jnp.float32), (weight_all, global_post, col_ids, local_pre))
        return from_sets(total)

    state_rates = initial_rates
    lowered_list, current_list, activity_list = [], [], []
    for time_index in range(TSTEPS):
        lowered = state_rates.astype(jnp.bfloat16)
        current = forward_currents(lowered) + drive[time_index]
        activity = jnp.tanh(neuron_gain[None, :] * current)
        state_rates = 0.5 * state_rates + 0.5 * activity
        lowered_list.append(lowered)
        current_list.append(current)
        activity_list.append(activity)

    adjoint = cotangent[TSTEPS - 1]
    gain_sums = jnp.zeros((NEUR,), jnp.float32)
    delta_list = [None] * TSTEPS
    for time_index in reversed(range(TSTEPS)):
        activity = activity_list[time_index]
        pressure = adjoint * 0.5 * (1.0 - activity * activity)
        delta = (pressure * neuron_gain[None, :]).astype(jnp.bfloat16)
        gain_sums = gain_sums + jnp.sum(pressure * current_list[time_index], axis=0)
        delta_list[time_index] = delta
        if time_index > 0:
            adjoint = cotangent[time_index - 1] + 0.5 * adjoint + backward_currents(delta)

    pre_all = jnp.stack([to_sets(item) for item in lowered_list])
    delta_all = jnp.stack([item.reshape(B, block_total, BLOCK) for item in delta_list])

    def grad_device(carry, inputs):
        post_ids, column, pre_ids = inputs
        presyn = pre_all[:, :, column][:, :, pre_ids].astype(jnp.float32)
        postsyn = delta_all[:, :, post_ids].astype(jnp.float32)
        grads = jnp.einsum('tbki,tbkj->kij', postsyn, presyn)
        return carry, grads.astype(jnp.bfloat16)

    _, weight_grads = lax.scan(grad_device, jnp.zeros((), jnp.float32), (global_post, col_ids, local_pre))
    weight_grads = weight_grads.reshape(N_ROW, N_COL, KS, BLOCK, BLOCK)
    gain_grads = jax.ops.segment_sum(gain_sums, cell_type, num_segments=TYPES)
    return state_rates, weight_grads, gain_grads
```

```python
import functools

import jax
import jax.numpy as jnp
from jax import lax
from jax.experimental import pallas as pl
from jax.experimental.pallas import tpu as pltpu
from jax.sharding import PartitionSpec as P

BLOCK = 128
EXTRA = 16
F32 = jnp.float32
BF16 = jnp.bfloat16
VMEM = pl.BlockSpec(memory_space=pltpu.VMEM)
SMEM = pl.BlockSpec(memory_space=pltpu.SMEM)


class Sizes:
    def __init__(self, row_count, col_count, batch, local, slots, types, channels, steps):
        self.rows, self.cols = row_count, col_count
        self.batch, self.local, self.slots = batch, local, slots
        self.types, self.channels, self.steps = types, channels, steps
        self.post = col_count * local // BLOCK
        self.pre = row_count * local // BLOCK
        self.half = row_count // 2
        offsets = [local * i % BLOCK for i in range(max(row_count, col_count))]
        self.frame = (max(offsets) + local + BLOCK - 1) // BLOCK
        self.wide = self.frame * BLOCK

    def first(self, i):
        return lax.div(i * self.local, jnp.int32(BLOCK))

    def offset(self, i):
        return lax.rem(i * self.local, jnp.int32(BLOCK))


def call(body, outs, scratch, ins, smem=(), flops=0):
    specs = [SMEM if i in smem else VMEM for i in range(len(ins))]
    moved = sum(x.size * x.dtype.itemsize for x in ins) + sum(x.size * x.dtype.itemsize for x in outs)
    return pl.pallas_call(
        body,
        out_shape=outs,
        in_specs=specs,
        out_specs=[VMEM] * len(outs),
        scratch_shapes=scratch,
        cost_estimate=pl.CostEstimate(flops=flops, bytes_accessed=moved, transcendentals=0),
        compiler_params=pltpu.CompilerParams(vmem_limit_bytes=32 * 1024 * 1024),
    )(*ins)


def shape(dims, kind=F32):
    return jax.ShapeDtypeStruct(tuple(dims), kind)


def flip(x, axis, k):
    count = lax.axis_size(axis)
    return lax.ppermute(x, axis, [(i, i ^ k) for i in range(count)])


def few(count):
    return count <= 4


def share(x, axis):
    count = lax.axis_size(axis)
    if few(count):
        return [x] + [flip(x, axis, k) for k in range(1, count)]
    return [lax.all_gather(x, axis)]


def exchange(parts, axis):
    count = lax.axis_size(axis)
    if few(count):
        return [parts[0]] + [flip(parts[k], axis, k) for k in range(1, count)]
    return [lax.all_to_all(parts[0], axis, 0, 0, tiled=True)]


def parcel(count, dims, kind):
    if few(count):
        return [shape(dims, kind)] * count
    return [shape((count, *dims), kind)]


def slot_of(refs, count, me, k):
    return refs[k] if few(count) else refs[0].at[me ^ k]


def loop(count, body):
    lax.fori_loop(0, count, lambda i, c: (body(i), c)[1], 0, unroll=count <= 8)


def rotated(blocks, amount, z):
    whole = jnp.concatenate(blocks, axis=1)
    return pltpu.roll(whole, lax.rem(amount + z.wide, jnp.int32(z.wide)), 1)


def cut(whole, z):
    return [whole[:, i * BLOCK : (i + 1) * BLOCK] for i in range(z.frame)]


def pack_kernel(z, meta, rates, types, inputs, cots, message, own, cot_frames, pad):
    p = meta[2 * z.slots]
    offset = z.offset(p)
    pad[...] = jnp.zeros_like(pad)
    n = z.batch
    pad[0:n, 0 : z.local] = rates[...]
    t, m = types[...], inputs[...]
    pad[n : n + 1, 0 : z.local] = (lax.shift_right_logical(t, 7) + 1).astype(F32)
    pad[n + 1 : n + 2, 0 : z.local] = (t & 127).astype(F32)
    pad[n + 2 : n + 3, 0 : z.local] = (lax.shift_right_logical(m, 7) + 1).astype(F32)
    pad[n + 3 : n + 4, 0 : z.local] = (m & 127).astype(F32)
    moved = pltpu.roll(pad[...], offset, 1)
    for f, block in enumerate(cut(moved, z)):
        message[f] = block.astype(BF16)
        own[f] = block[0:n]
    pad[...] = jnp.zeros_like(pad)
    for t in range(z.steps):
        pad[0:n, 0 : z.local] = cots[t]
        moved = pltpu.roll(pad[...], offset, 1)
        for f, block in enumerate(cut(moved, z)):
            cot_frames[t, f] = block[0:n]


def prepare_kernel(z, aux, table, stimuli, gain, drive):
    highs = z.types // BLOCK
    t = jnp.transpose(table[...])
    t1 = t.astype(BF16)
    t2 = (t - t1.astype(F32)).astype(BF16)
    t3 = (t - t1.astype(F32) - t2.astype(F32)).astype(BF16)
    tables = [t1, t2, t3]
    high_ids = lax.broadcasted_iota(jnp.int32, (highs, BLOCK), 0).astype(F32) + 1.0
    low_ids = lax.broadcasted_iota(jnp.int32, (BLOCK, BLOCK), 0).astype(F32)
    channel_ids = lax.broadcasted_iota(jnp.int32, (z.channels, BLOCK), 0).astype(F32)
    stim = stimuli[...]

    def one(a):
        for f in range(z.frame):
            codes = aux[a, f].astype(F32)
            pick = (high_ids == codes[0:1]).astype(BF16)
            rows = sum(jnp.dot(x, pick, preferred_element_type=F32) for x in tables)
            mine = jnp.where(low_ids == codes[1:2], rows, 0.0)
            gain[a, f] = jnp.broadcast_to(jnp.sum(mine, axis=0, keepdims=True), (8, BLOCK))
            channel = (codes[2:3] - 1.0) * BLOCK + codes[3:4]
            chosen = (channel_ids == channel).astype(BF16)
            got = jnp.dot(stim, chosen, preferred_element_type=F32)
            for step in range(z.steps):
                drive[step, a, f] = got[step * z.batch : (step + 1) * z.batch].astype(BF16)

    loop(z.rows, one)


def multiply_forward(z, meta, weights, x, total, parts):
    c = meta[2 * z.slots + 1]
    total[...] = jnp.zeros_like(total)
    for s in range(z.slots):
        total[meta[s]] += lax.dot_general(
            x[meta[z.slots + s]], weights[s], (((1,), (1,)), ((), ())), preferred_element_type=F32
        )
    for k in range(z.cols):
        ref = slot_of(parts, z.cols, c, k)
        first = z.first(c ^ k)
        for f in range(z.frame):
            ref[0, f] = total[first + f].astype(BF16)
            ref[1, f] = total[z.post + first + f].astype(BF16)


def gather_pre(z, rates, sums, x):
    sums[...] = jnp.zeros_like(sums)

    def one(a):
        first = z.first(a)
        for f in range(z.frame):
            sums[first + f] += rates[a, f]

    loop(z.rows, one)
    x[...] = sums[...].astype(BF16)


def first_kernel(z, count, *refs):
    meta, weights, own = refs[:3]
    got = refs[3 : 3 + count]
    rates, aux, x = refs[3 + count : 6 + count]
    parts, (sums, total) = refs[6 + count : -2], refs[-2:]
    p = meta[2 * z.slots]
    for k in range(z.rows):
        ref = slot_of(got, z.rows, p, k)
        for f in range(z.frame):
            rates[p ^ k, f] = ref[f, 0 : z.batch].astype(F32)
            aux[p ^ k, f] = ref[f, z.batch :]
    rates[p] = own[...]
    gather_pre(z, rates, sums, x)
    multiply_forward(z, meta, weights, x, total, parts)


def sum_kernel(z, count, *refs):
    meta = refs[0]
    got = refs[1 : 1 + count]
    rest, out = refs[1 + count : -1], refs[-1]
    p, c = meta[2 * z.slots], meta[2 * z.slots + 1]
    begin = z.offset(c)
    lanes = lax.broadcasted_iota(jnp.int32, (z.batch, z.wide), 1)
    keep = (lanes >= begin) & (lanes < begin + z.local)
    for piece in range(2):
        blocks = []
        for f in range(z.frame):
            total = slot_of(got, z.cols, c, 0)[piece, f].astype(F32)
            for k in range(1, z.cols):
                total = total + slot_of(got, z.cols, c, k)[piece, f].astype(F32)
            blocks.append(total)
        whole = jnp.where(keep, jnp.concatenate(blocks, axis=1), 0.0)
        target = p ^ (piece * z.half)
        turned = pltpu.roll(whole, lax.rem(z.offset(target) - begin + z.wide, jnp.int32(z.wide)), 1)
        for f, block in enumerate(cut(turned, z)):
            out[piece, f] = block.astype(BF16)
    for cot in rest:
        for f in range(z.frame):
            out[2, f] = cot[f].astype(BF16)


def next_kernel(z, count, *refs):
    meta, weights, rates, gain, drive = refs[:5]
    got = refs[5 : 5 + count]
    new, act_pair, cur_pair, x = refs[5 + count : 9 + count]
    parts, (stack, acts, curs, sums, total) = refs[9 + count : -5], refs[-5:]
    p = meta[2 * z.slots]
    if few(z.rows):
        for k in range(z.rows):
            stack[p ^ k] = got[k][...]
        source = stack
    else:
        source = got[0]

    def one(a):
        for f in range(z.frame):
            current = (
                source[a, 0, f].astype(F32)
                + source[a ^ z.half, 1, f].astype(F32)
                + drive[a, f].astype(F32)
            )
            activity = jnp.tanh(gain[a, f, 0:1] * current)
            new[a, f] = 0.5 * rates[a, f] + 0.5 * activity
            curs[a, f] = current
            acts[a, f] = activity

    loop(z.rows, one)
    for piece in range(2):
        act_pair[piece] = acts[p ^ (piece * z.half)]
        cur_pair[piece] = curs[p ^ (piece * z.half)]
    gather_pre(z, new, sums, x)
    multiply_forward(z, meta, weights, x, total, parts)


def push_delta(z, p, c, piece, pressures, gain, message):
    row = p ^ (piece * z.half)
    blocks = [pressures[f] * gain[row, f, 0:1] for f in range(z.frame)]
    whole = jnp.concatenate(blocks, axis=1)
    amount = z.offset(c) - z.offset(row) + z.wide
    turned = pltpu.roll(whole, lax.rem(amount, jnp.int32(z.wide)), 1)
    for f, block in enumerate(cut(turned, z)):
        message[piece, f, 0 : z.batch] = block.astype(BF16)


def turn_kernel(z, meta, rates, gain, drive, mine, theirs, cots, final, act_pair, message, gains, base):
    p, c = meta[2 * z.slots], meta[2 * z.slots + 1]
    for piece in range(2):
        row = p ^ (piece * z.half)
        first, second = (mine, theirs) if piece == 0 else (theirs, mine)
        pressures, blocks = [], []
        for f in range(z.frame):
            current = first[0, f].astype(F32) + second[1, f].astype(F32) + drive[row, f].astype(F32)
            activity = jnp.tanh(gain[row, f, 0:1] * current)
            act_pair[piece, f] = activity
            adjoint = cots[z.steps - 1, f] if piece == 0 else theirs[2, f].astype(F32)
            pressure = adjoint * 0.5 * (1.0 - activity * activity)
            pressures.append(pressure)
            gains[piece, f] = jnp.broadcast_to(
                jnp.sum(pressure * current, axis=0, keepdims=True), (8, BLOCK)
            )
            if piece == 0:
                blocks.append(0.5 * rates[p, f] + 0.5 * activity)
                base[f] = cots[z.steps - 2, f] + 0.5 * adjoint
        push_delta(z, p, c, piece, pressures, gain, message)
        if piece == 0:
            back = pltpu.roll(
                jnp.concatenate(blocks, axis=1),
                lax.rem(z.wide - z.offset(p), jnp.int32(z.wide)),
                1,
            )
            final[...] = back[:, 0 : z.local]


def gather_post(z, c, got, sums, d):
    sums[...] = jnp.zeros_like(sums)
    for k in range(z.cols):
        ref = slot_of(got, z.cols, c, k)
        first = z.first(c ^ k)
        for f in range(z.frame):
            sums[first + f] += ref[0, f, 0 : z.batch].astype(F32)
            sums[z.post + first + f] += ref[1, f, 0 : z.batch].astype(F32)
    d[...] = sums[...].astype(BF16)


def back_kernel(z, count, *refs):
    meta, weights, base = refs[:3]
    got = refs[3 : 3 + count]
    d = refs[3 + count]
    parts, (sums, total) = refs[4 + count : -2], refs[-2:]
    p, c = meta[2 * z.slots], meta[2 * z.slots + 1]
    gather_post(z, c, got, sums, d)
    total[...] = jnp.zeros_like(total)
    for s in range(z.slots):
        total[meta[z.slots + s]] += jnp.dot(d[meta[s]], weights[s], preferred_element_type=F32)
    for k in range(z.rows):
        ref = slot_of(parts, z.rows, p, k)
        row = p ^ k
        first, other = z.first(row), z.first(row ^ z.half)
        for f in range(z.frame):
            ref[0, f] = total[first + f].astype(BF16)
            block = total[other + f]
            if k == z.half:
                block = block + base[f]
            ref[1, f] = block.astype(BF16)


def delta_kernel(z, count, last, *refs):
    meta, gain, base, act_pair, cur_pair, gains_in, tail = refs[:7]
    got = refs[7 : 7 + count]
    message, tally, base_out = refs[7 + count :]
    p, c = meta[2 * z.slots], meta[2 * z.slots + 1]
    for piece in range(2):
        row = p ^ (piece * z.half)
        pressures = []
        for f in range(z.frame):
            adjoint = slot_of(got, z.rows, p, 0)[piece, f].astype(F32)
            for k in range(1, z.rows):
                adjoint = adjoint + slot_of(got, z.rows, p, k)[piece, f].astype(F32)
            if piece == 0:
                adjoint = adjoint + base[f]
                base_out[f] = tail[f] + 0.5 * adjoint
            activity = act_pair[piece, f]
            pressure = adjoint * 0.5 * (1.0 - activity * activity)
            pressures.append(pressure)
            gained = gains_in[piece, f] + jnp.sum(
                pressure * cur_pair[piece, f], axis=0, keepdims=True
            )
            tally[piece, f] = gained
        push_delta(z, p, c, piece, pressures, gain, message)


def last_delta_kernel(z, count, *refs):
    meta, gain, base, act_pair, cur_pair, gains_in, aux = refs[:7]
    got = refs[7 : 7 + count]
    message = refs[7 + count]
    p, c = meta[2 * z.slots], meta[2 * z.slots + 1]
    rows = lax.broadcasted_iota(jnp.int32, (EXTRA, BLOCK), 0)
    for piece in range(2):
        row = p ^ (piece * z.half)
        pressures = []
        for f in range(z.frame):
            adjoint = slot_of(got, z.rows, p, 0)[piece, f].astype(F32)
            for k in range(1, z.rows):
                adjoint = adjoint + slot_of(got, z.rows, p, k)[piece, f].astype(F32)
            if piece == 0:
                adjoint = adjoint + base[f]
            activity = act_pair[piece, f]
            pressure = adjoint * 0.5 * (1.0 - activity * activity)
            pressures.append(pressure)
            sums = jnp.sum(pressure * cur_pair[piece, f], axis=0, keepdims=True)
            g = gains_in[piece, f, 0:1] + sums
            g1 = g.astype(BF16).astype(F32)
            g2 = (g - g1).astype(BF16).astype(F32)
            g3 = g - g1 - g2
            codes = aux[row, f].astype(F32)
            tail = jnp.where(rows == 2, g1, codes)
            tail = jnp.where(rows == 3, g2, tail)
            tail = jnp.where(rows == 4, g3, tail)
            message[piece, f, z.batch :] = tail.astype(BF16)
        push_delta(z, p, c, piece, pressures, gain, message)


def table_kernel(z, count, *refs):
    meta, got, out = refs[0], refs[1:-1], refs[-1]
    c = meta[2 * z.slots + 1]
    highs = z.types // BLOCK
    high_ids = lax.broadcasted_iota(jnp.int32, (highs, BLOCK), 0).astype(F32) + 1.0
    low_ids = lax.broadcasted_iota(jnp.int32, (BLOCK, BLOCK), 0).astype(F32)
    total = jnp.zeros((3 * highs, BLOCK), F32)
    for k in range(z.cols):
        ref = slot_of(got, z.cols, c, k)
        for piece in range(2):
            for f in range(z.frame):
                codes = ref[piece, f, z.batch :].astype(F32)
                hit = high_ids == codes[0:1]
                terms = [jnp.where(hit, codes[2 + i : 3 + i], 0.0) for i in range(3)]
                left = jnp.concatenate(terms, axis=0).astype(BF16)
                right = (low_ids == codes[1:2]).astype(BF16)
                total = total + lax.dot_general(
                    left, right, (((1,), (1,)), ((), ())), preferred_element_type=F32
                )
    out[...] = total[0:highs] + total[highs : 2 * highs] + total[2 * highs :]


def grad_kernel(z, count, per_step, *refs):
    meta = refs[0]
    xs = refs[1 : 1 + z.steps]
    ds = refs[1 + z.steps : z.steps + z.steps]
    got = refs[2 * z.steps : 2 * z.steps + count]
    out = refs[2 * z.steps + count]
    sums, d0, right, left = refs[2 * z.steps + count + 1 :]
    n = z.batch

    @pl.when(pl.program_id(0) == 0)
    def _():
        c = meta[2 * z.slots + 1]
        gather_post(z, c, got, sums, d0)

        def lay_right(q):
            for t in range(z.steps):
                right[q, t * n : (t + 1) * n] = xs[t][q]

        loop(z.pre, lay_right)

        def lay_left(q):
            parts = [d0[q]] + [d[q] for d in ds]
            whole = jnp.concatenate([x.astype(F32) for x in parts], axis=0)
            left[q] = jnp.transpose(whole).astype(BF16)

        loop(2 * z.post, lay_left)

    begin = pl.program_id(0) * per_step
    for s in range(per_step):
        product = jnp.dot(
            left[meta[begin + s]], right[meta[z.slots + begin + s]], preferred_element_type=F32
        )
        out[s] = product.astype(BF16)


def shards(
    initial_rates,
    stimuli,
    cotangent,
    weight_blocks,
    slot_owner,
    slot_post,
    slot_pre,
    cell_type,
    type_gain,
    input_map,
):
    batch, local = initial_rates.shape
    slots = weight_blocks.shape[2]
    steps, _, channels = stimuli.shape
    types = type_gain.shape[0]
    z = Sizes(
        lax.axis_size("row"), lax.axis_size("col"), batch, local, slots, types, channels, steps
    )
    weights = weight_blocks.reshape(slots, BLOCK, BLOCK)
    place = jnp.stack([lax.axis_index("row"), lax.axis_index("col")]).astype(jnp.int32)
    meta = jnp.concatenate(
        [slot_owner.reshape(slots) * z.post + slot_post.reshape(slots), slot_pre.reshape(slots), place]
    )
    frame = (z.frame, batch, BLOCK)
    product_flops = 2 * slots * batch * BLOCK * BLOCK

    message, own, cots = call(
        functools.partial(pack_kernel, z),
        [
            shape((z.frame, batch + EXTRA, BLOCK), BF16),
            shape(frame),
            shape((steps, *frame)),
        ],
        [pltpu.VMEM((batch + EXTRA, z.wide), F32)],
        [meta, initial_rates, cell_type.reshape(1, local), input_map.reshape(1, local), cotangent],
        smem=(0,),
    )
    got = share(message, "row")
    col_parts = parcel(z.cols, (2, *frame), BF16)
    row_parts = parcel(z.rows, (2, *frame), BF16)
    pre_sums = pltpu.VMEM((z.pre, batch, BLOCK), F32)
    post_sums = pltpu.VMEM((2 * z.post, batch, BLOCK), F32)
    rates, aux, x, *parts = call(
        functools.partial(first_kernel, z, len(got)),
        [
            shape((z.rows, *frame)),
            shape((z.rows, z.frame, EXTRA, BLOCK), BF16),
            shape((z.pre, batch, BLOCK), BF16),
            *col_parts,
        ],
        [pre_sums, post_sums],
        [meta, weights, own, *got],
        smem=(0,),
        flops=product_flops,
    )
    gain, drive = call(
        functools.partial(prepare_kernel, z),
        [shape((z.rows, z.frame, 8, BLOCK)), shape((steps, z.rows, *frame), BF16)],
        [],
        [aux, type_gain.reshape(types // BLOCK, BLOCK), stimuli.reshape(steps * batch, channels)],
    )
    xs, acts, curs = [x], [], []
    for t in range(steps):
        got = exchange(parts, "col")
        last = t == steps - 1
        tail = [cots[steps - 1]] if last else []
        (sums,) = call(
            functools.partial(sum_kernel, z, len(got)),
            [shape((2 + len(tail), *frame), BF16)],
            [],
            [meta, *got, *tail],
            smem=(0,),
        )
        if last:
            break
        got = share(sums, "row")
        rates, act, cur, x, *parts = call(
            functools.partial(next_kernel, z, len(got)),
            [
                shape((z.rows, *frame)),
                shape((2, *frame)),
                shape((2, *frame)),
                shape((z.pre, batch, BLOCK), BF16),
                *col_parts,
            ],
            [
                pltpu.VMEM((z.rows, 2, *frame), BF16),
                pltpu.VMEM((z.rows, *frame), F32),
                pltpu.VMEM((z.rows, *frame), F32),
                pre_sums,
                post_sums,
            ],
            [meta, weights, rates, gain, drive[t], *got],
            smem=(0,),
            flops=product_flops,
        )
        xs.append(x)
        acts.append(act)
        curs.append(cur)
    theirs = flip(sums, "row", z.half)
    final_rates, _, message, gains, base = call(
        functools.partial(turn_kernel, z),
        [
            shape((batch, local)),
            shape((2, *frame)),
            shape((2, *frame), BF16),
            shape((2, z.frame, 8, BLOCK)),
            shape(frame),
        ],
        [],
        [meta, rates, gain, drive[steps - 1], sums, theirs, cots],
        smem=(0,),
    )
    ds = []
    for t in reversed(range(1, steps)):
        got = share(message, "col")
        d, *parts = call(
            functools.partial(back_kernel, z, len(got)),
            [shape((2 * z.post, batch, BLOCK), BF16), *row_parts],
            [post_sums, pre_sums],
            [meta, weights, base, *got],
            smem=(0,),
            flops=product_flops,
        )
        ds.insert(0, d)
        got = exchange(parts, "row")
        before = t - 1
        if before > 0:
            message, gains, base = call(
                functools.partial(delta_kernel, z, len(got), False),
                [shape((2, *frame), BF16), shape((2, z.frame, 8, BLOCK)), shape(frame)],
                [],
                [meta, gain, base, acts[before], curs[before], gains, cots[before - 1], *got],
                smem=(0,),
            )
        else:
            (message,) = call(
                functools.partial(last_delta_kernel, z, len(got)),
                [shape((2, z.frame, batch + EXTRA, BLOCK), BF16)],
                [],
                [meta, gain, base, acts[0], curs[0], gains, aux, *got],
                smem=(0,),
            )
    got = share(message, "col")
    (table,) = call(
        functools.partial(table_kernel, z, len(got)),
        [shape((types // BLOCK, BLOCK))],
        [],
        [meta, *got],
        smem=(0,),
    )
    if z.rows == 4:
        table = table + flip(table, "row", 1)
    else:
        table = 0.5 * lax.psum(table, "row")
    gain_grads = table.reshape(types)

    grid = 4
    per_step = slots // grid
    deep = steps * batch
    ins = [meta, *xs, *ds, *got]
    weight_grads = pl.pallas_call(
        functools.partial(grad_kernel, z, len(got), per_step),
        grid=(grid,),
        out_shape=shape((slots, BLOCK, BLOCK), BF16),
        in_specs=[SMEM] + [VMEM] * (len(ins) - 1),
        out_specs=pl.BlockSpec((per_step, BLOCK, BLOCK), lambda i: (i, 0, 0)),
        scratch_shapes=[
            post_sums,
            pltpu.VMEM((2 * z.post, batch, BLOCK), BF16),
            pltpu.VMEM((z.pre, deep, BLOCK), BF16),
            pltpu.VMEM((2 * z.post, BLOCK, deep), BF16),
        ],
        cost_estimate=pl.CostEstimate(
            flops=2 * slots * deep * BLOCK * BLOCK, bytes_accessed=4 * 1024 * 1024, transcendentals=0
        ),
        compiler_params=pltpu.CompilerParams(vmem_limit_bytes=32 * 1024 * 1024),
    )(*ins)
    return (final_rates, weight_grads.reshape(1, 1, slots, BLOCK, BLOCK), gain_grads)


def solution(mesh):
    in_specs = (
        P("groups", ("row", "col")),
        P(None, "groups", None),
        P(None, "groups", ("row", "col")),
        P("row", "col", None, None, None),
        P("row", "col", None),
        P("row", "col", None),
        P("row", "col", None),
        P(("row", "col")),
        P(),
        P(("row", "col")),
    )
    out_specs = (P("groups", ("row", "col")), P("row", "col", "groups", None, None), P("groups"))
    return jax.shard_map(shards, mesh=mesh, in_specs=in_specs, out_specs=out_specs, check_vma=False)
```

```python
import functools

import jax
import jax.numpy as jnp
from jax import lax
from jax.experimental import pallas as pl
from jax.experimental.pallas import tpu as pltpu
from jax.sharding import PartitionSpec as P

BLOCK = 128
CODES = 16
F32 = jnp.float32
BF16 = jnp.bfloat16
VMEM = pl.BlockSpec(memory_space=pltpu.VMEM)
SMEM = pl.BlockSpec(memory_space=pltpu.SMEM)
ANY = pl.BlockSpec(memory_space=pl.ANY)


class Sizes:
    def __init__(self, row_count, col_count, batch, local, slots, types, channels, steps):
        self.rows, self.cols = row_count, col_count
        self.batch, self.local, self.slots = batch, local, slots
        self.types, self.channels, self.steps = types, channels, steps
        self.post = col_count * local // BLOCK
        self.pre = row_count * local // BLOCK
        self.half = row_count // 2
        self.full, self.rest = local // BLOCK, local % BLOCK
        self.groups = BLOCK // self.rest
        self.tall = batch // self.groups
        self.piece = self.full * batch + self.tall
        self.pair = 2 * self.piece
        offsets = [local * i % BLOCK for i in range(max(row_count, col_count))]
        self.frame = (max(offsets) + local + BLOCK - 1) // BLOCK
        self.wide = self.frame * BLOCK
        assert BLOCK % self.rest == 0 and batch % (8 * self.groups) == 0
        assert self.frame == self.full + 1 and self.pair % 16 == 0

    def first(self, i):
        return lax.div(i * self.local, jnp.int32(BLOCK))

    def offset(self, i):
        return lax.rem(i * self.local, jnp.int32(BLOCK))

    def pack(self, whole):
        parts = [whole[:, i * BLOCK : (i + 1) * BLOCK] for i in range(self.full)]
        tail = whole[:, self.full * BLOCK :]
        lanes = lax.broadcasted_iota(jnp.int32, (self.tall, BLOCK), 1)
        joined = tail[0 : self.tall]
        for g in range(1, self.groups):
            moved = pltpu.roll(tail[g * self.tall : (g + 1) * self.tall], g * self.rest, 1)
            joined = jnp.where(lanes < g * self.rest, joined, moved)
        return jnp.concatenate(parts + [joined], axis=0)

    def unpack(self, piece):
        parts = [piece[i * self.batch : (i + 1) * self.batch] for i in range(self.full)]
        joined = piece[self.full * self.batch :]
        lanes = lax.broadcasted_iota(jnp.int32, (self.tall, BLOCK), 1)
        tails = []
        for g in range(self.groups):
            moved = joined if g == 0 else pltpu.roll(joined, BLOCK - g * self.rest, 1)
            tails.append(jnp.where(lanes < self.rest, moved, 0.0))
        return jnp.concatenate(parts + [jnp.concatenate(tails, axis=0)], axis=1)

    def add_blocks(self, target, base, i, piece):
        turned = pltpu.roll(self.unpack(piece), self.offset(i), 1)
        first = base + self.first(i)
        for f in range(self.frame):
            target[first + f] += turned[:, f * BLOCK : (f + 1) * BLOCK]

    def take_blocks(self, source, base, i):
        first = base + self.first(i)
        whole = jnp.concatenate([source[first + f] for f in range(self.frame)], axis=1)
        back = lax.rem(self.wide - self.offset(i), jnp.int32(self.wide))
        return self.pack(pltpu.roll(whole, back, 1))


def call(body, outs, scratch, ins, places=None, flops=0, out_specs=None):
    specs = [(places or {}).get(i, VMEM) for i in range(len(ins))]
    moved = sum(x.size * x.dtype.itemsize for x in ins) + sum(x.size * x.dtype.itemsize for x in outs)
    return pl.pallas_call(
        body,
        out_shape=outs,
        in_specs=specs,
        out_specs=out_specs or [VMEM] * len(outs),
        scratch_shapes=scratch,
        cost_estimate=pl.CostEstimate(flops=flops, bytes_accessed=moved, transcendentals=0),
        compiler_params=pltpu.CompilerParams(vmem_limit_bytes=24 * 1024 * 1024),
    )(*ins)


def shape(dims, kind=F32):
    return jax.ShapeDtypeStruct(tuple(dims), kind)


def flip(x, axis, k):
    count = lax.axis_size(axis)
    return lax.ppermute(x, axis, [(i, i ^ k) for i in range(count)])


def few(count):
    return count <= 4


def near(axis, count):
    size = lax.axis_size(axis)
    return [list(range(i, i + count)) for i in range(0, size, count)]


def share(x, axis, count):
    if few(count):
        return [flip(x, axis, k) for k in range(1, count)]
    return [lax.all_gather(x, axis, axis_index_groups=near(axis, count))]


def exchange(parts, axis, count):
    if few(count):
        return [flip(parts[k - 1], axis, k) for k in range(1, count)]
    return [lax.all_to_all(parts[0], axis, 0, 0, axis_index_groups=near(axis, count), tiled=True)]


def parcel(count, dims, kind):
    if few(count):
        return [shape(dims, kind)] * (count - 1)
    return [shape((count, *dims), kind)]


def away(refs, count, me, k):
    return refs[k - 1] if few(count) else refs[0].at[(me ^ k) & (count - 1)]


def place():
    return lax.axis_index("row"), lax.axis_index("col")


def loop(count, body):
    lax.fori_loop(0, count, lambda i, c: (body(i), c)[1], 0, unroll=count <= 18)


def start_kernel(z, rates, types, inputs, message, pad, codes):
    pad[...] = jnp.zeros_like(pad)
    pad[:, 0 : z.local] = rates[...]
    codes[...] = jnp.zeros_like(codes)
    t = types[...].reshape(1, z.local)
    m = inputs[...].reshape(1, z.local)
    rows = [
        lax.shift_right_logical(t, 7) + 1,
        t & 127,
        lax.shift_right_logical(m, 7) + 1,
        m & 127,
    ]
    for r, row in enumerate(rows):
        codes[r : r + 1, 0 : z.local] = row.astype(F32)
    code = codes[...]
    blocks = [code[0:4, f * BLOCK : (f + 1) * BLOCK] for f in range(z.frame)]
    fill = message.shape[0] - z.piece - 4 * z.frame
    extra = jnp.concatenate(blocks + [jnp.zeros((fill, BLOCK), F32)], axis=0)
    message[...] = jnp.concatenate([z.pack(pad[...]), extra], axis=0).astype(BF16)


def load_kernel(z, after, owner, post, pre, weights, out, ids, sem):
    del after
    copy = pltpu.make_async_copy(weights.at[0, 0], out, sem)
    copy.start()

    def one(s, carry):
        ids[s] = owner[0, 0, s] * z.post + post[0, 0, s]
        ids[z.slots + s] = pre[0, 0, s]
        return carry

    lax.fori_loop(0, z.slots, one, 0, unroll=8)
    copy.wait()


def prepare_kernel(z, mine, theirs, rates, cots, table, stimuli, pair_rates, gain, drive, cot_out, pad):
    highs = z.types // BLOCK
    t = jnp.transpose(table[...])
    t1 = t.astype(BF16)
    t2 = (t - t1.astype(F32)).astype(BF16)
    t3 = (t - t1.astype(F32) - t2.astype(F32)).astype(BF16)
    high_ids = lax.broadcasted_iota(jnp.int32, (highs, BLOCK), 0).astype(F32) + 1.0
    low_ids = lax.broadcasted_iota(jnp.int32, (BLOCK, BLOCK), 0).astype(F32)
    channel_ids = lax.broadcasted_iota(jnp.int32, (z.channels, BLOCK), 0).astype(F32)
    stim = stimuli[...]
    for side, ref in enumerate((mine, theirs)):
        rows = slice(side * z.piece, (side + 1) * z.piece)
        message = ref[...].astype(F32)
        gains, drives = [], []
        for f in range(z.frame):
            at = z.piece + 4 * f
            codes = message[at : at + 4]
            pick = (high_ids == codes[0:1]).astype(BF16)
            got = sum(jnp.dot(x, pick, preferred_element_type=F32) for x in (t1, t2, t3))
            mine_only = jnp.where(low_ids == codes[1:2], got, 0.0)
            line = jnp.sum(mine_only, axis=0, keepdims=True)
            gains.append(jnp.broadcast_to(line, (z.batch, BLOCK)))
            channel = (codes[2:3] - 1.0) * BLOCK + codes[3:4]
            chosen = (channel_ids == channel).astype(BF16)
            drives.append(jnp.dot(stim, chosen, preferred_element_type=F32))
        gain[rows] = z.pack(jnp.concatenate(gains, axis=1))
        for step in range(z.steps):
            part = [d[step * z.batch : (step + 1) * z.batch] for d in drives]
            drive[step, rows] = z.pack(jnp.concatenate(part, axis=1))
        if side == 1:
            pair_rates[rows] = message[0 : z.piece]
    pad[...] = jnp.zeros_like(pad)
    pad[:, 0 : z.local] = rates[...]
    pair_rates[0 : z.piece] = z.pack(pad[...])
    for step in range(z.steps):
        pad[:, 0 : z.local] = cots[step]
        cot_out[step] = z.pack(pad[...])


def multiply_forward(z, c, ids, weights, x, total, own, parts):
    total[...] = jnp.zeros_like(total)
    for s in range(z.slots):
        total[ids[s]] += lax.dot_general(
            x[ids[z.slots + s]], weights[s], (((1,), (1,)), ((), ())), preferred_element_type=F32
        )
    for k in range(z.cols):
        both = jnp.concatenate(
            [z.take_blocks(total, 0, c ^ k), z.take_blocks(total, z.post, c ^ k)], axis=0
        )
        if k == 0:
            own[...] = both
        else:
            away(parts, z.cols, c, k)[...] = both.astype(BF16)


def first_kernel(z, count, *refs):
    ids, weights, mine = refs[:3]
    got = refs[3 : 3 + count]
    x, own = refs[3 + count : 5 + count]
    parts, (sums, total) = refs[5 + count : -2], refs[-2:]
    p, c = place()
    sums[...] = jnp.zeros_like(sums)
    for k in range(z.rows):
        ref = mine if k == 0 else away(got, z.rows, p, k)
        z.add_blocks(sums, 0, p ^ k, ref[...].astype(F32)[0 : z.piece])
    x[...] = sums[...].astype(BF16)
    multiply_forward(z, c, ids, weights, x, total, own, parts)


def forward_kernel(z, count, *refs):
    ids, weights, mine = refs[:3]
    got = refs[3 : 3 + count]
    x, own = refs[3 + count : 5 + count]
    parts, (sums, total) = refs[5 + count : -2], refs[-2:]
    p, c = place()
    sums[...] = jnp.zeros_like(sums)
    for k in range(z.half):
        pair = (mine if k == 0 else away(got, z.half, p, k))[...].astype(F32)
        z.add_blocks(sums, 0, p ^ k, pair[0 : z.piece])
        z.add_blocks(sums, 0, p ^ k ^ z.half, pair[z.piece :])
    x[...] = sums[...].astype(BF16)
    multiply_forward(z, c, ids, weights, x, total, own, parts)


def sum_kernel(z, count, with_cot, *refs):
    own, got = refs[0], refs[1 : 1 + count]
    kept, message = refs[-2:]
    _, c = place()
    total = own[...]
    for k in range(1, z.cols):
        total = total + away(got, z.cols, c, k)[...].astype(F32)
    kept[...] = total
    if with_cot:
        cot = refs[1 + count]
        fill = message.shape[0] - z.pair - z.piece
        parts = [total, cot[z.steps - 1], jnp.zeros((fill, BLOCK), F32)]
        total = jnp.concatenate(parts, axis=0)
    message[...] = total.astype(BF16)


def currents(z, kept, theirs, drive):
    other = theirs[...].astype(F32)
    swapped = jnp.concatenate([other[z.piece : z.pair], other[0 : z.piece]], axis=0)
    own = kept[0 : z.piece] + swapped[0 : z.piece]
    partner = kept[z.piece :] + swapped[z.piece :]
    return jnp.concatenate([own, partner], axis=0) + drive, other


def rate_kernel(z, step, kept, theirs, rates, gain, drive, new, act, cur, lowered):
    current, _ = currents(z, kept, theirs, drive[step])
    activity = jnp.tanh(gain[...] * current)
    fresh = 0.5 * rates[...] + 0.5 * activity
    new[...] = fresh
    act[...] = activity
    cur[...] = current
    lowered[...] = fresh.astype(BF16)


def turn_kernel(z, kept, theirs, rates, gain, drive, cots, final, message, tally, base):
    current, other = currents(z, kept, theirs, drive[z.steps - 1])
    activity = jnp.tanh(gain[...] * current)
    fresh = 0.5 * rates[0 : z.piece] + 0.5 * activity[0 : z.piece]
    final[...] = z.unpack(fresh)[:, 0 : z.local]
    mine = cots[z.steps - 1]
    adjoint = jnp.concatenate([mine, other[z.pair : z.pair + z.piece]], axis=0)
    pressure = adjoint * 0.5 * (1.0 - activity * activity)
    message[...] = (gain[...] * pressure).astype(BF16)
    tally[...] = pressure * current
    base[...] = cots[z.steps - 2] + 0.5 * mine


def gather_post(z, c, mine, got, sums, d):
    sums[...] = jnp.zeros_like(sums)
    for k in range(z.cols):
        pair = (mine if k == 0 else away(got, z.cols, c, k))[...].astype(F32)
        z.add_blocks(sums, 0, c ^ k, pair[0 : z.piece])
        z.add_blocks(sums, z.post, c ^ k, pair[z.piece : z.pair])
    d[...] = sums[...].astype(BF16)


def back_kernel(z, count, *refs):
    ids, weights, mine = refs[:3]
    got = refs[3 : 3 + count]
    d, own = refs[3 + count : 5 + count]
    parts, (sums, total) = refs[5 + count : -2], refs[-2:]
    p, c = place()
    gather_post(z, c, mine, got, sums, d)
    total[...] = jnp.zeros_like(total)
    for s in range(z.slots):
        total[ids[z.slots + s]] += jnp.dot(d[ids[s]], weights[s], preferred_element_type=F32)
    for k in range(z.half):
        both = jnp.concatenate(
            [z.take_blocks(total, 0, p ^ k), z.take_blocks(total, 0, p ^ k ^ z.half)], axis=0
        )
        if k == 0:
            own[...] = both
        else:
            away(parts, z.half, p, k)[...] = both.astype(BF16)


def near_kernel(z, count, *refs):
    own, base, got = refs[0], refs[1], refs[2 : 2 + count]
    kept, message = refs[-2:]
    p, _ = place()
    total = own[...]
    for k in range(1, z.half):
        total = total + away(got, z.half, p, k)[...].astype(F32)
    total = jnp.concatenate([total[0 : z.piece] + base[...], total[z.piece :]], axis=0)
    kept[...] = total
    message[...] = total.astype(BF16)


def adjoints(z, kept, theirs):
    other = theirs[...].astype(F32)
    return kept[...] + jnp.concatenate([other[z.piece :], other[0 : z.piece]], axis=0)


def delta_kernel(z, before, kept, theirs, gain, act, cur, tally_in, cots, message, tally, base):
    adjoint = adjoints(z, kept, theirs)
    activity = act[...]
    pressure = adjoint * 0.5 * (1.0 - activity * activity)
    message[...] = (gain[...] * pressure).astype(BF16)
    tally[...] = tally_in[...] + pressure * cur[...]
    base[...] = cots[before - 1] + 0.5 * adjoint[0 : z.piece]


def last_delta_kernel(z, kept, theirs, gain, act, cur, tally_in, mine, partner, message):
    adjoint = adjoints(z, kept, theirs)
    activity = act[...]
    pressure = adjoint * 0.5 * (1.0 - activity * activity)
    tally = tally_in[...] + pressure * cur[...]
    rows = [gain[...] * pressure]
    lanes = lax.broadcasted_iota(jnp.int32, (1, BLOCK), 1)
    for side, ref in enumerate((mine, partner)):
        codes = ref[...].astype(F32)[z.piece :]
        begin = side * z.piece
        for f in range(z.frame):
            if f < z.full:
                at = begin + f * z.batch
                g = jnp.sum(tally[at : at + z.batch], axis=0, keepdims=True)
            else:
                at = begin + f * z.batch
                packed = jnp.sum(tally[at : at + z.tall], axis=0, keepdims=True)
                g = packed
                for i in range(1, z.groups):
                    g = g + pltpu.roll(packed, BLOCK - i * z.rest, 1)
                g = jnp.where(lanes < z.rest, g, 0.0)
            g1 = g.astype(BF16).astype(F32)
            g2 = (g - g1).astype(BF16).astype(F32)
            rows += [codes[4 * f : 4 * f + 2], g1, g2, g - g1 - g2]
        rows.append(jnp.zeros((CODES - 5 * z.frame, BLOCK), F32))
    message[...] = jnp.concatenate(rows, axis=0).astype(BF16)


def table_kernel(z, count, *refs):
    mine, got, out = refs[0], refs[1:-1], refs[-1]
    _, c = place()
    highs = z.types // BLOCK
    high_ids = lax.broadcasted_iota(jnp.int32, (highs, BLOCK), 0).astype(F32) + 1.0
    low_ids = lax.broadcasted_iota(jnp.int32, (BLOCK, BLOCK), 0).astype(F32)
    total = jnp.zeros((3 * highs, BLOCK), F32)
    for k in range(z.cols):
        ref = mine if k == 0 else away(got, z.cols, c, k)
        extra = ref[z.pair :].astype(F32)
        for side in range(2):
            for f in range(z.frame):
                at = side * CODES + 5 * f
                hit = high_ids == extra[at : at + 1]
                terms = [jnp.where(hit, extra[at + 2 + i : at + 3 + i], 0.0) for i in range(3)]
                left = jnp.concatenate(terms, axis=0).astype(BF16)
                right = (low_ids == extra[at + 1 : at + 2]).astype(BF16)
                total = total + lax.dot_general(
                    left, right, (((1,), (1,)), ((), ())), preferred_element_type=F32
                )
    out[...] = total[0:highs] + total[highs : 2 * highs] + total[2 * highs :]


def grad_kernel(z, count, per_step, *refs):
    ids, xs, ds = refs[0], refs[1 : 1 + z.steps], refs[1 + z.steps : 2 * z.steps]
    mine, got = refs[2 * z.steps], refs[2 * z.steps + 1 : 2 * z.steps + 1 + count]
    out = refs[2 * z.steps + 1 + count]
    sums, d0, right, left = refs[2 * z.steps + 2 + count :]
    n = z.batch
    deep = right.shape[1]

    @pl.when(pl.program_id(0) == 0)
    def _():
        _, c = place()
        gather_post(z, c, mine, got, sums, d0)

        def lay_right(q):
            for t in range(z.steps):
                right[q, t * n : (t + 1) * n] = xs[t][q]
            if deep > z.steps * n:
                right[q, z.steps * n :] = jnp.zeros((deep - z.steps * n, BLOCK), BF16)

        loop(z.pre, lay_right)

        def lay_left(q):
            parts = [d0[q].astype(F32)] + [d[q].astype(F32) for d in ds]
            if deep > z.steps * n:
                parts.append(jnp.zeros((deep - z.steps * n, BLOCK), F32))
            left[q] = jnp.transpose(jnp.concatenate(parts, axis=0)).astype(BF16)

        loop(2 * z.post, lay_left)

    begin = pl.program_id(0) * per_step
    for s in range(per_step):
        product = jnp.dot(
            left[ids[begin + s]], right[ids[z.slots + begin + s]], preferred_element_type=F32
        )
        out[s] = product.astype(BF16)


def shards(
    initial_rates,
    stimuli,
    cotangent,
    weight_blocks,
    slot_owner,
    slot_post,
    slot_pre,
    cell_type,
    type_gain,
    input_map,
):
    batch, local = initial_rates.shape
    slots = weight_blocks.shape[2]
    steps, _, channels = stimuli.shape
    types = type_gain.shape[0]
    z = Sizes(
        lax.axis_size("row"), lax.axis_size("col"), batch, local, slots, types, channels, steps
    )
    pair = (z.pair, BLOCK)
    product_flops = 2 * slots * batch * BLOCK * BLOCK
    opening = (z.piece + 4 * z.frame + 15) // 16 * 16
    closing = (z.pair + z.piece + 15) // 16 * 16

    (message,) = call(
        functools.partial(start_kernel, z),
        [shape((opening, BLOCK), BF16)],
        [pltpu.VMEM((batch, z.wide), F32), pltpu.VMEM((8, z.wide), F32)],
        [initial_rates, cell_type, input_map],
    )
    got = share(message, "row", z.rows)
    weights, ids = call(
        functools.partial(load_kernel, z),
        [shape((slots, BLOCK, BLOCK), BF16), shape((2 * slots,), jnp.int32)],
        [pltpu.SemaphoreType.DMA],
        [message, slot_owner, slot_post, slot_pre, weight_blocks],
        {1: SMEM, 2: SMEM, 3: SMEM, 4: ANY},
        out_specs=[VMEM, SMEM],
    )
    if few(z.rows):
        partner_message = got[z.half - 1]
    else:
        partner_message = flip(message, "row", z.half)
    pre_sums = pltpu.VMEM((z.pre, batch, BLOCK), F32)
    post_sums = pltpu.VMEM((2 * z.post, batch, BLOCK), F32)
    x_shape = shape((z.pre, batch, BLOCK), BF16)
    col_parts = parcel(z.cols, pair, BF16)
    row_parts = parcel(z.half, pair, BF16)
    x, own, *parts = call(
        functools.partial(first_kernel, z, len(got)),
        [x_shape, shape(pair), *col_parts],
        [pre_sums, post_sums],
        [ids, weights, message, *got],
        {0: SMEM},
        flops=product_flops,
    )
    rates, gain, drive, cots = call(
        functools.partial(prepare_kernel, z),
        [shape(pair), shape(pair), shape((steps, *pair)), shape((steps, z.piece, BLOCK))],
        [pltpu.VMEM((batch, z.wide), F32)],
        [
            message,
            partner_message,
            initial_rates,
            cotangent,
            type_gain.reshape(types // BLOCK, BLOCK),
            stimuli.reshape(steps * batch, channels),
        ],
    )
    xs, acts, curs = [x], [], []
    for t in range(steps):
        last = t == steps - 1
        got = exchange(parts, "col", z.cols)
        kept, sent = call(
            functools.partial(sum_kernel, z, len(got), last),
            [shape(pair), shape((closing, BLOCK) if last else pair, BF16)],
            [],
            [own, *got] + ([cots] if last else []),
        )
        theirs = flip(sent, "row", z.half)
        if last:
            break
        rates, act, cur, lowered = call(
            functools.partial(rate_kernel, z, t),
            [shape(pair), shape(pair), shape(pair), shape(pair, BF16)],
            [],
            [kept, theirs, rates, gain, drive],
        )
        got = share(lowered, "row", z.half)
        x, own, *parts = call(
            functools.partial(forward_kernel, z, len(got)),
            [x_shape, shape(pair), *col_parts],
            [pre_sums, post_sums],
            [ids, weights, lowered, *got],
            {0: SMEM},
            flops=product_flops,
        )
        xs.append(x)
        acts.append(act)
        curs.append(cur)
    final_rates, delta, tally, base = call(
        functools.partial(turn_kernel, z),
        [shape((batch, local)), shape(pair, BF16), shape(pair), shape((z.piece, BLOCK))],
        [],
        [kept, theirs, rates, gain, drive, cots],
    )
    ds = []
    for t in reversed(range(1, steps)):
        got = share(delta, "col", z.cols)
        d, own, *parts = call(
            functools.partial(back_kernel, z, len(got)),
            [shape((2 * z.post, batch, BLOCK), BF16), shape(pair), *row_parts],
            [post_sums, pre_sums],
            [ids, weights, delta, *got],
            {0: SMEM},
            flops=product_flops,
        )
        ds.insert(0, d)
        got = exchange(parts, "row", z.half)
        kept, sent = call(
            functools.partial(near_kernel, z, len(got)),
            [shape(pair), shape(pair, BF16)],
            [],
            [own, base, *got],
        )
        theirs = flip(sent, "row", z.half)
        before = t - 1
        if before > 0:
            delta, tally, base = call(
                functools.partial(delta_kernel, z, before),
                [shape(pair, BF16), shape(pair), shape((z.piece, BLOCK))],
                [],
                [kept, theirs, gain, acts[before], curs[before], tally, cots],
            )
        else:
            (delta,) = call(
                functools.partial(last_delta_kernel, z),
                [shape((z.pair + 2 * CODES, BLOCK), BF16)],
                [],
                [kept, theirs, gain, acts[0], curs[0], tally, message, partner_message],
            )
    got = share(delta, "col", z.cols)
    (table,) = call(
        functools.partial(table_kernel, z, len(got)), [shape((types // BLOCK, BLOCK))], [], [delta, *got]
    )
    if z.half == 2:
        table = table + flip(table, "row", 1)
    else:
        table = 0.5 * lax.psum(table, "row")
    gain_grads = table.reshape(types)

    grid = 4
    per_step = slots // grid
    deep = (steps * batch + BLOCK - 1) // BLOCK * BLOCK
    ins = [ids, *xs, *ds, delta, *got]
    weight_grads = pl.pallas_call(
        functools.partial(grad_kernel, z, len(got), per_step),
        grid=(grid,),
        out_shape=shape((slots, BLOCK, BLOCK), BF16),
        in_specs=[SMEM] + [VMEM] * (len(ins) - 1),
        out_specs=pl.BlockSpec((per_step, BLOCK, BLOCK), lambda i: (i, 0, 0)),
        scratch_shapes=[
            post_sums,
            pltpu.VMEM((2 * z.post, batch, BLOCK), BF16),
            pltpu.VMEM((z.pre, deep, BLOCK), BF16),
            pltpu.VMEM((2 * z.post, BLOCK, deep), BF16),
        ],
        cost_estimate=pl.CostEstimate(
            flops=2 * slots * deep * BLOCK * BLOCK, bytes_accessed=4 * 1024 * 1024, transcendentals=0
        ),
        compiler_params=pltpu.CompilerParams(vmem_limit_bytes=24 * 1024 * 1024),
    )(*ins)
    return (final_rates, weight_grads.reshape(1, 1, slots, BLOCK, BLOCK), gain_grads)


def solution(mesh):
    in_specs = (
        P("groups", ("row", "col")),
        P(None, "groups", None),
        P(None, "groups", ("row", "col")),
        P("row", "col", None, None, None),
        P("row", "col", None),
        P("row", "col", None),
        P("row", "col", None),
        P(("row", "col")),
        P(),
        P(("row", "col")),
    )
    out_specs = (P("groups", ("row", "col")), P("row", "col", "groups", None, None), P("groups"))
    return jax.shard_map(shards, mesh=mesh, in_specs=in_specs, out_specs=out_specs, check_vma=False)
```

```python
import functools

import jax
import jax.numpy as jnp
from jax import lax
from jax.experimental import pallas as pl
from jax.experimental.pallas import tpu as pltpu
from jax.sharding import PartitionSpec as P

BLOCK = 128
CODES = 16
F32 = jnp.float32
BF16 = jnp.bfloat16
VMEM = pl.BlockSpec(memory_space=pltpu.VMEM)
SMEM = pl.BlockSpec(memory_space=pltpu.SMEM)
HBM = pl.BlockSpec(memory_space=pltpu.HBM)


class Sizes:
    def __init__(self, row_count, col_count, batch, local, slots, types, channels, steps):
        self.rows, self.cols = row_count, col_count
        self.batch, self.local, self.slots = batch, local, slots
        self.types, self.channels, self.steps = types, channels, steps
        self.post = col_count * local // BLOCK
        self.pre = row_count * local // BLOCK
        self.half = row_count // 2
        self.full, self.rest = local // BLOCK, local % BLOCK
        self.groups = BLOCK // self.rest
        self.tall = batch // self.groups
        self.piece = self.full * batch + self.tall
        self.pair = 2 * self.piece
        offsets = [local * i % BLOCK for i in range(max(row_count, col_count))]
        self.frame = (max(offsets) + local + BLOCK - 1) // BLOCK
        self.wide = self.frame * BLOCK
        assert BLOCK % self.rest == 0 and batch % (8 * self.groups) == 0
        assert self.frame == self.full + 1 and self.pair % 16 == 0

    def first(self, i):
        return lax.div(i * self.local, jnp.int32(BLOCK))

    def offset(self, i):
        return lax.rem(i * self.local, jnp.int32(BLOCK))

    def pack(self, whole):
        parts = [whole[:, i * BLOCK : (i + 1) * BLOCK] for i in range(self.full)]
        tail = whole[:, self.full * BLOCK :]
        lanes = lax.broadcasted_iota(jnp.int32, (self.tall, BLOCK), 1)
        joined = tail[0 : self.tall]
        for g in range(1, self.groups):
            moved = pltpu.roll(tail[g * self.tall : (g + 1) * self.tall], g * self.rest, 1)
            joined = jnp.where(lanes < g * self.rest, joined, moved)
        return jnp.concatenate(parts + [joined], axis=0)

    def unpack(self, piece):
        parts = [piece[i * self.batch : (i + 1) * self.batch] for i in range(self.full)]
        joined = piece[self.full * self.batch :]
        lanes = lax.broadcasted_iota(jnp.int32, (self.tall, BLOCK), 1)
        tails = []
        for g in range(self.groups):
            moved = joined if g == 0 else pltpu.roll(joined, BLOCK - g * self.rest, 1)
            tails.append(jnp.where(lanes < self.rest, moved, 0.0))
        return jnp.concatenate(parts + [jnp.concatenate(tails, axis=0)], axis=1)

    def add_blocks(self, target, base, i, piece):
        turned = pltpu.roll(self.unpack(piece), self.offset(i), 1)
        first = base + self.first(i)
        for f in range(self.frame):
            target[first + f] += turned[:, f * BLOCK : (f + 1) * BLOCK]

    def take_blocks(self, source, base, i):
        first = base + self.first(i)
        whole = jnp.concatenate([source[first + f] for f in range(self.frame)], axis=1)
        back = lax.rem(self.wide - self.offset(i), jnp.int32(self.wide))
        return self.pack(pltpu.roll(whole, back, 1))


def call(body, outs, scratch, ins, places=None, flops=0, out_specs=None):
    specs = [(places or {}).get(i, VMEM) for i in range(len(ins))]
    moved = sum(x.size * x.dtype.itemsize for x in ins) + sum(x.size * x.dtype.itemsize for x in outs)
    return pl.pallas_call(
        body,
        out_shape=outs,
        in_specs=specs,
        out_specs=out_specs or [VMEM] * len(outs),
        scratch_shapes=scratch,
        cost_estimate=pl.CostEstimate(flops=flops, bytes_accessed=moved, transcendentals=0),
        compiler_params=pltpu.CompilerParams(vmem_limit_bytes=24 * 1024 * 1024),
    )(*ins)


def shape(dims, kind=F32):
    return jax.ShapeDtypeStruct(tuple(dims), kind)


def flip(x, axis, k):
    count = lax.axis_size(axis)
    return lax.ppermute(x, axis, [(i, i ^ k) for i in range(count)])


def few(count):
    return count <= 4


def share(x, axis):
    count = lax.axis_size(axis)
    if few(count):
        return [flip(x, axis, k) for k in reversed(range(1, count))][::-1]
    return [lax.all_gather(x, axis)]


def exchange(parts, axis):
    count = lax.axis_size(axis)
    if len(parts) == count - 1:
        return [flip(parts[k - 1], axis, k) for k in reversed(range(1, count))][::-1]
    return [lax.all_to_all(parts[0], axis, 0, 0, tiled=True)]


def parcel(count, dims, kind, whole=False):
    if few(count) and not whole:
        return [shape(dims, kind)] * (count - 1)
    return [shape((count, *dims), kind)]


def away(refs, count, me, k):
    return refs[k - 1] if len(refs) == count - 1 else refs[0].at[me ^ k]


def place():
    return lax.axis_index("row"), lax.axis_index("col")


def loop(count, body):
    lax.fori_loop(0, count, lambda i, c: (body(i), c)[1], 0, unroll=count <= 18)


def fetch(pairs, sems):
    copies = [pltpu.make_async_copy(a, b, sems.at[i]) for i, (a, b) in enumerate(pairs)]
    for copy in copies:
        copy.start()
    return copies


def start_kernel(z, rates_in, types_in, inputs_in, message, own, rates, types, inputs, pad, codes, sems):
    copies = fetch([(rates_in, rates), (types_in, types), (inputs_in, inputs)], sems)
    pad[...] = jnp.zeros_like(pad)
    codes[...] = jnp.zeros_like(codes)
    for copy in copies:
        copy.wait()
    pad[:, 0 : z.local] = rates[...]
    t = types[...].reshape(1, z.local)
    m = inputs[...].reshape(1, z.local)
    rows = [
        lax.shift_right_logical(t, 7) + 1,
        t & 127,
        lax.shift_right_logical(m, 7) + 1,
        m & 127,
    ]
    for r, row in enumerate(rows):
        codes[r : r + 1, 0 : z.local] = row.astype(F32)
    code = codes[...]
    blocks = [code[0:4, f * BLOCK : (f + 1) * BLOCK] for f in range(z.frame)]
    fill = message.shape[0] - z.piece - 4 * z.frame
    extra = jnp.concatenate(blocks + [jnp.zeros((fill, BLOCK), F32)], axis=0)
    packed = z.pack(pad[...])
    own[...] = packed
    message[...] = jnp.concatenate([packed, extra], axis=0).astype(BF16)


def load_kernel(z, after, owner_in, post_in, pre_in, weights, out, ids, owner, post, pre, sems):
    del after
    copies = fetch(
        [(owner_in, owner), (post_in, post), (pre_in, pre), (weights.at[0, 0], out)], sems
    )
    for copy in copies[:3]:
        copy.wait()

    def one(s, carry):
        ids[s] = owner[0, 0, s] * z.post + post[0, 0, s]
        ids[z.slots + s] = pre[0, 0, s]
        return carry

    lax.fori_loop(0, z.slots, one, 0, unroll=8)
    copies[3].wait()


def prepare_kernel(z, count, *refs):
    mine, own, cots, table, stimuli = refs[:5]
    got = refs[5 : 5 + count]
    rates, gain, drive, cot_out, pad = refs[5 + count :]
    p, _ = place()
    highs = z.types // BLOCK
    t = jnp.transpose(table[...])
    t1 = t.astype(BF16)
    t2 = (t - t1.astype(F32)).astype(BF16)
    t3 = (t - t1.astype(F32) - t2.astype(F32)).astype(BF16)
    high_ids = lax.broadcasted_iota(jnp.int32, (highs, BLOCK), 0).astype(F32) + 1.0
    low_ids = lax.broadcasted_iota(jnp.int32, (BLOCK, BLOCK), 0).astype(F32)
    channel_ids = lax.broadcasted_iota(jnp.int32, (z.channels, BLOCK), 0).astype(F32)
    stim = stimuli[...]
    for k in range(z.rows):
        ref = mine if k == 0 else away(got, z.rows, p, k)
        rows = slice(k * z.piece, (k + 1) * z.piece)
        message = ref[...].astype(F32)
        gains, drives = [], []
        for f in range(z.frame):
            at = z.piece + 4 * f
            codes = message[at : at + 4]
            pick = (high_ids == codes[0:1]).astype(BF16)
            found = sum(jnp.dot(x, pick, preferred_element_type=F32) for x in (t1, t2, t3))
            line = jnp.sum(jnp.where(low_ids == codes[1:2], found, 0.0), axis=0, keepdims=True)
            gains.append(jnp.broadcast_to(line, (z.batch, BLOCK)))
            channel = (codes[2:3] - 1.0) * BLOCK + codes[3:4]
            chosen = (channel_ids == channel).astype(BF16)
            drives.append(jnp.dot(stim, chosen, preferred_element_type=F32))
        gain[rows] = z.pack(jnp.concatenate(gains, axis=1))
        for step in range(z.steps):
            part = [d[step * z.batch : (step + 1) * z.batch] for d in drives]
            drive[step, rows] = z.pack(jnp.concatenate(part, axis=1))
        rates[rows] = own[...] if k == 0 else message[0 : z.piece]
    pad[...] = jnp.zeros_like(pad)
    for step in range(z.steps):
        pad[:, 0 : z.local] = cots[step]
        cot_out[step] = z.pack(pad[...])


def multiply_forward(z, c, ids, weights, x, total, own, parts):
    total[...] = jnp.zeros_like(total)
    for s in range(z.slots):
        total[ids[s]] += lax.dot_general(
            x[ids[z.slots + s]], weights[s], (((1,), (1,)), ((), ())), preferred_element_type=F32
        )
    for k in range(z.cols):
        both = jnp.concatenate(
            [z.take_blocks(total, 0, c ^ k), z.take_blocks(total, z.post, c ^ k)], axis=0
        )
        if k == 0:
            own[...] = both
        else:
            away(parts, z.cols, c, k)[...] = both.astype(BF16)


def first_kernel(z, count, *refs):
    ids, weights, mine = refs[:3]
    got = refs[3 : 3 + count]
    x, own = refs[3 + count : 5 + count]
    parts, (sums, total) = refs[5 + count : -2], refs[-2:]
    p, c = place()
    sums[...] = jnp.zeros_like(sums)
    for k in range(z.rows):
        ref = mine if k == 0 else away(got, z.rows, p, k)
        z.add_blocks(sums, 0, p ^ k, ref[...].astype(F32)[0 : z.piece])
    x[...] = sums[...].astype(BF16)
    multiply_forward(z, c, ids, weights, x, total, own, parts)


def forward_kernel(z, step, count, *refs):
    ids, weights, kept, rates, gain, drive = refs[:6]
    got = refs[6 : 6 + count]
    new, act_pair, cur_pair, x, own = refs[6 + count : 11 + count]
    parts, (sums, total) = refs[11 + count : -2], refs[-2:]
    p, c = place()
    sums[...] = jnp.zeros_like(sums)

    def sent(k, side):
        ref = kept if k == 0 else away(got, z.rows, p, k)
        return ref[side * z.piece : (side + 1) * z.piece].astype(F32)

    for k in range(z.rows):
        rows = slice(k * z.piece, (k + 1) * z.piece)
        current = sent(k, 0) + sent(k ^ z.half, 1) + drive[step, rows]
        activity = jnp.tanh(gain[rows] * current)
        fresh = 0.5 * rates[rows] + 0.5 * activity
        new[rows] = fresh
        if k % z.half == 0:
            at = k // z.half * z.piece
            act_pair[at : at + z.piece] = activity
            cur_pair[at : at + z.piece] = current
        z.add_blocks(sums, 0, p ^ k, fresh)
    x[...] = sums[...].astype(BF16)
    multiply_forward(z, c, ids, weights, x, total, own, parts)


def sum_kernel(z, count, with_cot, *refs):
    own, got = refs[0], refs[1 : 1 + count]
    kept, message = refs[-2:]
    _, c = place()
    total = own[...]
    for k in range(1, z.cols):
        total = total + away(got, z.cols, c, k)[...].astype(F32)
    kept[...] = total
    if with_cot:
        cot = refs[1 + count]
        fill = message.shape[0] - z.pair - z.piece
        parts = [total, cot[z.steps - 1], jnp.zeros((fill, BLOCK), F32)]
        total = jnp.concatenate(parts, axis=0)
    message[...] = total.astype(BF16)


def pair_of(z, ref):
    at = z.half * z.piece
    return jnp.concatenate([ref[0 : z.piece], ref[at : at + z.piece]], axis=0)


def turn_kernel(z, kept, theirs, rates, gain, drive, cots, final, message, gain_pair, tally, base):
    other = theirs[...].astype(F32)
    swapped = jnp.concatenate([other[z.piece : z.pair], other[0 : z.piece]], axis=0)
    gains = pair_of(z, gain)
    current = kept[...] + swapped + pair_of(z, drive.at[z.steps - 1])
    activity = jnp.tanh(gains * current)
    fresh = 0.5 * rates[0 : z.piece] + 0.5 * activity[0 : z.piece]
    final[...] = z.unpack(fresh)[:, 0 : z.local]
    mine = cots[z.steps - 1]
    adjoint = jnp.concatenate([mine, other[z.pair : z.pair + z.piece]], axis=0)
    pressure = adjoint * 0.5 * (1.0 - activity * activity)
    message[...] = (gains * pressure).astype(BF16)
    gain_pair[...] = gains
    tally[...] = pressure * current
    base[...] = cots[z.steps - 2] + 0.5 * mine


def gather_post(z, c, mine, got, sums, d):
    sums[...] = jnp.zeros_like(sums)
    for k in range(z.cols):
        pair = (mine if k == 0 else away(got, z.cols, c, k))[...].astype(F32)
        z.add_blocks(sums, 0, c ^ k, pair[0 : z.piece])
        z.add_blocks(sums, z.post, c ^ k, pair[z.piece : z.pair])
    d[...] = sums[...].astype(BF16)


def back_kernel(z, count, *refs):
    ids, weights, base, mine = refs[:4]
    got = refs[4 : 4 + count]
    d, own = refs[4 + count : 6 + count]
    parts, (sums, total) = refs[6 + count : -2], refs[-2:]
    p, c = place()
    gather_post(z, c, mine, got, sums, d)
    total[...] = jnp.zeros_like(total)
    for s in range(z.slots):
        total[ids[z.slots + s]] += jnp.dot(d[ids[s]], weights[s], preferred_element_type=F32)
    pieces = [z.take_blocks(total, 0, p ^ k) for k in range(z.rows)]
    for k in range(z.rows):
        other = pieces[k ^ z.half]
        if k == 0:
            own[...] = jnp.concatenate([pieces[0] + base[...], other], axis=0)
        else:
            if k == z.half:
                other = other + base[...]
            both = jnp.concatenate([pieces[k], other], axis=0)
            away(parts, z.rows, p, k)[...] = both.astype(BF16)


def adjoints(z, own, got):
    p, _ = place()
    total = own[...]
    for k in range(1, z.rows):
        total = total + away(got, z.rows, p, k)[...].astype(F32)
    return total


def delta_kernel(z, before, count, own, gain, act, cur, tally_in, cots, *refs):
    got, (message, tally, base) = refs[:count], refs[count:]
    adjoint = adjoints(z, own, got)
    activity = act[...]
    pressure = adjoint * 0.5 * (1.0 - activity * activity)
    message[...] = (gain[...] * pressure).astype(BF16)
    tally[...] = tally_in[...] + pressure * cur[...]
    base[...] = cots[before - 1] + 0.5 * adjoint[0 : z.piece]


def last_delta_kernel(z, count, own, gain, act, cur, tally_in, mine, partner, *refs):
    got, message = refs[:count], refs[count]
    adjoint = adjoints(z, own, got)
    activity = act[...]
    pressure = adjoint * 0.5 * (1.0 - activity * activity)
    tally = tally_in[...] + pressure * cur[...]
    rows = [gain[...] * pressure]
    lanes = lax.broadcasted_iota(jnp.int32, (1, BLOCK), 1)
    for side, ref in enumerate((mine, partner)):
        codes = ref[...].astype(F32)[z.piece :]
        begin = side * z.piece
        for f in range(z.frame):
            at = begin + f * z.batch
            if f < z.full:
                g = jnp.sum(tally[at : at + z.batch], axis=0, keepdims=True)
            else:
                packed = jnp.sum(tally[at : at + z.tall], axis=0, keepdims=True)
                g = packed
                for i in range(1, z.groups):
                    g = g + pltpu.roll(packed, BLOCK - i * z.rest, 1)
                g = jnp.where(lanes < z.rest, g, 0.0)
            g1 = g.astype(BF16).astype(F32)
            g2 = (g - g1).astype(BF16).astype(F32)
            rows += [codes[4 * f : 4 * f + 2], g1, g2, g - g1 - g2]
        rows.append(jnp.zeros((CODES - 5 * z.frame, BLOCK), F32))
    message[...] = jnp.concatenate(rows, axis=0).astype(BF16)


def table_kernel(z, count, *refs):
    mine, got, out = refs[0], refs[1:-1], refs[-1]
    _, c = place()
    highs = z.types // BLOCK
    high_ids = lax.broadcasted_iota(jnp.int32, (highs, BLOCK), 0).astype(F32) + 1.0
    low_ids = lax.broadcasted_iota(jnp.int32, (BLOCK, BLOCK), 0).astype(F32)
    total = jnp.zeros((3 * highs, BLOCK), F32)
    for k in range(z.cols):
        ref = mine if k == 0 else away(got, z.cols, c, k)
        extra = ref[z.pair :].astype(F32)
        for side in range(2):
            for f in range(z.frame):
                at = side * CODES + 5 * f
                hit = high_ids == extra[at : at + 1]
                terms = [jnp.where(hit, extra[at + 2 + i : at + 3 + i], 0.0) for i in range(3)]
                left = jnp.concatenate(terms, axis=0).astype(BF16)
                right = (low_ids == extra[at + 1 : at + 2]).astype(BF16)
                total = total + lax.dot_general(
                    left, right, (((1,), (1,)), ((), ())), preferred_element_type=F32
                )
    out[...] = total[0:highs] + total[highs : 2 * highs] + total[2 * highs :]


def grad_kernel(z, count, per_step, *refs):
    ids, xs, ds = refs[0], refs[1 : 1 + z.steps], refs[1 + z.steps : 2 * z.steps]
    mine, got = refs[2 * z.steps], refs[2 * z.steps + 1 : 2 * z.steps + 1 + count]
    out = refs[2 * z.steps + 1 + count]
    sums, d0, right, left = refs[2 * z.steps + 2 + count :]
    n = z.batch
    deep = right.shape[1]

    @pl.when(pl.program_id(0) == 0)
    def _():
        _, c = place()
        gather_post(z, c, mine, got, sums, d0)

        def lay_right(q):
            for t in range(z.steps):
                right[q, t * n : (t + 1) * n] = xs[t][q]
            if deep > z.steps * n:
                right[q, z.steps * n :] = jnp.zeros((deep - z.steps * n, BLOCK), BF16)

        loop(z.pre, lay_right)

        def lay_left(q):
            parts = [d0[q].astype(F32)] + [d[q].astype(F32) for d in ds]
            if deep > z.steps * n:
                parts.append(jnp.zeros((deep - z.steps * n, BLOCK), F32))
            left[q] = jnp.transpose(jnp.concatenate(parts, axis=0)).astype(BF16)

        loop(2 * z.post, lay_left)

    begin = pl.program_id(0) * per_step
    for s in range(per_step):
        product = jnp.dot(
            left[ids[begin + s]], right[ids[z.slots + begin + s]], preferred_element_type=F32
        )
        out[s] = product.astype(BF16)


def shards(
    initial_rates,
    stimuli,
    cotangent,
    weight_blocks,
    slot_owner,
    slot_post,
    slot_pre,
    cell_type,
    type_gain,
    input_map,
):
    batch, local = initial_rates.shape
    slots = weight_blocks.shape[2]
    steps, _, channels = stimuli.shape
    types = type_gain.shape[0]
    z = Sizes(
        lax.axis_size("row"), lax.axis_size("col"), batch, local, slots, types, channels, steps
    )
    pair = (z.pair, BLOCK)
    product_flops = 2 * slots * batch * BLOCK * BLOCK
    opening = (z.piece + 4 * z.frame + 15) // 16 * 16
    closing = (z.pair + z.piece + 15) // 16 * 16

    message, own_rates = call(
        functools.partial(start_kernel, z),
        [shape((opening, BLOCK), BF16), shape((z.piece, BLOCK))],
        [
            pltpu.VMEM((batch, local), F32),
            pltpu.VMEM((local,), jnp.int32),
            pltpu.VMEM((local,), jnp.int32),
            pltpu.VMEM((batch, z.wide), F32),
            pltpu.VMEM((8, z.wide), F32),
            pltpu.SemaphoreType.DMA((3,)),
        ],
        [initial_rates, cell_type, input_map],
        {0: HBM, 1: HBM, 2: HBM},
    )
    got = share(message, "row")
    weights, ids = call(
        functools.partial(load_kernel, z),
        [shape((slots, BLOCK, BLOCK), BF16), shape((2 * slots,), jnp.int32)],
        [pltpu.SMEM((1, 1, slots), jnp.int32)] * 3 + [pltpu.SemaphoreType.DMA((4,))],
        [message, slot_owner, slot_post, slot_pre, weight_blocks],
        {1: HBM, 2: HBM, 3: HBM, 4: HBM},
        out_specs=[VMEM, SMEM],
    )
    if few(z.rows):
        partner_message = got[z.half - 1]
    else:
        partner_message = flip(message, "row", z.half)
    pre_sums = pltpu.VMEM((z.pre, batch, BLOCK), F32)
    post_sums = pltpu.VMEM((2 * z.post, batch, BLOCK), F32)
    x_shape = shape((z.pre, batch, BLOCK), BF16)
    row_parts = parcel(z.rows, pair, BF16)
    x, own, *parts = call(
        functools.partial(first_kernel, z, len(got)),
        [x_shape, shape(pair), *parcel(z.cols, pair, BF16, True)],
        [pre_sums, post_sums],
        [ids, weights, message, *got],
        {0: SMEM},
        flops=product_flops,
    )
    every = (z.rows * z.piece, BLOCK)
    rates, gain, drive, cots = call(
        functools.partial(prepare_kernel, z, len(got)),
        [shape(every), shape(every), shape((steps, *every)), shape((steps, z.piece, BLOCK))],
        [pltpu.VMEM((batch, z.wide), F32)],
        [
            message,
            own_rates,
            cotangent,
            type_gain.reshape(types // BLOCK, BLOCK),
            stimuli.reshape(steps * batch, channels),
            *got,
        ],
    )
    xs, acts, curs = [x], [], []
    for t in range(steps):
        last = t == steps - 1
        got = exchange(parts, "col")
        kept, sent = call(
            functools.partial(sum_kernel, z, len(got), last),
            [shape(pair), shape((closing, BLOCK) if last else pair, BF16)],
            [],
            [own, *got] + ([cots] if last else []),
        )
        if last:
            break
        got = share(sent, "row")
        rates, act, cur, x, own, *parts = call(
            functools.partial(forward_kernel, z, t, len(got)),
            [shape(every), shape(pair), shape(pair), x_shape, shape(pair)]
            + parcel(z.cols, pair, BF16),
            [pre_sums, post_sums],
            [ids, weights, kept, rates, gain, drive, *got],
            {0: SMEM},
            flops=product_flops,
        )
        xs.append(x)
        acts.append(act)
        curs.append(cur)
    theirs = flip(sent, "row", z.half)
    final_rates, delta, gain, tally, base = call(
        functools.partial(turn_kernel, z),
        [
            shape((batch, local)),
            shape(pair, BF16),
            shape(pair),
            shape(pair),
            shape((z.piece, BLOCK)),
        ],
        [],
        [kept, theirs, rates, gain, drive, cots],
    )
    ds = []
    for t in reversed(range(1, steps)):
        got = share(delta, "col")
        d, own, *parts = call(
            functools.partial(back_kernel, z, len(got)),
            [shape((2 * z.post, batch, BLOCK), BF16), shape(pair), *row_parts],
            [post_sums, pre_sums],
            [ids, weights, base, delta, *got],
            {0: SMEM},
            flops=product_flops,
        )
        ds.insert(0, d)
        got = exchange(parts, "row")
        before = t - 1
        if before > 0:
            delta, tally, base = call(
                functools.partial(delta_kernel, z, before, len(got)),
                [shape(pair, BF16), shape(pair), shape((z.piece, BLOCK))],
                [],
                [own, gain, acts[before], curs[before], tally, cots, *got],
            )
        else:
            (delta,) = call(
                functools.partial(last_delta_kernel, z, len(got)),
                [shape((z.pair + 2 * CODES, BLOCK), BF16)],
                [],
                [own, gain, acts[0], curs[0], tally, message, partner_message, *got],
            )
    got = share(delta, "col")
    (table,) = call(
        functools.partial(table_kernel, z, len(got)), [shape((types // BLOCK, BLOCK))], [], [delta, *got]
    )
    if z.half == 2:
        table = table + flip(table, "row", 1)
    else:
        table = 0.5 * lax.psum(table, "row")
    gain_grads = table.reshape(types)

    grid = 4
    per_step = slots // grid
    deep = (steps * batch + BLOCK - 1) // BLOCK * BLOCK
    ins = [ids, *xs, *ds, delta, *got]
    weight_grads = pl.pallas_call(
        functools.partial(grad_kernel, z, len(got), per_step),
        grid=(grid,),
        out_shape=shape((slots, BLOCK, BLOCK), BF16),
        in_specs=[SMEM] + [VMEM] * (len(ins) - 1),
        out_specs=pl.BlockSpec((per_step, BLOCK, BLOCK), lambda i: (i, 0, 0)),
        scratch_shapes=[
            post_sums,
            pltpu.VMEM((2 * z.post, batch, BLOCK), BF16),
            pltpu.VMEM((z.pre, deep, BLOCK), BF16),
            pltpu.VMEM((2 * z.post, BLOCK, deep), BF16),
        ],
        cost_estimate=pl.CostEstimate(
            flops=2 * slots * deep * BLOCK * BLOCK, bytes_accessed=4 * 1024 * 1024, transcendentals=0
        ),
        compiler_params=pltpu.CompilerParams(vmem_limit_bytes=24 * 1024 * 1024),
    )(*ins)
    return (final_rates, weight_grads.reshape(1, 1, slots, BLOCK, BLOCK), gain_grads)


def solution(mesh):
    in_specs = (
        P("groups", ("row", "col")),
        P(None, "groups", None),
        P(None, "groups", ("row", "col")),
        P("row", "col", None, None, None),
        P("row", "col", None),
        P("row", "col", None),
        P("row", "col", None),
        P(("row", "col")),
        P(),
        P(("row", "col")),
    )
    out_specs = (P("groups", ("row", "col")), P("row", "col", "groups", None, None), P("groups"))
    return jax.shard_map(shards, mesh=mesh, in_specs=in_specs, out_specs=out_specs, check_vma=False)
```

```python
import functools

import jax
import jax.numpy as jnp
from jax import lax
from jax.experimental import pallas as pl
from jax.experimental.pallas import tpu as pltpu
from jax.sharding import PartitionSpec as P

BLOCK = 128
CODES = 16
F32 = jnp.float32
BF16 = jnp.bfloat16
VMEM = pl.BlockSpec(memory_space=pltpu.VMEM)
SMEM = pl.BlockSpec(memory_space=pltpu.SMEM)


class Sizes:
    def __init__(self, row_count, col_count, batch, local, slots, types, channels, steps):
        self.rows, self.cols = row_count, col_count
        self.batch, self.local, self.slots = batch, local, slots
        self.types, self.channels, self.steps = types, channels, steps
        self.post = col_count * local // BLOCK
        self.pre = row_count * local // BLOCK
        self.half = row_count // 2
        self.full, self.rest = local // BLOCK, local % BLOCK
        self.groups = BLOCK // self.rest
        self.tall = batch // self.groups
        self.piece = self.full * batch + self.tall
        self.pair = 2 * self.piece
        offsets = [local * i % BLOCK for i in range(max(row_count, col_count))]
        self.frame = (max(offsets) + local + BLOCK - 1) // BLOCK
        self.wide = self.frame * BLOCK
        assert BLOCK % self.rest == 0 and batch % (8 * self.groups) == 0
        assert self.frame == self.full + 1 and self.pair % 16 == 0

    def first(self, i):
        return lax.div(i * self.local, jnp.int32(BLOCK))

    def offset(self, i):
        return lax.rem(i * self.local, jnp.int32(BLOCK))

    def pack(self, whole):
        parts = [whole[:, i * BLOCK : (i + 1) * BLOCK] for i in range(self.full)]
        tail = whole[:, self.full * BLOCK :]
        lanes = lax.broadcasted_iota(jnp.int32, (self.tall, BLOCK), 1)
        joined = tail[0 : self.tall]
        for g in range(1, self.groups):
            moved = pltpu.roll(tail[g * self.tall : (g + 1) * self.tall], g * self.rest, 1)
            joined = jnp.where(lanes < g * self.rest, joined, moved)
        return jnp.concatenate(parts + [joined], axis=0)

    def unpack(self, piece):
        parts = [piece[i * self.batch : (i + 1) * self.batch] for i in range(self.full)]
        joined = piece[self.full * self.batch :]
        lanes = lax.broadcasted_iota(jnp.int32, (self.tall, BLOCK), 1)
        tails = []
        for g in range(self.groups):
            moved = joined if g == 0 else pltpu.roll(joined, BLOCK - g * self.rest, 1)
            tails.append(jnp.where(lanes < self.rest, moved, 0.0))
        return jnp.concatenate(parts + [jnp.concatenate(tails, axis=0)], axis=1)

    def add_blocks(self, target, base, i, piece):
        turned = pltpu.roll(self.unpack(piece), self.offset(i), 1)
        first = base + self.first(i)
        for f in range(self.frame):
            target[first + f] += turned[:, f * BLOCK : (f + 1) * BLOCK]

    def take_blocks(self, source, base, i):
        first = base + self.first(i)
        whole = jnp.concatenate([source[first + f] for f in range(self.frame)], axis=1)
        back = lax.rem(self.wide - self.offset(i), jnp.int32(self.wide))
        return self.pack(pltpu.roll(whole, back, 1))


def call(body, outs, scratch, ins, places=None, flops=0, out_specs=None, aliases=None):
    specs = [(places or {}).get(i, VMEM) for i in range(len(ins))]
    moved = sum(x.size * x.dtype.itemsize for x in ins) + sum(x.size * x.dtype.itemsize for x in outs)
    return pl.pallas_call(
        body,
        out_shape=outs,
        in_specs=specs,
        out_specs=out_specs or [VMEM] * len(outs),
        scratch_shapes=scratch,
        cost_estimate=pl.CostEstimate(flops=flops, bytes_accessed=moved, transcendentals=0),
        compiler_params=pltpu.CompilerParams(vmem_limit_bytes=24 * 1024 * 1024),
        input_output_aliases=aliases or {},
    )(*ins)


def shape(dims, kind=F32):
    return jax.ShapeDtypeStruct(tuple(dims), kind)


def flip(x, axis, k):
    count = lax.axis_size(axis)
    return lax.ppermute(x, axis, [(i, i ^ k) for i in range(count)])


def few(count):
    return count <= 4


def paired(axis):
    return axis == "col" and lax.axis_size(axis) == 4


def share(x, axis):
    count = lax.axis_size(axis)
    if paired(axis):
        far = flip(x, axis, 2)
        return [flip(x, axis, 1), far, flip(far, axis, 1)]
    if few(count):
        return [flip(x, axis, k) for k in reversed(range(1, count))][::-1]
    return [lax.all_gather(x, axis)]


def exchange(parts, axis):
    count = lax.axis_size(axis)
    if len(parts) == count - 1:
        return [flip(parts[k - 1], axis, k) for k in reversed(range(1, count))][::-1]
    return [lax.all_to_all(parts[0], axis, 0, 0, tiled=True)]


def parcel(count, dims, kind):
    if few(count):
        return [shape(dims, kind)] * (count - 1)
    return [shape((count, *dims), kind)]


def away(refs, count, me, k):
    return refs[k - 1] if len(refs) == count - 1 else refs[0].at[me ^ k]


def place():
    return lax.axis_index("row"), lax.axis_index("col")


def loop(count, body):
    lax.fori_loop(0, count, lambda i, c: (body(i), c)[1], 0, unroll=count <= 18)


def start_kernel(z, rates, numbers, message, own, pad):
    pad[...] = jnp.zeros_like(pad)
    pad[:, 0 : z.local] = rates[...]
    packed = z.pack(pad[...])
    own[...] = packed
    number = numbers[...]
    high = (lax.shift_right_arithmetic(number, 7) + 1).astype(F32)
    low = (number & 127).astype(F32)
    blocks = []
    for f in range(z.frame):
        for r in (f, z.frame + f):
            blocks += [high[r : r + 1], low[r : r + 1]]
    fill = message.shape[0] - z.piece - 4 * z.frame
    extra = jnp.concatenate(blocks + [jnp.zeros((fill, BLOCK), F32)], axis=0)
    message[...] = jnp.concatenate([packed, extra], axis=0).astype(BF16)


def load_kernel(z, after, owner, post, pre, weights, ids):
    del after, weights

    def one(s, carry):
        ids[s] = owner[0, 0, s] * z.post + post[0, 0, s]
        ids[z.slots + s] = pre[0, 0, s]
        return carry

    lax.fori_loop(0, z.slots, one, 0, unroll=8)


def prepare_kernel(z, count, *refs):
    mine, own, cots, table, stimuli = refs[:5]
    got = refs[5 : 5 + count]
    rates, gain, drive, cot_out, pad = refs[5 + count :]
    p, _ = place()
    highs = z.types // BLOCK
    t = jnp.transpose(table[...])
    t1 = t.astype(BF16)
    t2 = (t - t1.astype(F32)).astype(BF16)
    t3 = (t - t1.astype(F32) - t2.astype(F32)).astype(BF16)
    high_ids = lax.broadcasted_iota(jnp.int32, (highs, BLOCK), 0).astype(F32) + 1.0
    low_ids = lax.broadcasted_iota(jnp.int32, (BLOCK, BLOCK), 0).astype(F32)
    channel_ids = lax.broadcasted_iota(jnp.int32, (z.channels, BLOCK), 0).astype(F32)
    stim = stimuli[...]
    for k in range(z.rows):
        ref = mine if k == 0 else away(got, z.rows, p, k)
        rows = slice(k * z.piece, (k + 1) * z.piece)
        message = ref[...].astype(F32)
        gains, drives = [], []
        for f in range(z.frame):
            at = z.piece + 4 * f
            codes = message[at : at + 4]
            pick = (high_ids == codes[0:1]).astype(BF16)
            found = sum(jnp.dot(x, pick, preferred_element_type=F32) for x in (t1, t2, t3))
            line = jnp.sum(jnp.where(low_ids == codes[1:2], found, 0.0), axis=0, keepdims=True)
            gains.append(jnp.broadcast_to(line, (z.batch, BLOCK)))
            channel = (codes[2:3] - 1.0) * BLOCK + codes[3:4]
            chosen = (channel_ids == channel).astype(BF16)
            drives.append(jnp.dot(stim, chosen, preferred_element_type=F32))
        gain[rows] = z.pack(jnp.concatenate(gains, axis=1))
        for step in range(z.steps):
            part = [d[step * z.batch : (step + 1) * z.batch] for d in drives]
            drive[step, rows] = z.pack(jnp.concatenate(part, axis=1))
        rates[rows] = own[...] if k == 0 else message[0 : z.piece]
    pad[...] = jnp.zeros_like(pad)
    for step in range(z.steps):
        pad[:, 0 : z.local] = cots[step]
        cot_out[step] = z.pack(pad[...])


def multiply_forward(z, c, ids, weights, x, total, own, parts):
    total[...] = jnp.zeros_like(total)
    for s in range(z.slots):
        total[ids[s]] += lax.dot_general(
            x[ids[z.slots + s]], weights[s], (((1,), (1,)), ((), ())), preferred_element_type=F32
        )
    for k in range(z.cols):
        both = jnp.concatenate(
            [z.take_blocks(total, 0, c ^ k), z.take_blocks(total, z.post, c ^ k)], axis=0
        )
        if z.cols == 4:
            rows = slice(k // 2 * z.pair, (k // 2 + 1) * z.pair)
            if k % 2 == 0:
                own[rows] = both
            else:
                parts[0][rows] = both.astype(BF16)
        elif k == 0:
            own[...] = both
        else:
            away(parts, z.cols, c, k)[...] = both.astype(BF16)


def first_kernel(z, count, *refs):
    ids, weights, mine = refs[:3]
    got = refs[3 : 3 + count]
    x, own = refs[3 + count : 5 + count]
    parts, (sums, total) = refs[5 + count : -2], refs[-2:]
    p, c = place()
    sums[...] = jnp.zeros_like(sums)
    for k in range(z.rows):
        ref = mine if k == 0 else away(got, z.rows, p, k)
        z.add_blocks(sums, 0, p ^ k, ref[...].astype(F32)[0 : z.piece])
    x[...] = sums[...].astype(BF16)
    multiply_forward(z, c, ids, weights, x, total, own, parts)


def forward_kernel(z, step, count, *refs):
    ids, weights, kept, rates, gain, drive = refs[:6]
    got = refs[6 : 6 + count]
    new, act_pair, cur_pair, x, own = refs[6 + count : 11 + count]
    parts, (sums, total) = refs[11 + count : -2], refs[-2:]
    p, c = place()
    sums[...] = jnp.zeros_like(sums)

    def sent(k, side):
        ref = kept if k == 0 else away(got, z.rows, p, k)
        return ref[side * z.piece : (side + 1) * z.piece].astype(F32)

    for k in range(z.rows):
        rows = slice(k * z.piece, (k + 1) * z.piece)
        current = sent(k, 0) + sent(k ^ z.half, 1) + drive[step, rows]
        activity = jnp.tanh(gain[rows] * current)
        fresh = 0.5 * rates[rows] + 0.5 * activity
        new[rows] = fresh
        if k % z.half == 0:
            at = k // z.half * z.piece
            act_pair[at : at + z.piece] = activity
            cur_pair[at : at + z.piece] = current
        z.add_blocks(sums, 0, p ^ k, fresh)
    x[...] = sums[...].astype(BF16)
    multiply_forward(z, c, ids, weights, x, total, own, parts)


def half_kernel(z, own, got, kept, message):
    total = own[...] + got[...].astype(F32)
    kept[...] = total[0 : z.pair]
    message[...] = total[z.pair :].astype(BF16)


def sum_kernel(z, count, with_cot, *refs):
    own, got = refs[0], refs[1 : 1 + count]
    kept, message = refs[-2:]
    _, c = place()
    total = own[...]
    if z.cols == 4:
        total = total + got[0][...].astype(F32)
    else:
        for k in range(1, z.cols):
            total = total + away(got, z.cols, c, k)[...].astype(F32)
    kept[...] = total
    if with_cot:
        cot = refs[1 + count]
        fill = message.shape[0] - z.pair - z.piece
        parts = [total, cot[z.steps - 1], jnp.zeros((fill, BLOCK), F32)]
        total = jnp.concatenate(parts, axis=0)
    message[...] = total.astype(BF16)


def pair_of(z, ref):
    at = z.half * z.piece
    return jnp.concatenate([ref[0 : z.piece], ref[at : at + z.piece]], axis=0)


def turn_kernel(z, kept, theirs, rates, gain, drive, cots, final, message, gain_pair, tally, base):
    other = theirs[...].astype(F32)
    swapped = jnp.concatenate([other[z.piece : z.pair], other[0 : z.piece]], axis=0)
    gains = pair_of(z, gain)
    current = kept[...] + swapped + pair_of(z, drive.at[z.steps - 1])
    activity = jnp.tanh(gains * current)
    fresh = 0.5 * rates[0 : z.piece] + 0.5 * activity[0 : z.piece]
    final[...] = z.unpack(fresh)[:, 0 : z.local]
    mine = cots[z.steps - 1]
    adjoint = jnp.concatenate([mine, other[z.pair : z.pair + z.piece]], axis=0)
    pressure = adjoint * 0.5 * (1.0 - activity * activity)
    message[...] = (gains * pressure).astype(BF16)
    gain_pair[...] = gains
    tally[...] = pressure * current
    base[...] = cots[z.steps - 2] + 0.5 * mine


def gather_post(z, c, mine, got, sums, d):
    sums[...] = jnp.zeros_like(sums)
    for k in range(z.cols):
        pair = (mine if k == 0 else away(got, z.cols, c, k))[...].astype(F32)
        z.add_blocks(sums, 0, c ^ k, pair[0 : z.piece])
        z.add_blocks(sums, z.post, c ^ k, pair[z.piece : z.pair])
    d[...] = sums[...].astype(BF16)


def back_kernel(z, count, *refs):
    ids, weights, base, mine = refs[:4]
    got = refs[4 : 4 + count]
    d, own = refs[4 + count : 6 + count]
    parts, (sums, total) = refs[6 + count : -2], refs[-2:]
    p, c = place()
    gather_post(z, c, mine, got, sums, d)
    total[...] = jnp.zeros_like(total)
    for s in range(z.slots):
        total[ids[z.slots + s]] += jnp.dot(d[ids[s]], weights[s], preferred_element_type=F32)
    pieces = [z.take_blocks(total, 0, p ^ k) for k in range(z.rows)]
    for k in range(z.rows):
        other = pieces[k ^ z.half]
        if k == 0:
            own[...] = jnp.concatenate([pieces[0] + base[...], other], axis=0)
        else:
            if k == z.half:
                other = other + base[...]
            both = jnp.concatenate([pieces[k], other], axis=0)
            away(parts, z.rows, p, k)[...] = both.astype(BF16)


def adjoints(z, own, got):
    p, _ = place()
    total = own[...]
    for k in range(1, z.rows):
        total = total + away(got, z.rows, p, k)[...].astype(F32)
    return total


def delta_kernel(z, before, count, own, gain, act, cur, tally_in, cots, *refs):
    got, (message, tally, base) = refs[:count], refs[count:]
    adjoint = adjoints(z, own, got)
    activity = act[...]
    pressure = adjoint * 0.5 * (1.0 - activity * activity)
    message[...] = (gain[...] * pressure).astype(BF16)
    tally[...] = tally_in[...] + pressure * cur[...]
    base[...] = cots[before - 1] + 0.5 * adjoint[0 : z.piece]


def last_delta_kernel(z, count, own, gain, act, cur, tally_in, mine, partner, *refs):
    got, message = refs[:count], refs[count]
    adjoint = adjoints(z, own, got)
    activity = act[...]
    pressure = adjoint * 0.5 * (1.0 - activity * activity)
    tally = tally_in[...] + pressure * cur[...]
    rows = [gain[...] * pressure]
    lanes = lax.broadcasted_iota(jnp.int32, (1, BLOCK), 1)
    for side, ref in enumerate((mine, partner)):
        codes = ref[...].astype(F32)[z.piece :]
        begin = side * z.piece
        for f in range(z.frame):
            at = begin + f * z.batch
            if f < z.full:
                g = jnp.sum(tally[at : at + z.batch], axis=0, keepdims=True)
            else:
                packed = jnp.sum(tally[at : at + z.tall], axis=0, keepdims=True)
                g = packed
                for i in range(1, z.groups):
                    g = g + pltpu.roll(packed, BLOCK - i * z.rest, 1)
                g = jnp.where(lanes < z.rest, g, 0.0)
            g1 = g.astype(BF16).astype(F32)
            g2 = (g - g1).astype(BF16).astype(F32)
            rows += [codes[4 * f : 4 * f + 2], g1, g2, g - g1 - g2]
        rows.append(jnp.zeros((CODES - 5 * z.frame, BLOCK), F32))
    message[...] = jnp.concatenate(rows, axis=0).astype(BF16)


def table_kernel(z, count, *refs):
    mine, got, out = refs[0], refs[1:-1], refs[-1]
    _, c = place()
    highs = z.types // BLOCK
    high_ids = lax.broadcasted_iota(jnp.int32, (highs, BLOCK), 0).astype(F32) + 1.0
    low_ids = lax.broadcasted_iota(jnp.int32, (BLOCK, BLOCK), 0).astype(F32)
    total = jnp.zeros((3 * highs, BLOCK), F32)
    for k in range(z.cols):
        ref = mine if k == 0 else away(got, z.cols, c, k)
        extra = ref[z.pair :].astype(F32)
        for side in range(2):
            for f in range(z.frame):
                at = side * CODES + 5 * f
                hit = high_ids == extra[at : at + 1]
                terms = [jnp.where(hit, extra[at + 2 + i : at + 3 + i], 0.0) for i in range(3)]
                left = jnp.concatenate(terms, axis=0).astype(BF16)
                right = (low_ids == extra[at + 1 : at + 2]).astype(BF16)
                total = total + lax.dot_general(
                    left, right, (((1,), (1,)), ((), ())), preferred_element_type=F32
                )
    out[...] = total[0:highs] + total[highs : 2 * highs] + total[2 * highs :]


def grad_kernel(z, count, per_step, *refs):
    ids, xs, ds = refs[0], refs[1 : 1 + z.steps], refs[1 + z.steps : 2 * z.steps]
    mine, got = refs[2 * z.steps], refs[2 * z.steps + 1 : 2 * z.steps + 1 + count]
    out = refs[2 * z.steps + 1 + count]
    sums, d0, right, left = refs[2 * z.steps + 2 + count :]
    n = z.batch
    deep = right.shape[1]

    @pl.when(pl.program_id(0) == 0)
    def _():
        _, c = place()
        gather_post(z, c, mine, got, sums, d0)

        def lay_right(q):
            for t in range(z.steps):
                right[q, t * n : (t + 1) * n] = xs[t][q]
            if deep > z.steps * n:
                right[q, z.steps * n :] = jnp.zeros((deep - z.steps * n, BLOCK), BF16)

        loop(z.pre, lay_right)

        def lay_left(q):
            parts = [d0[q].astype(F32)] + [d[q].astype(F32) for d in ds]
            if deep > z.steps * n:
                parts.append(jnp.zeros((deep - z.steps * n, BLOCK), F32))
            left[q] = jnp.transpose(jnp.concatenate(parts, axis=0)).astype(BF16)

        loop(2 * z.post, lay_left)

    begin = pl.program_id(0) * per_step
    for s in range(per_step):
        product = jnp.dot(
            left[ids[begin + s]], right[ids[z.slots + begin + s]], preferred_element_type=F32
        )
        out[s] = product.astype(BF16)


def shards(
    initial_rates,
    stimuli,
    cotangent,
    weight_blocks,
    slot_owner,
    slot_post,
    slot_pre,
    cell_type,
    type_gain,
    input_map,
):
    batch, local = initial_rates.shape
    slots = weight_blocks.shape[2]
    steps, _, channels = stimuli.shape
    types = type_gain.shape[0]
    z = Sizes(
        lax.axis_size("row"), lax.axis_size("col"), batch, local, slots, types, channels, steps
    )
    pair = (z.pair, BLOCK)
    product_flops = 2 * slots * batch * BLOCK * BLOCK
    opening = (z.piece + 4 * z.frame + 15) // 16 * 16
    closing = (z.pair + z.piece + 15) // 16 * 16

    fill = jnp.full((z.wide - local,), -BLOCK, jnp.int32)
    numbers = jnp.concatenate([cell_type, fill, input_map, fill])
    message, own_rates = call(
        functools.partial(start_kernel, z),
        [shape((opening, BLOCK), BF16), shape((z.piece, BLOCK))],
        [pltpu.VMEM((batch, z.wide), F32)],
        [initial_rates, numbers.reshape(2 * z.frame, BLOCK)],
    )
    got = share(message, "row")
    weights = weight_blocks.reshape(slots, BLOCK, BLOCK)
    (ids,) = call(
        functools.partial(load_kernel, z),
        [shape((2 * slots,), jnp.int32)],
        [],
        [message, slot_owner, slot_post, slot_pre, weights],
        {1: SMEM, 2: SMEM, 3: SMEM},
        out_specs=[SMEM],
    )
    if few(z.rows):
        partner_message = got[z.half - 1]
    else:
        partner_message = flip(message, "row", z.half)
    pre_sums = pltpu.VMEM((z.pre, batch, BLOCK), F32)
    post_sums = pltpu.VMEM((2 * z.post, batch, BLOCK), F32)
    x_shape = shape((z.pre, batch, BLOCK), BF16)
    row_parts = parcel(z.rows, pair, BF16)
    two = paired("col")
    if two:
        col_parts = [shape((2 * z.pair, BLOCK)), shape((2 * z.pair, BLOCK), BF16)]
    else:
        col_parts = [shape(pair), *parcel(z.cols, pair, BF16)]
    x, own, *parts = call(
        functools.partial(first_kernel, z, len(got)),
        [x_shape, *col_parts],
        [pre_sums, post_sums],
        [ids, weights, message, *got],
        {0: SMEM},
        flops=product_flops,
    )
    every = (z.rows * z.piece, BLOCK)
    rates, gain, drive, cots = call(
        functools.partial(prepare_kernel, z, len(got)),
        [shape(every), shape(every), shape((steps, *every)), shape((steps, z.piece, BLOCK))],
        [pltpu.VMEM((batch, z.wide), F32)],
        [
            message,
            own_rates,
            cotangent,
            type_gain.reshape(types // BLOCK, BLOCK),
            stimuli.reshape(steps * batch, channels),
            *got,
        ],
    )
    xs, acts, curs = [x], [], []
    for t in range(steps):
        last = t == steps - 1
        if two:
            near = flip(parts[0], "col", 1)
            own, far = call(
                functools.partial(half_kernel, z), [shape(pair), shape(pair, BF16)], [], [own, near]
            )
            got = [flip(far, "col", 2)]
        else:
            got = exchange(parts, "col")
        kept, sent = call(
            functools.partial(sum_kernel, z, len(got), last),
            [shape(pair), shape((closing, BLOCK) if last else pair, BF16)],
            [],
            [own, *got] + ([cots] if last else []),
        )
        if last:
            break
        got = share(sent, "row")
        rates, act, cur, x, own, *parts = call(
            functools.partial(forward_kernel, z, t, len(got)),
            [shape(every), shape(pair), shape(pair), x_shape, *col_parts],
            [pre_sums, post_sums],
            [ids, weights, kept, rates, gain, drive, *got],
            {0: SMEM},
            flops=product_flops,
        )
        xs.append(x)
        acts.append(act)
        curs.append(cur)
    theirs = flip(sent, "row", z.half)
    final_rates, delta, gain, tally, base = call(
        functools.partial(turn_kernel, z),
        [
            shape((batch, local)),
            shape(pair, BF16),
            shape(pair),
            shape(pair),
            shape((z.piece, BLOCK)),
        ],
        [],
        [kept, theirs, rates, gain, drive, cots],
    )
    ds = []
    for t in reversed(range(1, steps)):
        got = share(delta, "col")
        d, own, *parts = call(
            functools.partial(back_kernel, z, len(got)),
            [shape((2 * z.post, batch, BLOCK), BF16), shape(pair), *row_parts],
            [post_sums, pre_sums],
            [ids, weights, base, delta, *got],
            {0: SMEM},
            flops=product_flops,
        )
        ds.insert(0, d)
        got = exchange(parts, "row")
        before = t - 1
        if before > 0:
            delta, tally, base = call(
                functools.partial(delta_kernel, z, before, len(got)),
                [shape(pair, BF16), shape(pair), shape((z.piece, BLOCK))],
                [],
                [own, gain, acts[before], curs[before], tally, cots, *got],
            )
        else:
            (delta,) = call(
                functools.partial(last_delta_kernel, z, len(got)),
                [shape((z.pair + 2 * CODES, BLOCK), BF16)],
                [],
                [own, gain, acts[0], curs[0], tally, message, partner_message, *got],
            )
    got = share(delta, "col")
    (table,) = call(
        functools.partial(table_kernel, z, len(got)), [shape((types // BLOCK, BLOCK))], [], [delta, *got]
    )
    if z.half == 2:
        table = table + flip(table, "row", 1)
    else:
        table = 0.5 * lax.psum(table, "row")
    gain_grads = table.reshape(types)

    grid = 4
    per_step = slots // grid
    deep = (steps * batch + BLOCK - 1) // BLOCK * BLOCK
    ins = [ids, *xs, *ds, delta, *got]
    weight_grads = pl.pallas_call(
        functools.partial(grad_kernel, z, len(got), per_step),
        grid=(grid,),
        out_shape=shape((slots, BLOCK, BLOCK), BF16),
        in_specs=[SMEM] + [VMEM] * (len(ins) - 1),
        out_specs=pl.BlockSpec((per_step, BLOCK, BLOCK), lambda i: (i, 0, 0)),
        scratch_shapes=[
            post_sums,
            pltpu.VMEM((2 * z.post, batch, BLOCK), BF16),
            pltpu.VMEM((z.pre, deep, BLOCK), BF16),
            pltpu.VMEM((2 * z.post, BLOCK, deep), BF16),
        ],
        cost_estimate=pl.CostEstimate(
            flops=2 * slots * deep * BLOCK * BLOCK, bytes_accessed=4 * 1024 * 1024, transcendentals=0
        ),
        compiler_params=pltpu.CompilerParams(vmem_limit_bytes=24 * 1024 * 1024),
    )(*ins)
    return (final_rates, weight_grads.reshape(1, 1, slots, BLOCK, BLOCK), gain_grads)


def solution(mesh):
    in_specs = (
        P("groups", ("row", "col")),
        P(None, "groups", None),
        P(None, "groups", ("row", "col")),
        P("row", "col", None, None, None),
        P("row", "col", None),
        P("row", "col", None),
        P("row", "col", None),
        P(("row", "col")),
        P(),
        P(("row", "col")),
    )
    out_specs = (P("groups", ("row", "col")), P("row", "col", "groups", None, None), P("groups"))
    return jax.shard_map(shards, mesh=mesh, in_specs=in_specs, out_specs=out_specs, check_vma=False)
```

```python
import functools

import jax
import jax.numpy as jnp
from jax import lax
from jax.experimental import pallas as pl
from jax.experimental.pallas import tpu as pltpu
from jax.sharding import PartitionSpec as P

BLOCK = 128
CODES = 16
F32 = jnp.float32
BF16 = jnp.bfloat16
VMEM = pl.BlockSpec(memory_space=pltpu.VMEM)


class Sizes:
    def __init__(self, row_count, col_count, batch, local, slots, types, channels, steps):
        self.rows, self.cols = row_count, col_count
        self.batch, self.local, self.slots = batch, local, slots
        self.types, self.channels, self.steps = types, channels, steps
        self.post = col_count * local // BLOCK
        self.pre = row_count * local // BLOCK
        self.half = row_count // 2
        self.full, self.rest = local // BLOCK, local % BLOCK
        self.groups = BLOCK // self.rest
        self.tall = batch // self.groups
        self.piece = self.full * batch + self.tall
        self.pair = 2 * self.piece
        offsets = [local * i % BLOCK for i in range(max(row_count, col_count))]
        self.frame = (max(offsets) + local + BLOCK - 1) // BLOCK
        self.wide = self.frame * BLOCK
        assert BLOCK % self.rest == 0 and batch % (8 * self.groups) == 0
        assert self.frame == self.full + 1 and self.pair % 16 == 0

    def first(self, i):
        return lax.div(i * self.local, jnp.int32(BLOCK))

    def offset(self, i):
        return lax.rem(i * self.local, jnp.int32(BLOCK))

    def pack(self, whole):
        parts = [whole[:, i * BLOCK : (i + 1) * BLOCK] for i in range(self.full)]
        tail = whole[:, self.full * BLOCK :]
        lanes = lax.broadcasted_iota(jnp.int32, (self.tall, BLOCK), 1)
        joined = tail[0 : self.tall]
        for g in range(1, self.groups):
            moved = pltpu.roll(tail[g * self.tall : (g + 1) * self.tall], g * self.rest, 1)
            joined = jnp.where(lanes < g * self.rest, joined, moved)
        return jnp.concatenate(parts + [joined], axis=0)

    def unpack(self, piece):
        parts = [piece[i * self.batch : (i + 1) * self.batch] for i in range(self.full)]
        joined = piece[self.full * self.batch :]
        lanes = lax.broadcasted_iota(jnp.int32, (self.tall, BLOCK), 1)
        tails = []
        for g in range(self.groups):
            moved = joined if g == 0 else pltpu.roll(joined, BLOCK - g * self.rest, 1)
            tails.append(jnp.where(lanes < self.rest, moved, 0.0))
        return jnp.concatenate(parts + [jnp.concatenate(tails, axis=0)], axis=1)

    def add_blocks(self, target, base, i, piece):
        turned = pltpu.roll(self.unpack(piece), self.offset(i), 1)
        first = base + self.first(i)
        for f in range(self.frame):
            target[first + f] += turned[:, f * BLOCK : (f + 1) * BLOCK]

    def take_blocks(self, source, base, i):
        first = base + self.first(i)
        whole = jnp.concatenate([source[first + f] for f in range(self.frame)], axis=1)
        back = lax.rem(self.wide - self.offset(i), jnp.int32(self.wide))
        return self.pack(pltpu.roll(whole, back, 1))


def call(body, outs, scratch, ins, places=None, flops=0, out_specs=None, aliases=None):
    specs = [(places or {}).get(i, VMEM) for i in range(len(ins))]
    moved = sum(x.size * x.dtype.itemsize for x in ins) + sum(x.size * x.dtype.itemsize for x in outs)
    return pl.pallas_call(
        body,
        out_shape=outs,
        in_specs=specs,
        out_specs=out_specs or [VMEM] * len(outs),
        scratch_shapes=scratch,
        cost_estimate=pl.CostEstimate(flops=flops, bytes_accessed=moved, transcendentals=0),
        compiler_params=pltpu.CompilerParams(vmem_limit_bytes=24 * 1024 * 1024),
        input_output_aliases=aliases or {},
    )(*ins)


def shape(dims, kind=F32):
    return jax.ShapeDtypeStruct(tuple(dims), kind)


def flip(x, axis, k):
    count = lax.axis_size(axis)
    return lax.ppermute(x, axis, [(i, i ^ k) for i in range(count)])


def few(count):
    return count <= 4


def share(x, axis):
    count = lax.axis_size(axis)
    if few(count):
        return [flip(x, axis, k) for k in reversed(range(1, count))]
    return [lax.all_gather(x, axis)]


def exchange(parts, axis):
    count = lax.axis_size(axis)
    if len(parts) == count - 1:
        return [flip(part, axis, count - 1 - i) for i, part in enumerate(parts)]
    return [lax.all_to_all(parts[0], axis, 0, 0, tiled=True)]


def parcel(count, dims, kind):
    if few(count):
        return [shape(dims, kind)] * (count - 1)
    return [shape((count, *dims), kind)]


def away(refs, count, me, k):
    return refs[count - 1 - k] if len(refs) == count - 1 else refs[0].at[me ^ k]


def place():
    return lax.axis_index("row"), lax.axis_index("col")


def loop(count, body):
    lax.fori_loop(0, count, lambda i, c: (body(i), c)[1], 0, unroll=count <= 18)


def start_kernel(z, rates, numbers, message, own, pad):
    pad[...] = jnp.zeros_like(pad)
    pad[:, 0 : z.local] = rates[...]
    packed = z.pack(pad[...])
    own[...] = packed
    number = numbers[...]
    high = (lax.shift_right_arithmetic(number, 7) + 1).astype(F32)
    low = (number & 127).astype(F32)
    blocks = []
    for f in range(z.frame):
        for r in (f, z.frame + f):
            blocks += [high[r : r + 1], low[r : r + 1]]
    fill = message.shape[0] - z.piece - 4 * z.frame
    extra = jnp.concatenate(blocks + [jnp.zeros((fill, BLOCK), F32)], axis=0)
    message[...] = jnp.concatenate([packed, extra], axis=0).astype(BF16)


def list_kernel(z, after, owner, post, pre, weights, ids):
    del after, weights
    ids[...] = jnp.concatenate([owner[0] * z.post + post[0], pre[0]], axis=1)


def prepare_kernel(z, count, *refs):
    mine, own, cots, table, stimuli = refs[:5]
    got = refs[5 : 5 + count]
    rates, gain, drive, cot_out, pad = refs[5 + count :]
    p, _ = place()
    highs = z.types // BLOCK
    t = jnp.transpose(table[...])
    t1 = t.astype(BF16)
    t2 = (t - t1.astype(F32)).astype(BF16)
    t3 = (t - t1.astype(F32) - t2.astype(F32)).astype(BF16)
    high_ids = lax.broadcasted_iota(jnp.int32, (highs, BLOCK), 0).astype(F32) + 1.0
    low_ids = lax.broadcasted_iota(jnp.int32, (BLOCK, BLOCK), 0).astype(F32)
    channel_ids = lax.broadcasted_iota(jnp.int32, (z.channels, BLOCK), 0).astype(F32)
    stim = stimuli[...]
    for k in range(z.rows):
        ref = mine if k == 0 else away(got, z.rows, p, k)
        rows = slice(k * z.piece, (k + 1) * z.piece)
        message = ref[...].astype(F32)
        gains, drives = [], []
        for f in range(z.frame):
            at = z.piece + 4 * f
            codes = message[at : at + 4]
            pick = (high_ids == codes[0:1]).astype(BF16)
            found = sum(jnp.dot(x, pick, preferred_element_type=F32) for x in (t1, t2, t3))
            line = jnp.sum(jnp.where(low_ids == codes[1:2], found, 0.0), axis=0, keepdims=True)
            gains.append(jnp.broadcast_to(line, (z.batch, BLOCK)))
            channel = (codes[2:3] - 1.0) * BLOCK + codes[3:4]
            chosen = (channel_ids == channel).astype(BF16)
            drives.append(jnp.dot(stim, chosen, preferred_element_type=F32))
        gain[rows] = z.pack(jnp.concatenate(gains, axis=1))
        for step in range(z.steps):
            part = [d[step * z.batch : (step + 1) * z.batch] for d in drives]
            drive[step, rows] = z.pack(jnp.concatenate(part, axis=1))
        rates[rows] = own[...] if k == 0 else message[0 : z.piece]
    pad[...] = jnp.zeros_like(pad)
    for step in range(z.steps):
        pad[:, 0 : z.local] = cots[step]
        cot_out[step] = z.pack(pad[...])


def multiply_forward(z, c, ids, weights, x, total, own, parts):
    total[...] = jnp.zeros_like(total)
    for s in range(z.slots):
        total[ids[0, s]] += lax.dot_general(
            x[ids[0, z.slots + s]], weights[s], (((1,), (1,)), ((), ())), preferred_element_type=F32
        )
    for k in range(z.cols):
        both = jnp.concatenate(
            [z.take_blocks(total, 0, c ^ k), z.take_blocks(total, z.post, c ^ k)], axis=0
        )
        if k == 0:
            own[...] = both
        else:
            away(parts, z.cols, c, k)[...] = both.astype(BF16)


def first_kernel(z, count, *refs):
    near_ids, weights, mine = refs[:3]
    got = refs[3 : 3 + count]
    x, own = refs[3 + count : 5 + count]
    parts, (sums, total, ids, sem) = refs[5 + count : -4], refs[-4:]
    bring = pltpu.make_async_copy(near_ids, ids, sem)
    bring.start()
    p, c = place()
    sums[...] = jnp.zeros_like(sums)
    for k in range(z.rows):
        ref = mine if k == 0 else away(got, z.rows, p, k)
        z.add_blocks(sums, 0, p ^ k, ref[...].astype(F32)[0 : z.piece])
    x[...] = sums[...].astype(BF16)
    bring.wait()
    multiply_forward(z, c, ids, weights, x, total, own, parts)


def forward_kernel(z, step, count, *refs):
    near_ids, weights, kept, rates, gain, drive = refs[:6]
    got = refs[6 : 6 + count]
    new, act_pair, cur_pair, x, own = refs[6 + count : 11 + count]
    parts, (sums, total, ids, sem) = refs[11 + count : -4], refs[-4:]
    bring = pltpu.make_async_copy(near_ids, ids, sem)
    bring.start()
    p, c = place()
    sums[...] = jnp.zeros_like(sums)

    def sent(k, side):
        ref = kept if k == 0 else away(got, z.rows, p, k)
        return ref[side * z.piece : (side + 1) * z.piece].astype(F32)

    for k in range(z.rows):
        rows = slice(k * z.piece, (k + 1) * z.piece)
        current = sent(k, 0) + sent(k ^ z.half, 1) + drive[step, rows]
        activity = jnp.tanh(gain[rows] * current)
        fresh = 0.5 * rates[rows] + 0.5 * activity
        new[rows] = fresh
        if k % z.half == 0:
            at = k // z.half * z.piece
            act_pair[at : at + z.piece] = activity
            cur_pair[at : at + z.piece] = current
        z.add_blocks(sums, 0, p ^ k, fresh)
    x[...] = sums[...].astype(BF16)
    bring.wait()
    multiply_forward(z, c, ids, weights, x, total, own, parts)


def sum_kernel(z, count, with_cot, *refs):
    own, got = refs[0], refs[1 : 1 + count]
    kept, message = refs[-2:]
    _, c = place()
    total = own[...]
    for k in range(1, z.cols):
        total = total + away(got, z.cols, c, k)[...].astype(F32)
    kept[...] = total
    if with_cot:
        cot = refs[1 + count]
        fill = message.shape[0] - z.pair - z.piece
        parts = [total, cot[z.steps - 1], jnp.zeros((fill, BLOCK), F32)]
        total = jnp.concatenate(parts, axis=0)
    message[...] = total.astype(BF16)


def pair_of(z, ref):
    at = z.half * z.piece
    return jnp.concatenate([ref[0 : z.piece], ref[at : at + z.piece]], axis=0)


def turn_kernel(z, kept, theirs, rates, gain, drive, cots, final, message, gain_pair, tally, base):
    other = theirs[...].astype(F32)
    swapped = jnp.concatenate([other[z.piece : z.pair], other[0 : z.piece]], axis=0)
    gains = pair_of(z, gain)
    current = kept[...] + swapped + pair_of(z, drive.at[z.steps - 1])
    activity = jnp.tanh(gains * current)
    fresh = 0.5 * rates[0 : z.piece] + 0.5 * activity[0 : z.piece]
    final[...] = fresh
    mine = cots[z.steps - 1]
    adjoint = jnp.concatenate([mine, other[z.pair : z.pair + z.piece]], axis=0)
    pressure = adjoint * 0.5 * (1.0 - activity * activity)
    message[...] = (gains * pressure).astype(BF16)
    gain_pair[...] = gains
    tally[...] = pressure * current
    base[...] = cots[z.steps - 2] + 0.5 * mine


def gather_post(z, c, mine, got, sums, d):
    sums[...] = jnp.zeros_like(sums)
    for k in range(z.cols):
        pair = (mine if k == 0 else away(got, z.cols, c, k))[...].astype(F32)
        z.add_blocks(sums, 0, c ^ k, pair[0 : z.piece])
        z.add_blocks(sums, z.post, c ^ k, pair[z.piece : z.pair])
    d[...] = sums[...].astype(BF16)


def back_kernel(z, count, *refs):
    near_ids, weights, base, mine = refs[:4]
    got = refs[4 : 4 + count]
    d, own = refs[4 + count : 6 + count]
    parts, (sums, total, ids, sem) = refs[6 + count : -4], refs[-4:]
    bring = pltpu.make_async_copy(near_ids, ids, sem)
    bring.start()
    p, c = place()
    gather_post(z, c, mine, got, sums, d)
    total[...] = jnp.zeros_like(total)
    bring.wait()
    for s in range(z.slots):
        total[ids[0, z.slots + s]] += jnp.dot(d[ids[0, s]], weights[s], preferred_element_type=F32)
    pieces = [z.take_blocks(total, 0, p ^ k) for k in range(z.rows)]
    for k in range(z.rows):
        other = pieces[k ^ z.half]
        if k == 0:
            own[...] = jnp.concatenate([pieces[0] + base[...], other], axis=0)
        else:
            if k == z.half:
                other = other + base[...]
            both = jnp.concatenate([pieces[k], other], axis=0)
            away(parts, z.rows, p, k)[...] = both.astype(BF16)


def adjoints(z, own, got):
    p, _ = place()
    total = own[...]
    for k in range(1, z.rows):
        total = total + away(got, z.rows, p, k)[...].astype(F32)
    return total


def delta_kernel(z, before, count, own, gain, act, cur, tally_in, cots, *refs):
    got, (message, tally, base) = refs[:count], refs[count:]
    adjoint = adjoints(z, own, got)
    activity = act[...]
    pressure = adjoint * 0.5 * (1.0 - activity * activity)
    message[...] = (gain[...] * pressure).astype(BF16)
    tally[...] = tally_in[...] + pressure * cur[...]
    base[...] = cots[before - 1] + 0.5 * adjoint[0 : z.piece]


def last_delta_kernel(z, count, own, gain, act, cur, tally_in, mine, partner, *refs):
    got, message = refs[:count], refs[count]
    adjoint = adjoints(z, own, got)
    activity = act[...]
    pressure = adjoint * 0.5 * (1.0 - activity * activity)
    tally = tally_in[...] + pressure * cur[...]
    rows = [gain[...] * pressure]
    lanes = lax.broadcasted_iota(jnp.int32, (1, BLOCK), 1)
    for side, ref in enumerate((mine, partner)):
        codes = ref[...].astype(F32)[z.piece :]
        begin = side * z.piece
        for f in range(z.frame):
            at = begin + f * z.batch
            if f < z.full:
                g = jnp.sum(tally[at : at + z.batch], axis=0, keepdims=True)
            else:
                packed = jnp.sum(tally[at : at + z.tall], axis=0, keepdims=True)
                g = packed
                for i in range(1, z.groups):
                    g = g + pltpu.roll(packed, BLOCK - i * z.rest, 1)
                g = jnp.where(lanes < z.rest, g, 0.0)
            g1 = g.astype(BF16).astype(F32)
            g2 = (g - g1).astype(BF16).astype(F32)
            rows += [codes[4 * f : 4 * f + 2], g1, g2, g - g1 - g2]
        rows.append(jnp.zeros((CODES - 5 * z.frame, BLOCK), F32))
    message[...] = jnp.concatenate(rows, axis=0).astype(BF16)


def table_kernel(z, count, *refs):
    mine, got, out = refs[1], refs[2:-1], refs[-1]
    _, c = place()
    highs = z.types // BLOCK
    high_ids = lax.broadcasted_iota(jnp.int32, (highs, BLOCK), 0).astype(F32) + 1.0
    low_ids = lax.broadcasted_iota(jnp.int32, (BLOCK, BLOCK), 0).astype(F32)
    total = jnp.zeros((3 * highs, BLOCK), F32)
    for k in range(z.cols):
        ref = mine if k == 0 else away(got, z.cols, c, k)
        extra = ref[z.pair :].astype(F32)
        for side in range(2):
            for f in range(z.frame):
                at = side * CODES + 5 * f
                hit = high_ids == extra[at : at + 1]
                terms = [jnp.where(hit, extra[at + 2 + i : at + 3 + i], 0.0) for i in range(3)]
                left = jnp.concatenate(terms, axis=0).astype(BF16)
                right = (low_ids == extra[at + 1 : at + 2]).astype(BF16)
                total = total + lax.dot_general(
                    left, right, (((1,), (1,)), ((), ())), preferred_element_type=F32
                )
    out[...] = total[0:highs] + total[highs : 2 * highs] + total[2 * highs :]


def lay_kernel(z, *refs):
    xs, ds = refs[: z.steps], refs[z.steps : 2 * z.steps - 1]
    last_rates, right, left, final = refs[2 * z.steps - 1 :]
    final[...] = z.unpack(last_rates[...])[:, 0 : z.local]
    n = z.batch
    deep = right.shape[1]
    rest = deep - z.steps * n

    def lay_right(q):
        for t in range(z.steps):
            right[q, t * n : (t + 1) * n] = xs[t][q]
        if rest:
            right[q, z.steps * n :] = jnp.zeros((rest, BLOCK), BF16)

    loop(z.pre, lay_right)

    def lay_left(q):
        parts = [jnp.zeros((n, BLOCK), F32)] + [d[q].astype(F32) for d in ds]
        if rest:
            parts.append(jnp.zeros((rest, BLOCK), F32))
        left[q] = jnp.transpose(jnp.concatenate(parts, axis=0)).astype(BF16)

    loop(2 * z.post, lay_left)


def grad_kernel(z, count, per_step, *refs):
    near_ids, right, later, mine = refs[:4]
    got = refs[4 : 4 + count]
    left, out, sums, d0, ids, sem = refs[4 + count :]
    n = z.batch
    deep = right.shape[1]

    @pl.when(pl.program_id(0) == 0)
    def _():
        bring = pltpu.make_async_copy(near_ids, ids, sem)
        bring.start()
        _, c = place()
        gather_post(z, c, mine, got, sums, d0)
        lanes = lax.broadcasted_iota(jnp.int32, (BLOCK, deep), 1)

        def lay_left(q):
            whole = jnp.concatenate([sums[q], jnp.zeros((deep - n, BLOCK), F32)], axis=0)
            turned = jnp.transpose(whole)
            left[q] = jnp.where(lanes < n, turned, later[q].astype(F32)).astype(BF16)

        loop(2 * z.post, lay_left)
        bring.wait()

    products(z, pl.program_id(0) * per_step, per_step, ids, left, right, out)


def products(z, begin, count, ids, left, right, out):
    for s in range(count):
        product = jnp.dot(
            left[ids[0, begin + s]], right[ids[0, z.slots + begin + s]], preferred_element_type=F32
        )
        out[s] = product.astype(BF16)


def rest_kernel(z, begin, per_step, near_ids, left, right, table, other, grads, out, sums, ids, sem):
    del grads
    bring = pltpu.make_async_copy(near_ids, ids, sem)
    bring.start()
    sums[...] = table[...] + other[...]
    bring.wait()
    products(z, begin + pl.program_id(0) * per_step, per_step, ids, left, right, out)


def shards(
    initial_rates,
    stimuli,
    cotangent,
    weight_blocks,
    slot_owner,
    slot_post,
    slot_pre,
    cell_type,
    type_gain,
    input_map,
):
    batch, local = initial_rates.shape
    slots = weight_blocks.shape[2]
    steps, _, channels = stimuli.shape
    types = type_gain.shape[0]
    z = Sizes(
        lax.axis_size("row"), lax.axis_size("col"), batch, local, slots, types, channels, steps
    )
    pair = (z.pair, BLOCK)
    product_flops = 2 * slots * batch * BLOCK * BLOCK
    opening = (z.piece + 4 * z.frame + 15) // 16 * 16
    closing = (z.pair + z.piece + 15) // 16 * 16

    fill = jnp.full((z.wide - local,), -BLOCK, jnp.int32)
    numbers = jnp.concatenate([cell_type, fill, input_map, fill])
    message, own_rates = call(
        functools.partial(start_kernel, z),
        [shape((opening, BLOCK), BF16), shape((z.piece, BLOCK))],
        [pltpu.VMEM((batch, z.wide), F32)],
        [initial_rates, numbers.reshape(2 * z.frame, BLOCK)],
    )
    got = share(message, "row")
    weights = weight_blocks.reshape(slots, BLOCK, BLOCK)
    (ids,) = call(
        functools.partial(list_kernel, z),
        [shape((1, 2 * slots), jnp.int32)],
        [],
        [message, slot_owner, slot_post, slot_pre, weights],
    )
    held_ids = [pltpu.SMEM((1, 2 * slots), jnp.int32), pltpu.SemaphoreType.DMA]
    if few(z.rows):
        partner_message = got[z.rows - 1 - z.half]
    else:
        partner_message = flip(message, "row", z.half)
    pre_sums = pltpu.VMEM((z.pre, batch, BLOCK), F32)
    post_sums = pltpu.VMEM((2 * z.post, batch, BLOCK), F32)
    x_shape = shape((z.pre, batch, BLOCK), BF16)
    row_parts = parcel(z.rows, pair, BF16)
    col_parts = [shape(pair), *parcel(z.cols, pair, BF16)]
    x, own, *parts = call(
        functools.partial(first_kernel, z, len(got)),
        [x_shape, *col_parts],
        [pre_sums, post_sums, *held_ids],
        [ids, weights, message, *got],
        flops=product_flops,
    )
    every = (z.rows * z.piece, BLOCK)
    rates, gain, drive, cots = call(
        functools.partial(prepare_kernel, z, len(got)),
        [shape(every), shape(every), shape((steps, *every)), shape((steps, z.piece, BLOCK))],
        [pltpu.VMEM((batch, z.wide), F32)],
        [
            message,
            own_rates,
            cotangent,
            type_gain.reshape(types // BLOCK, BLOCK),
            stimuli.reshape(steps * batch, channels),
            *got,
        ],
    )
    xs, acts, curs = [x], [], []
    for t in range(steps):
        last = t == steps - 1
        got = exchange(parts, "col")
        kept, sent = call(
            functools.partial(sum_kernel, z, len(got), last),
            [shape(pair), shape((closing, BLOCK) if last else pair, BF16)],
            [],
            [own, *got] + ([cots] if last else []),
        )
        if last:
            break
        got = share(sent, "row")
        rates, act, cur, x, own, *parts = call(
            functools.partial(forward_kernel, z, t, len(got)),
            [shape(every), shape(pair), shape(pair), x_shape, *col_parts],
            [pre_sums, post_sums, *held_ids],
            [ids, weights, kept, rates, gain, drive, *got],
            flops=product_flops,
        )
        xs.append(x)
        acts.append(act)
        curs.append(cur)
    theirs = flip(sent, "row", z.half)
    last_rates, delta, gain, tally, base = call(
        functools.partial(turn_kernel, z),
        [
            shape((z.piece, BLOCK)),
            shape(pair, BF16),
            shape(pair),
            shape(pair),
            shape((z.piece, BLOCK)),
        ],
        [],
        [kept, theirs, rates, gain, drive, cots],
    )
    ds = []
    for t in reversed(range(1, steps)):
        got = share(delta, "col")
        d, own, *parts = call(
            functools.partial(back_kernel, z, len(got)),
            [shape((2 * z.post, batch, BLOCK), BF16), shape(pair), *row_parts],
            [post_sums, pre_sums, *held_ids],
            [ids, weights, base, delta, *got],
            flops=product_flops,
        )
        ds.insert(0, d)
        got = exchange(parts, "row")
        before = t - 1
        if before > 0:
            delta, tally, base = call(
                functools.partial(delta_kernel, z, before, len(got)),
                [shape(pair, BF16), shape(pair), shape((z.piece, BLOCK))],
                [],
                [own, gain, acts[before], curs[before], tally, cots, *got],
            )
        else:
            (delta,) = call(
                functools.partial(last_delta_kernel, z, len(got)),
                [shape((z.pair + 2 * CODES, BLOCK), BF16)],
                [],
                [own, gain, acts[0], curs[0], tally, message, partner_message, *got],
            )
    got = share(delta, "col")
    grid = 4
    per_step = slots // grid
    deep = (steps * batch + BLOCK - 1) // BLOCK * BLOCK
    left_shape = shape((2 * z.post, BLOCK, deep), BF16)
    right, later, final_rates = call(
        functools.partial(lay_kernel, z),
        [shape((z.pre, deep, BLOCK), BF16), left_shape, shape((batch, local))],
        [],
        [*xs, *ds, last_rates],
    )
    (table,) = call(
        functools.partial(table_kernel, z, len(got)), [shape((types // BLOCK, BLOCK))], [], [right, delta, *got]
    )
    if z.half == 2:
        other = flip(table, "row", 1)
    else:
        total = lax.psum(table, "row")
        other = 0.5 * total - table

    ins = [ids, right, later, delta, *got]
    cost = pl.CostEstimate(
        flops=2 * slots * deep * BLOCK * BLOCK, bytes_accessed=4 * 1024 * 1024, transcendentals=0
    )
    grads = shape((slots, BLOCK, BLOCK), BF16)
    limit = pltpu.CompilerParams(vmem_limit_bytes=24 * 1024 * 1024)
    left, weight_grads = pl.pallas_call(
        functools.partial(grad_kernel, z, len(got), per_step),
        grid=(grid - 1,),
        out_shape=[left_shape, grads],
        in_specs=[VMEM] * len(ins),
        out_specs=[VMEM, pl.BlockSpec((per_step, BLOCK, BLOCK), lambda i: (i, 0, 0))],
        scratch_shapes=[post_sums, pltpu.VMEM((2 * z.post, batch, BLOCK), BF16), *held_ids],
        cost_estimate=cost,
        compiler_params=limit,
    )(*ins)
    ins = [ids, left, right, table, other, weight_grads]
    weight_grads, table = pl.pallas_call(
        functools.partial(rest_kernel, z, slots - per_step, per_step),
        grid=(1,),
        out_shape=[grads, shape(table.shape)],
        in_specs=[VMEM] * 5 + [pl.BlockSpec(memory_space=pl.ANY)],
        out_specs=[pl.BlockSpec((per_step, BLOCK, BLOCK), lambda i: (i + grid - 1, 0, 0)), VMEM],
        scratch_shapes=held_ids,
        input_output_aliases={5: 0},
        cost_estimate=cost,
        compiler_params=limit,
    )(*ins)
    gain_grads = table.reshape(types)
    return (final_rates, weight_grads.reshape(1, 1, slots, BLOCK, BLOCK), gain_grads)


def solution(mesh):
    in_specs = (
        P("groups", ("row", "col")),
        P(None, "groups", None),
        P(None, "groups", ("row", "col")),
        P("row", "col", None, None, None),
        P("row", "col", None),
        P("row", "col", None),
        P("row", "col", None),
        P(("row", "col")),
        P(),
        P(("row", "col")),
    )
    out_specs = (P("groups", ("row", "col")), P("row", "col", "groups", None, None), P("groups"))
    return jax.shard_map(shards, mesh=mesh, in_specs=in_specs, out_specs=out_specs, check_vma=False)
```

```python
import functools

import jax
import jax.numpy as jnp
from jax import lax
from jax.experimental import pallas as pl
from jax.experimental.pallas import tpu as pltpu
from jax.sharding import PartitionSpec as P

BLOCK = 128
CODES = 16
F32 = jnp.float32
BF16 = jnp.bfloat16
VMEM = pl.BlockSpec(memory_space=pltpu.VMEM)


class Sizes:
    def __init__(self, row_count, col_count, batch, local, slots, types, channels, steps):
        self.rows, self.cols = row_count, col_count
        self.batch, self.local, self.slots = batch, local, slots
        self.types, self.channels, self.steps = types, channels, steps
        self.post = col_count * local // BLOCK
        self.pre = row_count * local // BLOCK
        self.half = row_count // 2
        self.full, self.rest = local // BLOCK, local % BLOCK
        self.groups = BLOCK // self.rest
        self.tall = batch // self.groups
        self.piece = self.full * batch + self.tall
        self.pair = 2 * self.piece
        offsets = [local * i % BLOCK for i in range(max(row_count, col_count))]
        self.frame = (max(offsets) + local + BLOCK - 1) // BLOCK
        self.wide = self.frame * BLOCK
        assert 2 * slots == BLOCK and BLOCK % self.rest == 0 and batch % (8 * self.groups) == 0
        assert self.frame == self.full + 1 and self.pair % 16 == 0

    def first(self, i):
        return lax.div(i * self.local, jnp.int32(BLOCK))

    def offset(self, i):
        return lax.rem(i * self.local, jnp.int32(BLOCK))

    def pack(self, whole):
        parts = [whole[:, i * BLOCK : (i + 1) * BLOCK] for i in range(self.full)]
        tail = whole[:, self.full * BLOCK :]
        lanes = lax.broadcasted_iota(jnp.int32, (self.tall, BLOCK), 1)
        joined = tail[0 : self.tall]
        for g in range(1, self.groups):
            moved = pltpu.roll(tail[g * self.tall : (g + 1) * self.tall], g * self.rest, 1)
            joined = jnp.where(lanes < g * self.rest, joined, moved)
        return jnp.concatenate(parts + [joined], axis=0)

    def unpack(self, piece):
        parts = [piece[i * self.batch : (i + 1) * self.batch] for i in range(self.full)]
        joined = piece[self.full * self.batch :]
        lanes = lax.broadcasted_iota(jnp.int32, (self.tall, BLOCK), 1)
        tails = []
        for g in range(self.groups):
            moved = joined if g == 0 else pltpu.roll(joined, BLOCK - g * self.rest, 1)
            tails.append(jnp.where(lanes < self.rest, moved, 0.0))
        return jnp.concatenate(parts + [jnp.concatenate(tails, axis=0)], axis=1)

    def add_blocks(self, target, base, i, piece):
        turned = pltpu.roll(self.unpack(piece), self.offset(i), 1)
        first = base + self.first(i)
        for f in range(self.frame):
            target[first + f] += turned[:, f * BLOCK : (f + 1) * BLOCK]

    def take_blocks(self, source, base, i):
        first = base + self.first(i)
        whole = jnp.concatenate([source[first + f] for f in range(self.frame)], axis=1)
        back = lax.rem(self.wide - self.offset(i), jnp.int32(self.wide))
        return self.pack(pltpu.roll(whole, back, 1))


def call(body, outs, scratch, ins, places=None, flops=0, out_specs=None, aliases=None):
    specs = [(places or {}).get(i, VMEM) for i in range(len(ins))]
    moved = sum(x.size * x.dtype.itemsize for x in ins) + sum(x.size * x.dtype.itemsize for x in outs)
    return pl.pallas_call(
        body,
        out_shape=outs,
        in_specs=specs,
        out_specs=out_specs or [VMEM] * len(outs),
        scratch_shapes=scratch,
        cost_estimate=pl.CostEstimate(flops=flops, bytes_accessed=moved, transcendentals=0),
        compiler_params=pltpu.CompilerParams(vmem_limit_bytes=24 * 1024 * 1024),
        input_output_aliases=aliases or {},
    )(*ins)


def shape(dims, kind=F32):
    return jax.ShapeDtypeStruct(tuple(dims), kind)


def flip(x, axis, k):
    count = lax.axis_size(axis)
    return lax.ppermute(x, axis, [(i, i ^ k) for i in range(count)])


def few(count):
    return count <= 4


def share(x, axis):
    count = lax.axis_size(axis)
    if few(count):
        return [flip(x, axis, k) for k in reversed(range(1, count))]
    return [lax.all_gather(x, axis)]


def exchange(parts, axis):
    count = lax.axis_size(axis)
    if len(parts) == count - 1:
        return [flip(part, axis, count - 1 - i) for i, part in enumerate(parts)]
    return [lax.all_to_all(parts[0], axis, 0, 0, tiled=True)]


def parcel(count, dims, kind):
    if few(count):
        return [shape(dims, kind)] * (count - 1)
    return [shape((count, *dims), kind)]


def away(refs, count, me, k):
    return refs[count - 1 - k] if len(refs) == count - 1 else refs[0].at[me ^ k]


def place():
    return lax.axis_index("row"), lax.axis_index("col")


def loop(count, body):
    lax.fori_loop(0, count, lambda i, c: (body(i), c)[1], 0, unroll=count <= 18)


def start_kernel(z, rates, numbers, message, own, ids, pad):
    pad[...] = jnp.zeros_like(pad)
    pad[:, 0 : z.local] = rates[...]
    packed = z.pack(pad[...])
    own[...] = packed
    number = numbers[...]
    at = 2 * z.frame
    lists = [number[at + r : at + r + 1] for r in range(3)]
    pre_lanes = pltpu.roll(lists[2], z.slots, 1)
    lanes = lax.broadcasted_iota(jnp.int32, (1, BLOCK), 1)
    ids[...] = jnp.where(lanes < z.slots, lists[0] * z.post + lists[1], pre_lanes)
    high = (lax.shift_right_arithmetic(number, 7) + 1).astype(F32)
    low = (number & 127).astype(F32)
    blocks = []
    for f in range(z.frame):
        for r in (f, z.frame + f):
            blocks += [high[r : r + 1], low[r : r + 1]]
    fill = message.shape[0] - z.piece - 4 * z.frame
    extra = jnp.concatenate(blocks + [jnp.zeros((fill, BLOCK), F32)], axis=0)
    message[...] = jnp.concatenate([packed, extra], axis=0).astype(BF16)


def turn_weights_kernel(z, after, weights, out):
    del after

    def one(s):
        out[s] = jnp.transpose(weights[s])

    lax.fori_loop(0, z.slots, lambda i, c: (one(i), c)[1], 0, unroll=8)


def prepare_kernel(z, count, *refs):
    mine, own, cots, table, stimuli = refs[:5]
    got = refs[5 : 5 + count]
    rates, gain, drive, cot_out, pad = refs[5 + count :]
    p, _ = place()
    highs = z.types // BLOCK
    t = jnp.transpose(table[...])
    t1 = t.astype(BF16)
    t2 = (t - t1.astype(F32)).astype(BF16)
    t3 = (t - t1.astype(F32) - t2.astype(F32)).astype(BF16)
    high_ids = lax.broadcasted_iota(jnp.int32, (highs, BLOCK), 0).astype(F32) + 1.0
    low_ids = lax.broadcasted_iota(jnp.int32, (BLOCK, BLOCK), 0).astype(F32)
    channel_ids = lax.broadcasted_iota(jnp.int32, (z.channels, BLOCK), 0).astype(F32)
    stim = stimuli[...]
    for k in range(z.rows):
        ref = mine if k == 0 else away(got, z.rows, p, k)
        rows = slice(k * z.piece, (k + 1) * z.piece)
        message = ref[...].astype(F32)
        gains, drives = [], []
        for f in range(z.frame):
            at = z.piece + 4 * f
            codes = message[at : at + 4]
            pick = (high_ids == codes[0:1]).astype(BF16)
            found = sum(jnp.dot(x, pick, preferred_element_type=F32) for x in (t1, t2, t3))
            line = jnp.sum(jnp.where(low_ids == codes[1:2], found, 0.0), axis=0, keepdims=True)
            gains.append(jnp.broadcast_to(line, (z.batch, BLOCK)))
            channel = (codes[2:3] - 1.0) * BLOCK + codes[3:4]
            chosen = (channel_ids == channel).astype(BF16)
            drives.append(jnp.dot(stim, chosen, preferred_element_type=F32))
        gain[rows] = z.pack(jnp.concatenate(gains, axis=1))
        for step in range(z.steps):
            part = [d[step * z.batch : (step + 1) * z.batch] for d in drives]
            drive[step, rows] = z.pack(jnp.concatenate(part, axis=1))
        rates[rows] = own[...] if k == 0 else message[0 : z.piece]
    pad[...] = jnp.zeros_like(pad)
    for step in range(z.steps):
        pad[:, 0 : z.local] = cots[step]
        cot_out[step] = z.pack(pad[...])


def multiply_forward(z, c, ids, weights, x, total, own, parts):
    total[...] = jnp.zeros_like(total)
    for s in range(z.slots):
        total[ids[0, s]] += jnp.dot(x[ids[0, z.slots + s]], weights[s], preferred_element_type=F32)
    for k in range(z.cols):
        both = jnp.concatenate(
            [z.take_blocks(total, 0, c ^ k), z.take_blocks(total, z.post, c ^ k)], axis=0
        )
        if k == 0:
            own[...] = both
        else:
            away(parts, z.cols, c, k)[...] = both.astype(BF16)


def first_kernel(z, count, *refs):
    near_ids, weights, mine = refs[:3]
    got = refs[3 : 3 + count]
    x, own = refs[3 + count : 5 + count]
    parts, (sums, total, ids, sem) = refs[5 + count : -4], refs[-4:]
    bring = pltpu.make_async_copy(near_ids, ids, sem)
    bring.start()
    p, c = place()
    sums[...] = jnp.zeros_like(sums)
    for k in range(z.rows):
        ref = mine if k == 0 else away(got, z.rows, p, k)
        z.add_blocks(sums, 0, p ^ k, ref[...].astype(F32)[0 : z.piece])
    x[...] = sums[...].astype(BF16)
    bring.wait()
    multiply_forward(z, c, ids, weights, x, total, own, parts)


def forward_kernel(z, step, count, *refs):
    near_ids, weights, kept, rates, gain, drive = refs[:6]
    got = refs[6 : 6 + count]
    new, act_pair, cur_pair, x, own = refs[6 + count : 11 + count]
    parts, (sums, total, ids, sem) = refs[11 + count : -4], refs[-4:]
    bring = pltpu.make_async_copy(near_ids, ids, sem)
    bring.start()
    p, c = place()
    sums[...] = jnp.zeros_like(sums)

    def sent(k, side):
        ref = kept if k == 0 else away(got, z.rows, p, k)
        return ref[side * z.piece : (side + 1) * z.piece].astype(F32)

    for k in range(z.rows):
        rows = slice(k * z.piece, (k + 1) * z.piece)
        current = sent(k, 0) + sent(k ^ z.half, 1) + drive[step, rows]
        activity = jnp.tanh(gain[rows] * current)
        fresh = 0.5 * rates[rows] + 0.5 * activity
        new[rows] = fresh
        if k % z.half == 0:
            at = k // z.half * z.piece
            act_pair[at : at + z.piece] = activity
            cur_pair[at : at + z.piece] = current
        z.add_blocks(sums, 0, p ^ k, fresh)
    x[...] = sums[...].astype(BF16)
    bring.wait()
    multiply_forward(z, c, ids, weights, x, total, own, parts)


def sum_kernel(z, count, with_cot, *refs):
    own, got = refs[0], refs[1 : 1 + count]
    kept, message = refs[-2:]
    _, c = place()
    total = own[...]
    for k in range(1, z.cols):
        total = total + away(got, z.cols, c, k)[...].astype(F32)
    kept[...] = total
    if with_cot:
        cot = refs[1 + count]
        fill = message.shape[0] - z.pair - z.piece
        parts = [total, cot[z.steps - 1], jnp.zeros((fill, BLOCK), F32)]
        total = jnp.concatenate(parts, axis=0)
    message[...] = total.astype(BF16)


def pair_of(z, ref):
    at = z.half * z.piece
    return jnp.concatenate([ref[0 : z.piece], ref[at : at + z.piece]], axis=0)


def turn_kernel(z, kept, theirs, rates, gain, drive, cots, final, message, gain_pair, tally, base):
    other = theirs[...].astype(F32)
    swapped = jnp.concatenate([other[z.piece : z.pair], other[0 : z.piece]], axis=0)
    gains = pair_of(z, gain)
    current = kept[...] + swapped + pair_of(z, drive.at[z.steps - 1])
    activity = jnp.tanh(gains * current)
    fresh = 0.5 * rates[0 : z.piece] + 0.5 * activity[0 : z.piece]
    final[...] = fresh
    mine = cots[z.steps - 1]
    adjoint = jnp.concatenate([mine, other[z.pair : z.pair + z.piece]], axis=0)
    pressure = adjoint * 0.5 * (1.0 - activity * activity)
    message[...] = (gains * pressure).astype(BF16)
    gain_pair[...] = gains
    tally[...] = pressure * current
    base[...] = cots[z.steps - 2] + 0.5 * mine


def gather_post(z, c, mine, got, sums, d):
    sums[...] = jnp.zeros_like(sums)
    for k in range(z.cols):
        pair = (mine if k == 0 else away(got, z.cols, c, k))[...].astype(F32)
        z.add_blocks(sums, 0, c ^ k, pair[0 : z.piece])
        z.add_blocks(sums, z.post, c ^ k, pair[z.piece : z.pair])
    d[...] = sums[...].astype(BF16)


def back_kernel(z, count, *refs):
    near_ids, weights, base, mine = refs[:4]
    got = refs[4 : 4 + count]
    d, own = refs[4 + count : 6 + count]
    parts, (sums, total, ids, sem) = refs[6 + count : -4], refs[-4:]
    bring = pltpu.make_async_copy(near_ids, ids, sem)
    bring.start()
    p, c = place()
    gather_post(z, c, mine, got, sums, d)
    total[...] = jnp.zeros_like(total)
    bring.wait()
    for s in range(z.slots):
        total[ids[0, z.slots + s]] += jnp.dot(d[ids[0, s]], weights[s], preferred_element_type=F32)
    pieces = [z.take_blocks(total, 0, p ^ k) for k in range(z.rows)]
    for k in range(z.rows):
        other = pieces[k ^ z.half]
        if k == 0:
            own[...] = jnp.concatenate([pieces[0] + base[...], other], axis=0)
        else:
            if k == z.half:
                other = other + base[...]
            both = jnp.concatenate([pieces[k], other], axis=0)
            away(parts, z.rows, p, k)[...] = both.astype(BF16)


def adjoints(z, own, got):
    p, _ = place()
    total = own[...]
    for k in range(1, z.rows):
        total = total + away(got, z.rows, p, k)[...].astype(F32)
    return total


def delta_kernel(z, before, count, own, gain, act, cur, tally_in, cots, *refs):
    got, (message, tally, base) = refs[:count], refs[count:]
    adjoint = adjoints(z, own, got)
    activity = act[...]
    pressure = adjoint * 0.5 * (1.0 - activity * activity)
    message[...] = (gain[...] * pressure).astype(BF16)
    tally[...] = tally_in[...] + pressure * cur[...]
    base[...] = cots[before - 1] + 0.5 * adjoint[0 : z.piece]


def last_delta_kernel(z, count, own, gain, act, cur, tally_in, mine, partner, *refs):
    got, message = refs[:count], refs[count]
    adjoint = adjoints(z, own, got)
    activity = act[...]
    pressure = adjoint * 0.5 * (1.0 - activity * activity)
    tally = tally_in[...] + pressure * cur[...]
    rows = [gain[...] * pressure]
    lanes = lax.broadcasted_iota(jnp.int32, (1, BLOCK), 1)
    for side, ref in enumerate((mine, partner)):
        codes = ref[...].astype(F32)[z.piece :]
        begin = side * z.piece
        for f in range(z.frame):
            at = begin + f * z.batch
            if f < z.full:
                g = jnp.sum(tally[at : at + z.batch], axis=0, keepdims=True)
            else:
                packed = jnp.sum(tally[at : at + z.tall], axis=0, keepdims=True)
                g = packed
                for i in range(1, z.groups):
                    g = g + pltpu.roll(packed, BLOCK - i * z.rest, 1)
                g = jnp.where(lanes < z.rest, g, 0.0)
            g1 = g.astype(BF16).astype(F32)
            g2 = (g - g1).astype(BF16).astype(F32)
            rows += [codes[4 * f : 4 * f + 2], g1, g2, g - g1 - g2]
        rows.append(jnp.zeros((CODES - 5 * z.frame, BLOCK), F32))
    message[...] = jnp.concatenate(rows, axis=0).astype(BF16)


def extras_kernel(z, count, right, mine, *refs):
    del right
    got, out = refs[:-1], refs[-1]
    _, c = place()
    for k in range(z.cols):
        ref = mine if k == 0 else away(got, z.cols, c, k)
        out[2 * CODES * k : 2 * CODES * (k + 1)] = ref[z.pair :]


def add_table(z, extras, out):
    highs = z.types // BLOCK
    high_ids = lax.broadcasted_iota(jnp.int32, (highs, BLOCK), 0).astype(F32) + 1.0
    low_ids = lax.broadcasted_iota(jnp.int32, (BLOCK, BLOCK), 0).astype(F32)
    total = jnp.zeros((3 * highs, BLOCK), F32)
    for ref in extras:
        for side in range(2 * z.cols):
            extra = ref[side * CODES : (side + 1) * CODES].astype(F32)
            for f in range(z.frame):
                at = 5 * f
                hit = high_ids == extra[at : at + 1]
                terms = [jnp.where(hit, extra[at + 2 + i : at + 3 + i], 0.0) for i in range(3)]
                left = jnp.concatenate(terms, axis=0).astype(BF16)
                right = (low_ids == extra[at + 1 : at + 2]).astype(BF16)
                total = total + lax.dot_general(
                    left, right, (((1,), (1,)), ((), ())), preferred_element_type=F32
                )
    out[...] = total[0:highs] + total[highs : 2 * highs] + total[2 * highs :]


def lay_kernel(z, *refs):
    xs, ds = refs[: z.steps], refs[z.steps : 2 * z.steps - 1]
    last_rates, right, left, final = refs[2 * z.steps - 1 :]
    final[...] = z.unpack(last_rates[...])[:, 0 : z.local]
    n = z.batch
    deep = right.shape[1]
    rest = deep - z.steps * n

    def lay_right(q):
        for t in range(z.steps):
            right[q, t * n : (t + 1) * n] = xs[t][q]
        if rest:
            right[q, z.steps * n :] = jnp.zeros((rest, BLOCK), BF16)

    loop(z.pre, lay_right)

    def lay_left(q):
        parts = [jnp.zeros((n, BLOCK), F32)] + [d[q].astype(F32) for d in ds]
        if rest:
            parts.append(jnp.zeros((rest, BLOCK), F32))
        left[q] = jnp.transpose(jnp.concatenate(parts, axis=0)).astype(BF16)

    loop(2 * z.post, lay_left)


def grad_kernel(z, count, per_step, *refs):
    near_ids, right, later, mine = refs[:4]
    got = refs[4 : 4 + count]
    left, out, sums, d0, ids, sem = refs[4 + count :]
    n = z.batch
    deep = right.shape[1]

    @pl.when(pl.program_id(0) == 0)
    def _():
        bring = pltpu.make_async_copy(near_ids, ids, sem)
        bring.start()
        _, c = place()
        gather_post(z, c, mine, got, sums, d0)
        lanes = lax.broadcasted_iota(jnp.int32, (BLOCK, deep), 1)

        def lay_left(q):
            whole = jnp.concatenate([sums[q], jnp.zeros((deep - n, BLOCK), F32)], axis=0)
            turned = jnp.transpose(whole)
            left[q] = jnp.where(lanes < n, turned, later[q].astype(F32)).astype(BF16)

        loop(2 * z.post, lay_left)
        bring.wait()

    products(z, pl.program_id(0) * per_step, per_step, ids, left, right, out)


def products(z, begin, count, ids, left, right, out):
    for s in range(count):
        product = jnp.dot(
            left[ids[0, begin + s]], right[ids[0, z.slots + begin + s]], preferred_element_type=F32
        )
        out[s] = product.astype(BF16)


def rest_kernel(z, count, begin, per_step, near_ids, left, right, grads, *refs):
    del grads
    extras = refs[:count]
    out, table, ids, sem = refs[count:]
    bring = pltpu.make_async_copy(near_ids, ids, sem)
    bring.start()
    add_table(z, extras, table)
    bring.wait()
    products(z, begin + pl.program_id(0) * per_step, per_step, ids, left, right, out)


def shards(
    initial_rates,
    stimuli,
    cotangent,
    weight_blocks,
    slot_owner,
    slot_post,
    slot_pre,
    cell_type,
    type_gain,
    input_map,
):
    batch, local = initial_rates.shape
    slots = weight_blocks.shape[2]
    steps, _, channels = stimuli.shape
    types = type_gain.shape[0]
    z = Sizes(
        lax.axis_size("row"), lax.axis_size("col"), batch, local, slots, types, channels, steps
    )
    pair = (z.pair, BLOCK)
    product_flops = 2 * slots * batch * BLOCK * BLOCK
    opening = (z.piece + 4 * z.frame + 15) // 16 * 16
    closing = (z.pair + z.piece + 15) // 16 * 16

    fill = jnp.full((z.wide - local,), -BLOCK, jnp.int32)
    blank = jnp.zeros((BLOCK - slots,), jnp.int32)
    lists = [cell_type, fill, input_map, fill]
    for x in (slot_owner, slot_post, slot_pre):
        lists += [x.reshape(slots), blank]
    numbers = jnp.concatenate(lists)
    message, own_rates, ids = call(
        functools.partial(start_kernel, z),
        [
            shape((opening, BLOCK), BF16),
            shape((z.piece, BLOCK)),
            shape((1, 2 * slots), jnp.int32),
        ],
        [pltpu.VMEM((batch, z.wide), F32)],
        [initial_rates, numbers.reshape(numbers.size // BLOCK, BLOCK)],
    )
    got = share(message, "row")
    weights = weight_blocks.reshape(slots, BLOCK, BLOCK)
    (turned,) = call(
        functools.partial(turn_weights_kernel, z),
        [shape((slots, BLOCK, BLOCK), BF16)],
        [],
        [message, weights],
    )
    held_ids = [pltpu.SMEM((1, 2 * slots), jnp.int32), pltpu.SemaphoreType.DMA]
    if few(z.rows):
        partner_message = got[z.rows - 1 - z.half]
    else:
        partner_message = flip(message, "row", z.half)
    pre_sums = pltpu.VMEM((z.pre, batch, BLOCK), F32)
    post_sums = pltpu.VMEM((2 * z.post, batch, BLOCK), F32)
    x_shape = shape((z.pre, batch, BLOCK), BF16)
    row_parts = parcel(z.rows, pair, BF16)
    col_parts = [shape(pair), *parcel(z.cols, pair, BF16)]
    x, own, *parts = call(
        functools.partial(first_kernel, z, len(got)),
        [x_shape, *col_parts],
        [pre_sums, post_sums, *held_ids],
        [ids, turned, message, *got],
        flops=product_flops,
    )
    every = (z.rows * z.piece, BLOCK)
    rates, gain, drive, cots = call(
        functools.partial(prepare_kernel, z, len(got)),
        [shape(every), shape(every), shape((steps, *every)), shape((steps, z.piece, BLOCK))],
        [pltpu.VMEM((batch, z.wide), F32)],
        [
            message,
            own_rates,
            cotangent,
            type_gain.reshape(types // BLOCK, BLOCK),
            stimuli.reshape(steps * batch, channels),
            *got,
        ],
    )
    xs, acts, curs = [x], [], []
    for t in range(steps):
        last = t == steps - 1
        got = exchange(parts, "col")
        kept, sent = call(
            functools.partial(sum_kernel, z, len(got), last),
            [shape(pair), shape((closing, BLOCK) if last else pair, BF16)],
            [],
            [own, *got] + ([cots] if last else []),
        )
        if last:
            break
        got = share(sent, "row")
        rates, act, cur, x, own, *parts = call(
            functools.partial(forward_kernel, z, t, len(got)),
            [shape(every), shape(pair), shape(pair), x_shape, *col_parts],
            [pre_sums, post_sums, *held_ids],
            [ids, turned, kept, rates, gain, drive, *got],
            flops=product_flops,
        )
        xs.append(x)
        acts.append(act)
        curs.append(cur)
    theirs = flip(sent, "row", z.half)
    last_rates, delta, gain, tally, base = call(
        functools.partial(turn_kernel, z),
        [
            shape((z.piece, BLOCK)),
            shape(pair, BF16),
            shape(pair),
            shape(pair),
            shape((z.piece, BLOCK)),
        ],
        [],
        [kept, theirs, rates, gain, drive, cots],
    )
    ds = []
    for t in reversed(range(1, steps)):
        got = share(delta, "col")
        d, own, *parts = call(
            functools.partial(back_kernel, z, len(got)),
            [shape((2 * z.post, batch, BLOCK), BF16), shape(pair), *row_parts],
            [post_sums, pre_sums, *held_ids],
            [ids, weights, base, delta, *got],
            flops=product_flops,
        )
        ds.insert(0, d)
        got = exchange(parts, "row")
        before = t - 1
        if before > 0:
            delta, tally, base = call(
                functools.partial(delta_kernel, z, before, len(got)),
                [shape(pair, BF16), shape(pair), shape((z.piece, BLOCK))],
                [],
                [own, gain, acts[before], curs[before], tally, cots, *got],
            )
        else:
            (delta,) = call(
                functools.partial(last_delta_kernel, z, len(got)),
                [shape((z.pair + 2 * CODES, BLOCK), BF16)],
                [],
                [own, gain, acts[0], curs[0], tally, message, partner_message, *got],
            )
    got = share(delta, "col")
    grid = 4
    per_step = slots // grid
    deep = (steps * batch + BLOCK - 1) // BLOCK * BLOCK
    left_shape = shape((2 * z.post, BLOCK, deep), BF16)
    right, later, final_rates = call(
        functools.partial(lay_kernel, z),
        [shape((z.pre, deep, BLOCK), BF16), left_shape, shape((batch, local))],
        [],
        [*xs, *ds, last_rates],
    )
    (extras,) = call(
        functools.partial(extras_kernel, z, len(got)),
        [shape((2 * CODES * z.cols, BLOCK), BF16)],
        [],
        [right, delta, *got],
    )
    all_extras = [extras, flip(extras, "row", 1)] if z.half == 2 else [extras]
    ins = [ids, right, later, delta, *got]
    cost = pl.CostEstimate(
        flops=2 * slots * deep * BLOCK * BLOCK, bytes_accessed=4 * 1024 * 1024, transcendentals=0
    )
    grads = shape((slots, BLOCK, BLOCK), BF16)
    limit = pltpu.CompilerParams(vmem_limit_bytes=24 * 1024 * 1024)
    left, weight_grads = pl.pallas_call(
        functools.partial(grad_kernel, z, len(got), per_step),
        grid=(grid - 1,),
        out_shape=[left_shape, grads],
        in_specs=[VMEM] * len(ins),
        out_specs=[VMEM, pl.BlockSpec((per_step, BLOCK, BLOCK), lambda i: (i, 0, 0))],
        scratch_shapes=[post_sums, pltpu.VMEM((2 * z.post, batch, BLOCK), BF16), *held_ids],
        cost_estimate=cost,
        compiler_params=limit,
    )(*ins)
    ins = [ids, left, right, weight_grads, *all_extras]
    weight_grads, table = pl.pallas_call(
        functools.partial(rest_kernel, z, len(all_extras), slots - per_step, per_step),
        grid=(1,),
        out_shape=[grads, shape((types // BLOCK, BLOCK))],
        in_specs=[VMEM] * 3 + [pl.BlockSpec(memory_space=pl.ANY)] + [VMEM] * len(all_extras),
        out_specs=[pl.BlockSpec((per_step, BLOCK, BLOCK), lambda i: (i + grid - 1, 0, 0)), VMEM],
        scratch_shapes=held_ids,
        input_output_aliases={3: 0},
        cost_estimate=cost,
        compiler_params=limit,
    )(*ins)
    if z.half != 2:
        table = 0.5 * lax.psum(table, "row")
    gain_grads = table.reshape(types)
    return (final_rates, weight_grads.reshape(1, 1, slots, BLOCK, BLOCK), gain_grads)


def solution(mesh):
    in_specs = (
        P("groups", ("row", "col")),
        P(None, "groups", None),
        P(None, "groups", ("row", "col")),
        P("row", "col", None, None, None),
        P("row", "col", None),
        P("row", "col", None),
        P("row", "col", None),
        P(("row", "col")),
        P(),
        P(("row", "col")),
    )
    out_specs = (P("groups", ("row", "col")), P("row", "col", "groups", None, None), P("groups"))
    return jax.shard_map(shards, mesh=mesh, in_specs=in_specs, out_specs=out_specs, check_vma=False)
```

```python
import functools

import jax
import jax.numpy as jnp
from jax import lax
from jax.experimental import pallas as pl
from jax.experimental.pallas import tpu as pltpu
from jax.sharding import PartitionSpec as P

BLOCK = 128
CODES = 16
F32 = jnp.float32
BF16 = jnp.bfloat16
VMEM = pl.BlockSpec(memory_space=pltpu.VMEM)


class Sizes:
    def __init__(self, row_count, col_count, batch, local, slots, types, channels, steps):
        self.rows, self.cols = row_count, col_count
        self.batch, self.local, self.slots = batch, local, slots
        self.types, self.channels, self.steps = types, channels, steps
        self.post = col_count * local // BLOCK
        self.pre = row_count * local // BLOCK
        self.half = row_count // 2
        self.full, self.rest = local // BLOCK, local % BLOCK
        self.groups = BLOCK // self.rest
        self.tall = batch // self.groups
        self.piece = self.full * batch + self.tall
        self.pair = 2 * self.piece
        offsets = [local * i % BLOCK for i in range(max(row_count, col_count))]
        self.frame = (max(offsets) + local + BLOCK - 1) // BLOCK
        self.wide = self.frame * BLOCK
        assert 2 * slots == BLOCK and BLOCK % self.rest == 0 and batch % (8 * self.groups) == 0
        assert self.frame == self.full + 1 and self.pair % 16 == 0

    def first(self, i):
        return lax.div(i * self.local, jnp.int32(BLOCK))

    def offset(self, i):
        return lax.rem(i * self.local, jnp.int32(BLOCK))

    def pack(self, whole):
        parts = [whole[:, i * BLOCK : (i + 1) * BLOCK] for i in range(self.full)]
        tail = whole[:, self.full * BLOCK :]
        lanes = lax.broadcasted_iota(jnp.int32, (self.tall, BLOCK), 1)
        joined = tail[0 : self.tall]
        for g in range(1, self.groups):
            moved = pltpu.roll(tail[g * self.tall : (g + 1) * self.tall], g * self.rest, 1)
            joined = jnp.where(lanes < g * self.rest, joined, moved)
        return jnp.concatenate(parts + [joined], axis=0)

    def unpack(self, piece):
        parts = [piece[i * self.batch : (i + 1) * self.batch] for i in range(self.full)]
        joined = piece[self.full * self.batch :]
        lanes = lax.broadcasted_iota(jnp.int32, (self.tall, BLOCK), 1)
        tails = []
        for g in range(self.groups):
            moved = joined if g == 0 else pltpu.roll(joined, BLOCK - g * self.rest, 1)
            tails.append(jnp.where(lanes < self.rest, moved, 0.0))
        return jnp.concatenate(parts + [jnp.concatenate(tails, axis=0)], axis=1)

    def add_blocks(self, target, base, i, piece):
        turned = pltpu.roll(self.unpack(piece), self.offset(i), 1)
        first = base + self.first(i)
        for f in range(self.frame):
            target[first + f] += turned[:, f * BLOCK : (f + 1) * BLOCK]

    def take_blocks(self, source, base, i):
        first = base + self.first(i)
        whole = jnp.concatenate([source[first + f] for f in range(self.frame)], axis=1)
        back = lax.rem(self.wide - self.offset(i), jnp.int32(self.wide))
        return self.pack(pltpu.roll(whole, back, 1))


def call(body, outs, scratch, ins, places=None, flops=0, out_specs=None, aliases=None):
    specs = [(places or {}).get(i, VMEM) for i in range(len(ins))]
    moved = sum(x.size * x.dtype.itemsize for x in ins) + sum(x.size * x.dtype.itemsize for x in outs)
    return pl.pallas_call(
        body,
        out_shape=outs,
        in_specs=specs,
        out_specs=out_specs or [VMEM] * len(outs),
        scratch_shapes=scratch,
        cost_estimate=pl.CostEstimate(flops=flops, bytes_accessed=moved, transcendentals=0),
        compiler_params=pltpu.CompilerParams(vmem_limit_bytes=24 * 1024 * 1024),
        input_output_aliases=aliases or {},
    )(*ins)


def shape(dims, kind=F32):
    return jax.ShapeDtypeStruct(tuple(dims), kind)


def flip(x, axis, k):
    count = lax.axis_size(axis)
    return lax.ppermute(x, axis, [(i, i ^ k) for i in range(count)])


def few(count):
    return count <= 4


def share(x, axis):
    count = lax.axis_size(axis)
    if few(count):
        return [flip(x, axis, k) for k in range(1, count)]
    return [lax.all_gather(x, axis)]


def exchange(parts, axis):
    count = lax.axis_size(axis)
    if len(parts) == count - 1:
        return [flip(part, axis, count - 1 - i) for i, part in enumerate(parts)]
    return [lax.all_to_all(parts[0], axis, 0, 0, tiled=True)]


def parcel(count, dims, kind):
    if few(count):
        return [shape(dims, kind)] * (count - 1)
    return [shape((count, *dims), kind)]


def away(refs, count, me, k):
    return refs[k - 1] if len(refs) == count - 1 else refs[0].at[me ^ k]


def parted(refs, count, me, k):
    return refs[count - 1 - k] if len(refs) == count - 1 else refs[0].at[me ^ k]


def place():
    return lax.axis_index("row"), lax.axis_index("col")


def loop(count, body):
    lax.fori_loop(0, count, lambda i, c: (body(i), c)[1], 0, unroll=count <= 18)


def start_kernel(z, rates, numbers, message, own, ids, pad):
    pad[...] = jnp.zeros_like(pad)
    pad[:, 0 : z.local] = rates[...]
    packed = z.pack(pad[...])
    own[...] = packed
    number = numbers[...]
    at = 2 * z.frame
    lists = [number[at + r : at + r + 1] for r in range(3)]
    pre_lanes = pltpu.roll(lists[2], z.slots, 1)
    lanes = lax.broadcasted_iota(jnp.int32, (1, BLOCK), 1)
    ids[...] = jnp.where(lanes < z.slots, lists[0] * z.post + lists[1], pre_lanes)
    high = (lax.shift_right_arithmetic(number, 7) + 1).astype(F32)
    low = (number & 127).astype(F32)
    blocks = []
    for f in range(z.frame):
        for r in (f, z.frame + f):
            blocks += [high[r : r + 1], low[r : r + 1]]
    fill = message.shape[0] - z.piece - 4 * z.frame
    extra = jnp.concatenate(blocks + [jnp.zeros((fill, BLOCK), F32)], axis=0)
    message[...] = jnp.concatenate([packed, extra], axis=0).astype(BF16)


def turn_weights_kernel(z, after, weights, out):
    del after

    def one(s):
        out[s] = jnp.transpose(weights[s])

    lax.fori_loop(0, z.slots, lambda i, c: (one(i), c)[1], 0, unroll=8)


def prepare_kernel(z, count, *refs):
    mine, own, cots, table, stimuli = refs[:5]
    got = refs[5 : 5 + count]
    rates, gain, drive, cot_out, pad = refs[5 + count :]
    p, _ = place()
    highs = z.types // BLOCK
    t = jnp.transpose(table[...])
    t1 = t.astype(BF16)
    t2 = (t - t1.astype(F32)).astype(BF16)
    t3 = (t - t1.astype(F32) - t2.astype(F32)).astype(BF16)
    high_ids = lax.broadcasted_iota(jnp.int32, (highs, BLOCK), 0).astype(F32) + 1.0
    low_ids = lax.broadcasted_iota(jnp.int32, (BLOCK, BLOCK), 0).astype(F32)
    channel_ids = lax.broadcasted_iota(jnp.int32, (z.channels, BLOCK), 0).astype(F32)
    stim = stimuli[...]
    for k in range(z.rows):
        ref = mine if k == 0 else away(got, z.rows, p, k)
        rows = slice(k * z.piece, (k + 1) * z.piece)
        message = ref[...].astype(F32)
        gains, drives = [], []
        for f in range(z.frame):
            at = z.piece + 4 * f
            codes = message[at : at + 4]
            pick = (high_ids == codes[0:1]).astype(BF16)
            found = sum(jnp.dot(x, pick, preferred_element_type=F32) for x in (t1, t2, t3))
            line = jnp.sum(jnp.where(low_ids == codes[1:2], found, 0.0), axis=0, keepdims=True)
            gains.append(jnp.broadcast_to(line, (z.batch, BLOCK)))
            channel = (codes[2:3] - 1.0) * BLOCK + codes[3:4]
            chosen = (channel_ids == channel).astype(BF16)
            drives.append(jnp.dot(stim, chosen, preferred_element_type=F32))
        gain[rows] = z.pack(jnp.concatenate(gains, axis=1))
        for step in range(z.steps):
            part = [d[step * z.batch : (step + 1) * z.batch] for d in drives]
            drive[step, rows] = z.pack(jnp.concatenate(part, axis=1))
        rates[rows] = own[...] if k == 0 else message[0 : z.piece]
    pad[...] = jnp.zeros_like(pad)
    for step in range(z.steps):
        pad[:, 0 : z.local] = cots[step]
        cot_out[step] = z.pack(pad[...])


def multiply_forward(z, c, ids, weights, x, total, own, parts):
    total[...] = jnp.zeros_like(total)
    for s in range(z.slots):
        total[ids[0, s]] += jnp.dot(x[ids[0, z.slots + s]], weights[s], preferred_element_type=F32)
    for k in range(z.cols):
        both = jnp.concatenate(
            [z.take_blocks(total, 0, c ^ k), z.take_blocks(total, z.post, c ^ k)], axis=0
        )
        if k == 0:
            own[...] = both
        else:
            parted(parts, z.cols, c, k)[...] = both.astype(BF16)


def first_kernel(z, count, *refs):
    near_ids, weights, mine = refs[:3]
    got = refs[3 : 3 + count]
    x, own = refs[3 + count : 5 + count]
    parts, (sums, total, ids, sem) = refs[5 + count : -4], refs[-4:]
    bring = pltpu.make_async_copy(near_ids, ids, sem)
    bring.start()
    p, c = place()
    sums[...] = jnp.zeros_like(sums)
    for k in range(z.rows):
        ref = mine if k == 0 else away(got, z.rows, p, k)
        z.add_blocks(sums, 0, p ^ k, ref[...].astype(F32)[0 : z.piece])
    x[...] = sums[...].astype(BF16)
    bring.wait()
    multiply_forward(z, c, ids, weights, x, total, own, parts)


def forward_kernel(z, step, count, *refs):
    near_ids, weights, kept, rates, gain, drive = refs[:6]
    got = refs[6 : 6 + count]
    new, act_pair, cur_pair, x, own = refs[6 + count : 11 + count]
    parts, (sums, total, ids, sem) = refs[11 + count : -4], refs[-4:]
    bring = pltpu.make_async_copy(near_ids, ids, sem)
    bring.start()
    p, c = place()
    sums[...] = jnp.zeros_like(sums)

    def sent(k, side):
        ref = kept if k == 0 else away(got, z.rows, p, k)
        return ref[side * z.piece : (side + 1) * z.piece].astype(F32)

    for k in range(z.rows):
        rows = slice(k * z.piece, (k + 1) * z.piece)
        current = sent(k, 0) + sent(k ^ z.half, 1) + drive[step, rows]
        activity = jnp.tanh(gain[rows] * current)
        fresh = 0.5 * rates[rows] + 0.5 * activity
        new[rows] = fresh
        if k % z.half == 0:
            at = k // z.half * z.piece
            act_pair[at : at + z.piece] = activity
            cur_pair[at : at + z.piece] = current
        z.add_blocks(sums, 0, p ^ k, fresh)
    x[...] = sums[...].astype(BF16)
    bring.wait()
    multiply_forward(z, c, ids, weights, x, total, own, parts)


def sum_kernel(z, count, with_cot, *refs):
    own, got = refs[0], refs[1 : 1 + count]
    kept, message = refs[-2:]
    _, c = place()
    total = own[...]
    for k in range(1, z.cols):
        total = total + parted(got, z.cols, c, k)[...].astype(F32)
    kept[...] = total
    if with_cot:
        cot = refs[1 + count]
        fill = message.shape[0] - z.pair - z.piece
        parts = [total, cot[z.steps - 1], jnp.zeros((fill, BLOCK), F32)]
        total = jnp.concatenate(parts, axis=0)
    message[...] = total.astype(BF16)


def pair_of(z, ref):
    at = z.half * z.piece
    return jnp.concatenate([ref[0 : z.piece], ref[at : at + z.piece]], axis=0)


def turn_kernel(z, kept, theirs, rates, gain, drive, cots, final, message, gain_pair, tally, base):
    other = theirs[...].astype(F32)
    swapped = jnp.concatenate([other[z.piece : z.pair], other[0 : z.piece]], axis=0)
    gains = pair_of(z, gain)
    current = kept[...] + swapped + pair_of(z, drive.at[z.steps - 1])
    activity = jnp.tanh(gains * current)
    fresh = 0.5 * rates[0 : z.piece] + 0.5 * activity[0 : z.piece]
    final[...] = fresh
    mine = cots[z.steps - 1]
    adjoint = jnp.concatenate([mine, other[z.pair : z.pair + z.piece]], axis=0)
    pressure = adjoint * 0.5 * (1.0 - activity * activity)
    message[...] = (gains * pressure).astype(BF16)
    gain_pair[...] = gains
    tally[...] = pressure * current
    base[...] = cots[z.steps - 2] + 0.5 * mine


def gather_post(z, c, mine, got, sums, d):
    sums[...] = jnp.zeros_like(sums)
    for k in range(z.cols):
        pair = (mine if k == 0 else away(got, z.cols, c, k))[...].astype(F32)
        z.add_blocks(sums, 0, c ^ k, pair[0 : z.piece])
        z.add_blocks(sums, z.post, c ^ k, pair[z.piece : z.pair])
    d[...] = sums[...].astype(BF16)


def back_kernel(z, count, *refs):
    near_ids, weights, base, mine = refs[:4]
    got = refs[4 : 4 + count]
    d, own = refs[4 + count : 6 + count]
    parts, (sums, total, ids, sem) = refs[6 + count : -4], refs[-4:]
    bring = pltpu.make_async_copy(near_ids, ids, sem)
    bring.start()
    p, c = place()
    gather_post(z, c, mine, got, sums, d)
    total[...] = jnp.zeros_like(total)
    bring.wait()
    for s in range(z.slots):
        total[ids[0, z.slots + s]] += jnp.dot(d[ids[0, s]], weights[s], preferred_element_type=F32)
    pieces = [z.take_blocks(total, 0, p ^ k) for k in range(z.rows)]
    for k in range(z.rows):
        other = pieces[k ^ z.half]
        if k == 0:
            own[...] = jnp.concatenate([pieces[0] + base[...], other], axis=0)
        else:
            if k == z.half:
                other = other + base[...]
            both = jnp.concatenate([pieces[k], other], axis=0)
            parted(parts, z.rows, p, k)[...] = both.astype(BF16)


def adjoints(z, own, got):
    p, _ = place()
    total = own[...]
    for k in range(1, z.rows):
        total = total + parted(got, z.rows, p, k)[...].astype(F32)
    return total


def delta_kernel(z, before, count, own, gain, act, cur, tally_in, cots, *refs):
    got, (message, tally, base) = refs[:count], refs[count:]
    adjoint = adjoints(z, own, got)
    activity = act[...]
    pressure = adjoint * 0.5 * (1.0 - activity * activity)
    message[...] = (gain[...] * pressure).astype(BF16)
    tally[...] = tally_in[...] + pressure * cur[...]
    base[...] = cots[before - 1] + 0.5 * adjoint[0 : z.piece]


def last_delta_kernel(z, count, own, gain, act, cur, tally_in, mine, partner, *refs):
    got, message = refs[:count], refs[count]
    adjoint = adjoints(z, own, got)
    activity = act[...]
    pressure = adjoint * 0.5 * (1.0 - activity * activity)
    tally = tally_in[...] + pressure * cur[...]
    rows = [gain[...] * pressure]
    lanes = lax.broadcasted_iota(jnp.int32, (1, BLOCK), 1)
    for side, ref in enumerate((mine, partner)):
        codes = ref[...].astype(F32)[z.piece :]
        begin = side * z.piece
        for f in range(z.frame):
            at = begin + f * z.batch
            if f < z.full:
                g = jnp.sum(tally[at : at + z.batch], axis=0, keepdims=True)
            else:
                packed = jnp.sum(tally[at : at + z.tall], axis=0, keepdims=True)
                g = packed
                for i in range(1, z.groups):
                    g = g + pltpu.roll(packed, BLOCK - i * z.rest, 1)
                g = jnp.where(lanes < z.rest, g, 0.0)
            g1 = g.astype(BF16).astype(F32)
            g2 = (g - g1).astype(BF16).astype(F32)
            rows += [codes[4 * f : 4 * f + 2], g1, g2, g - g1 - g2]
        rows.append(jnp.zeros((CODES - 5 * z.frame, BLOCK), F32))
    message[...] = jnp.concatenate(rows, axis=0).astype(BF16)


def extras_kernel(z, count, right, mine, *refs):
    del right
    got, out = refs[:-1], refs[-1]
    _, c = place()
    for k in range(z.cols):
        ref = mine if k == 0 else away(got, z.cols, c, k)
        out[2 * CODES * k : 2 * CODES * (k + 1)] = ref[z.pair :]


def add_table(z, extras, out):
    highs = z.types // BLOCK
    high_ids = lax.broadcasted_iota(jnp.int32, (highs, BLOCK), 0).astype(F32) + 1.0
    low_ids = lax.broadcasted_iota(jnp.int32, (BLOCK, BLOCK), 0).astype(F32)
    total = jnp.zeros((3 * highs, BLOCK), F32)
    for ref in extras:
        for side in range(2 * z.cols):
            extra = ref[side * CODES : (side + 1) * CODES].astype(F32)
            for f in range(z.frame):
                at = 5 * f
                hit = high_ids == extra[at : at + 1]
                terms = [jnp.where(hit, extra[at + 2 + i : at + 3 + i], 0.0) for i in range(3)]
                left = jnp.concatenate(terms, axis=0).astype(BF16)
                right = (low_ids == extra[at + 1 : at + 2]).astype(BF16)
                total = total + lax.dot_general(
                    left, right, (((1,), (1,)), ((), ())), preferred_element_type=F32
                )
    out[...] = total[0:highs] + total[highs : 2 * highs] + total[2 * highs :]


def lay_kernel(z, *refs):
    xs, ds = refs[: z.steps], refs[z.steps : 2 * z.steps - 1]
    last_rates, right, left, final = refs[2 * z.steps - 1 :]
    final[...] = z.unpack(last_rates[...])[:, 0 : z.local]
    n = z.batch
    deep = right.shape[1]
    rest = deep - z.steps * n

    def lay_right(q):
        for t in range(z.steps):
            right[q, t * n : (t + 1) * n] = xs[t][q]
        if rest:
            right[q, z.steps * n :] = jnp.zeros((rest, BLOCK), BF16)

    loop(z.pre, lay_right)

    def lay_left(q):
        parts = [jnp.zeros((n, BLOCK), F32)] + [d[q].astype(F32) for d in ds]
        if rest:
            parts.append(jnp.zeros((rest, BLOCK), F32))
        left[q] = jnp.transpose(jnp.concatenate(parts, axis=0)).astype(BF16)

    loop(2 * z.post, lay_left)


def grad_kernel(z, count, per_step, *refs):
    near_ids, right, later, mine = refs[:4]
    got = refs[4 : 4 + count]
    left, out, sums, d0, ids, sem = refs[4 + count :]
    n = z.batch
    deep = right.shape[1]

    @pl.when(pl.program_id(0) == 0)
    def _():
        bring = pltpu.make_async_copy(near_ids, ids, sem)
        bring.start()
        _, c = place()
        gather_post(z, c, mine, got, sums, d0)
        lanes = lax.broadcasted_iota(jnp.int32, (BLOCK, deep), 1)

        def lay_left(q):
            whole = jnp.concatenate([sums[q], jnp.zeros((deep - n, BLOCK), F32)], axis=0)
            turned = jnp.transpose(whole)
            left[q] = jnp.where(lanes < n, turned, later[q].astype(F32)).astype(BF16)

        loop(2 * z.post, lay_left)
        bring.wait()

    products(z, pl.program_id(0) * per_step, per_step, ids, left, right, out)


def products(z, begin, count, ids, left, right, out):
    for s in range(count):
        product = jnp.dot(
            left[ids[0, begin + s]], right[ids[0, z.slots + begin + s]], preferred_element_type=F32
        )
        out[s] = product.astype(BF16)


def rest_kernel(z, count, begin, per_step, near_ids, left, right, grads, *refs):
    del grads
    extras = refs[:count]
    out, table, ids, sem = refs[count:]
    bring = pltpu.make_async_copy(near_ids, ids, sem)
    bring.start()
    add_table(z, extras, table)
    bring.wait()
    products(z, begin + pl.program_id(0) * per_step, per_step, ids, left, right, out)


def shards(
    initial_rates,
    stimuli,
    cotangent,
    weight_blocks,
    slot_owner,
    slot_post,
    slot_pre,
    cell_type,
    type_gain,
    input_map,
):
    batch, local = initial_rates.shape
    slots = weight_blocks.shape[2]
    steps, _, channels = stimuli.shape
    types = type_gain.shape[0]
    z = Sizes(
        lax.axis_size("row"), lax.axis_size("col"), batch, local, slots, types, channels, steps
    )
    pair = (z.pair, BLOCK)
    product_flops = 2 * slots * batch * BLOCK * BLOCK
    opening = (z.piece + 4 * z.frame + 15) // 16 * 16
    closing = (z.pair + z.piece + 15) // 16 * 16

    fill = jnp.full((z.wide - local,), -BLOCK, jnp.int32)
    blank = jnp.zeros((BLOCK - slots,), jnp.int32)
    lists = [cell_type, fill, input_map, fill]
    for x in (slot_owner, slot_post, slot_pre):
        lists += [x.reshape(slots), blank]
    numbers = jnp.concatenate(lists)
    message, own_rates, ids = call(
        functools.partial(start_kernel, z),
        [
            shape((opening, BLOCK), BF16),
            shape((z.piece, BLOCK)),
            shape((1, 2 * slots), jnp.int32),
        ],
        [pltpu.VMEM((batch, z.wide), F32)],
        [initial_rates, numbers.reshape(numbers.size // BLOCK, BLOCK)],
    )
    got = share(message, "row")
    weights = weight_blocks.reshape(slots, BLOCK, BLOCK)
    (turned,) = call(
        functools.partial(turn_weights_kernel, z),
        [shape((slots, BLOCK, BLOCK), BF16)],
        [],
        [message, weights],
    )
    held_ids = [pltpu.SMEM((1, 2 * slots), jnp.int32), pltpu.SemaphoreType.DMA]
    if few(z.rows):
        partner_message = got[z.half - 1]
    else:
        partner_message = flip(message, "row", z.half)
    pre_sums = pltpu.VMEM((z.pre, batch, BLOCK), F32)
    post_sums = pltpu.VMEM((2 * z.post, batch, BLOCK), F32)
    x_shape = shape((z.pre, batch, BLOCK), BF16)
    row_parts = parcel(z.rows, pair, BF16)
    col_parts = [shape(pair), *parcel(z.cols, pair, BF16)]
    x, own, *parts = call(
        functools.partial(first_kernel, z, len(got)),
        [x_shape, *col_parts],
        [pre_sums, post_sums, *held_ids],
        [ids, turned, message, *got],
        flops=product_flops,
    )
    every = (z.rows * z.piece, BLOCK)
    rates, gain, drive, cots = call(
        functools.partial(prepare_kernel, z, len(got)),
        [shape(every), shape(every), shape((steps, *every)), shape((steps, z.piece, BLOCK))],
        [pltpu.VMEM((batch, z.wide), F32)],
        [
            message,
            own_rates,
            cotangent,
            type_gain.reshape(types // BLOCK, BLOCK),
            stimuli.reshape(steps * batch, channels),
            *got,
        ],
    )
    xs, acts, curs = [x], [], []
    for t in range(steps):
        last = t == steps - 1
        got = exchange(parts, "col")
        kept, sent = call(
            functools.partial(sum_kernel, z, len(got), last),
            [shape(pair), shape((closing, BLOCK) if last else pair, BF16)],
            [],
            [own, *got] + ([cots] if last else []),
        )
        if last:
            break
        got = share(sent, "row")
        rates, act, cur, x, own, *parts = call(
            functools.partial(forward_kernel, z, t, len(got)),
            [shape(every), shape(pair), shape(pair), x_shape, *col_parts],
            [pre_sums, post_sums, *held_ids],
            [ids, turned, kept, rates, gain, drive, *got],
            flops=product_flops,
        )
        xs.append(x)
        acts.append(act)
        curs.append(cur)
    theirs = flip(sent, "row", z.half)
    last_rates, delta, gain, tally, base = call(
        functools.partial(turn_kernel, z),
        [
            shape((z.piece, BLOCK)),
            shape(pair, BF16),
            shape(pair),
            shape(pair),
            shape((z.piece, BLOCK)),
        ],
        [],
        [kept, theirs, rates, gain, drive, cots],
    )
    ds = []
    for t in reversed(range(1, steps)):
        got = share(delta, "col")
        d, own, *parts = call(
            functools.partial(back_kernel, z, len(got)),
            [shape((2 * z.post, batch, BLOCK), BF16), shape(pair), *row_parts],
            [post_sums, pre_sums, *held_ids],
            [ids, weights, base, delta, *got],
            flops=product_flops,
        )
        ds.insert(0, d)
        got = exchange(parts, "row")
        before = t - 1
        if before > 0:
            delta, tally, base = call(
                functools.partial(delta_kernel, z, before, len(got)),
                [shape(pair, BF16), shape(pair), shape((z.piece, BLOCK))],
                [],
                [own, gain, acts[before], curs[before], tally, cots, *got],
            )
        else:
            (delta,) = call(
                functools.partial(last_delta_kernel, z, len(got)),
                [shape((z.pair + 2 * CODES, BLOCK), BF16)],
                [],
                [own, gain, acts[0], curs[0], tally, message, partner_message, *got],
            )
    got = share(delta, "col")
    grid = 4
    per_step = slots // grid
    deep = (steps * batch + BLOCK - 1) // BLOCK * BLOCK
    left_shape = shape((2 * z.post, BLOCK, deep), BF16)
    right, later, final_rates = call(
        functools.partial(lay_kernel, z),
        [shape((z.pre, deep, BLOCK), BF16), left_shape, shape((batch, local))],
        [],
        [*xs, *ds, last_rates],
    )
    (extras,) = call(
        functools.partial(extras_kernel, z, len(got)),
        [shape((2 * CODES * z.cols, BLOCK), BF16)],
        [],
        [right, delta, *got],
    )
    all_extras = [extras, flip(extras, "row", 1)] if z.half == 2 else [extras]
    ins = [ids, right, later, delta, *got]
    cost = pl.CostEstimate(
        flops=2 * slots * deep * BLOCK * BLOCK, bytes_accessed=4 * 1024 * 1024, transcendentals=0
    )
    grads = shape((slots, BLOCK, BLOCK), BF16)
    limit = pltpu.CompilerParams(vmem_limit_bytes=24 * 1024 * 1024)
    left, weight_grads = pl.pallas_call(
        functools.partial(grad_kernel, z, len(got), per_step),
        grid=(grid - 1,),
        out_shape=[left_shape, grads],
        in_specs=[VMEM] * len(ins),
        out_specs=[VMEM, pl.BlockSpec((per_step, BLOCK, BLOCK), lambda i: (i, 0, 0))],
        scratch_shapes=[post_sums, pltpu.VMEM((2 * z.post, batch, BLOCK), BF16), *held_ids],
        cost_estimate=cost,
        compiler_params=limit,
    )(*ins)
    ins = [ids, left, right, weight_grads, *all_extras]
    weight_grads, table = pl.pallas_call(
        functools.partial(rest_kernel, z, len(all_extras), slots - per_step, per_step),
        grid=(1,),
        out_shape=[grads, shape((types // BLOCK, BLOCK))],
        in_specs=[VMEM] * 3 + [pl.BlockSpec(memory_space=pl.ANY)] + [VMEM] * len(all_extras),
        out_specs=[pl.BlockSpec((per_step, BLOCK, BLOCK), lambda i: (i + grid - 1, 0, 0)), VMEM],
        scratch_shapes=held_ids,
        input_output_aliases={3: 0},
        cost_estimate=cost,
        compiler_params=limit,
    )(*ins)
    if z.half != 2:
        table = 0.5 * lax.psum(table, "row")
    gain_grads = table.reshape(types)
    return (final_rates, weight_grads.reshape(1, 1, slots, BLOCK, BLOCK), gain_grads)


def solution(mesh):
    in_specs = (
        P("groups", ("row", "col")),
        P(None, "groups", None),
        P(None, "groups", ("row", "col")),
        P("row", "col", None, None, None),
        P("row", "col", None),
        P("row", "col", None),
        P("row", "col", None),
        P(("row", "col")),
        P(),
        P(("row", "col")),
    )
    out_specs = (P("groups", ("row", "col")), P("row", "col", "groups", None, None), P("groups"))
    return jax.shard_map(shards, mesh=mesh, in_specs=in_specs, out_specs=out_specs, check_vma=False)
```

```python
import functools

import jax
import jax.numpy as jnp
from jax import lax
from jax.experimental import pallas as pl
from jax.experimental.pallas import tpu as pltpu
from jax.sharding import PartitionSpec as P

BLOCK = 128
CODES = 16
F32 = jnp.float32
BF16 = jnp.bfloat16
VMEM = pl.BlockSpec(memory_space=pltpu.VMEM)


class Sizes:
    def __init__(self, row_count, col_count, batch, local, slots, types, channels, steps):
        self.rows, self.cols = row_count, col_count
        self.batch, self.local, self.slots = batch, local, slots
        self.types, self.channels, self.steps = types, channels, steps
        self.post = col_count * local // BLOCK
        self.pre = row_count * local // BLOCK
        self.half = row_count // 2
        self.full, self.rest = local // BLOCK, local % BLOCK
        self.groups = BLOCK // self.rest
        self.tall = batch // self.groups
        self.piece = self.full * batch + self.tall
        self.pair = 2 * self.piece
        offsets = [local * i % BLOCK for i in range(max(row_count, col_count))]
        self.frame = (max(offsets) + local + BLOCK - 1) // BLOCK
        self.wide = self.frame * BLOCK
        assert 2 * slots == BLOCK and BLOCK % self.rest == 0 and batch % (8 * self.groups) == 0
        assert self.frame == self.full + 1 and self.pair % 16 == 0

    def first(self, i):
        return lax.div(i * self.local, jnp.int32(BLOCK))

    def offset(self, i):
        return lax.rem(i * self.local, jnp.int32(BLOCK))

    def pack(self, whole):
        parts = [whole[:, i * BLOCK : (i + 1) * BLOCK] for i in range(self.full)]
        tail = whole[:, self.full * BLOCK :]
        lanes = lax.broadcasted_iota(jnp.int32, (self.tall, BLOCK), 1)
        joined = tail[0 : self.tall]
        for g in range(1, self.groups):
            moved = pltpu.roll(tail[g * self.tall : (g + 1) * self.tall], g * self.rest, 1)
            joined = jnp.where(lanes < g * self.rest, joined, moved)
        return jnp.concatenate(parts + [joined], axis=0)

    def unpack(self, piece):
        parts = [piece[i * self.batch : (i + 1) * self.batch] for i in range(self.full)]
        joined = piece[self.full * self.batch :]
        lanes = lax.broadcasted_iota(jnp.int32, (self.tall, BLOCK), 1)
        tails = []
        for g in range(self.groups):
            moved = joined if g == 0 else pltpu.roll(joined, BLOCK - g * self.rest, 1)
            tails.append(jnp.where(lanes < self.rest, moved, 0.0))
        return jnp.concatenate(parts + [jnp.concatenate(tails, axis=0)], axis=1)

    def add_blocks(self, target, base, i, piece):
        turned = pltpu.roll(self.unpack(piece), self.offset(i), 1)
        first = base + self.first(i)
        for f in range(self.frame):
            target[first + f] += turned[:, f * BLOCK : (f + 1) * BLOCK]

    def take_blocks(self, source, base, i):
        first = base + self.first(i)
        whole = jnp.concatenate([source[first + f] for f in range(self.frame)], axis=1)
        back = lax.rem(self.wide - self.offset(i), jnp.int32(self.wide))
        return self.pack(pltpu.roll(whole, back, 1))


def call(body, outs, scratch, ins, places=None, flops=0, out_specs=None, aliases=None):
    specs = [(places or {}).get(i, VMEM) for i in range(len(ins))]
    moved = sum(x.size * x.dtype.itemsize for x in ins) + sum(x.size * x.dtype.itemsize for x in outs)
    return pl.pallas_call(
        body,
        out_shape=outs,
        in_specs=specs,
        out_specs=out_specs or [VMEM] * len(outs),
        scratch_shapes=scratch,
        cost_estimate=pl.CostEstimate(flops=flops, bytes_accessed=moved, transcendentals=0),
        compiler_params=pltpu.CompilerParams(vmem_limit_bytes=24 * 1024 * 1024),
        input_output_aliases=aliases or {},
    )(*ins)


def shape(dims, kind=F32):
    return jax.ShapeDtypeStruct(tuple(dims), kind)


def flip(x, axis, k):
    count = lax.axis_size(axis)
    return lax.ppermute(x, axis, [(i, i ^ k) for i in range(count)])


def few(count):
    return count <= 4


def order(axis, count):
    return (3, 1, 2) if axis == "row" and count == 4 else tuple(range(count - 1, 0, -1))


def share(x, axis):
    count = lax.axis_size(axis)
    if few(count):
        return [flip(x, axis, k) for k in order(axis, count)[::-1]]
    return [lax.all_gather(x, axis)]


def exchange(parts, axis):
    count = lax.axis_size(axis)
    if len(parts) == count - 1:
        return [flip(part, axis, k) for part, k in zip(parts, order(axis, count))]
    return [lax.all_to_all(parts[0], axis, 0, 0, tiled=True)]


def parcel(count, dims, kind):
    if few(count):
        return [shape(dims, kind)] * (count - 1)
    return [shape((count, *dims), kind)]


def away(refs, axis, count, me, k):
    if few(count):
        return refs[order(axis, count)[::-1].index(k)]
    return refs[0].at[me ^ k]


def parted(refs, axis, count, me, k):
    if few(count):
        return refs[order(axis, count).index(k)]
    return refs[0].at[me ^ k]


def place():
    return lax.axis_index("row"), lax.axis_index("col")


def loop(count, body):
    lax.fori_loop(0, count, lambda i, c: (body(i), c)[1], 0, unroll=count <= 18)


def start_kernel(z, rates, numbers, message, own, ids, pad):
    pad[...] = jnp.zeros_like(pad)
    pad[:, 0 : z.local] = rates[...]
    packed = z.pack(pad[...])
    own[...] = packed
    number = numbers[...]
    at = 2 * z.frame
    lists = [number[at + r : at + r + 1] for r in range(3)]
    pre_lanes = pltpu.roll(lists[2], z.slots, 1)
    lanes = lax.broadcasted_iota(jnp.int32, (1, BLOCK), 1)
    ids[...] = jnp.where(lanes < z.slots, lists[0] * z.post + lists[1], pre_lanes)
    high = (lax.shift_right_arithmetic(number, 7) + 1).astype(F32)
    low = (number & 127).astype(F32)
    blocks = []
    for f in range(z.frame):
        for r in (f, z.frame + f):
            blocks += [high[r : r + 1], low[r : r + 1]]
    fill = message.shape[0] - z.piece - 4 * z.frame
    extra = jnp.concatenate(blocks + [jnp.zeros((fill, BLOCK), F32)], axis=0)
    message[...] = jnp.concatenate([packed, extra], axis=0).astype(BF16)


def turn_weights_kernel(z, after, weights, out):
    del after

    def one(s):
        out[s] = jnp.transpose(weights[s])

    lax.fori_loop(0, z.slots, lambda i, c: (one(i), c)[1], 0, unroll=8)


def prepare_kernel(z, count, *refs):
    mine, own, cots, table, stimuli = refs[:5]
    got = refs[5 : 5 + count]
    rates, gain, drive, cot_out, pad = refs[5 + count :]
    p, _ = place()
    highs = z.types // BLOCK
    t = jnp.transpose(table[...])
    t1 = t.astype(BF16)
    t2 = (t - t1.astype(F32)).astype(BF16)
    t3 = (t - t1.astype(F32) - t2.astype(F32)).astype(BF16)
    high_ids = lax.broadcasted_iota(jnp.int32, (highs, BLOCK), 0).astype(F32) + 1.0
    low_ids = lax.broadcasted_iota(jnp.int32, (BLOCK, BLOCK), 0).astype(F32)
    channel_ids = lax.broadcasted_iota(jnp.int32, (z.channels, BLOCK), 0).astype(F32)
    stim = stimuli[...]
    for k in range(z.rows):
        ref = mine if k == 0 else away(got, "row", z.rows, p, k)
        rows = slice(k * z.piece, (k + 1) * z.piece)
        message = ref[...].astype(F32)
        gains, drives = [], []
        for f in range(z.frame):
            at = z.piece + 4 * f
            codes = message[at : at + 4]
            pick = (high_ids == codes[0:1]).astype(BF16)
            found = sum(jnp.dot(x, pick, preferred_element_type=F32) for x in (t1, t2, t3))
            line = jnp.sum(jnp.where(low_ids == codes[1:2], found, 0.0), axis=0, keepdims=True)
            gains.append(jnp.broadcast_to(line, (z.batch, BLOCK)))
            channel = (codes[2:3] - 1.0) * BLOCK + codes[3:4]
            chosen = (channel_ids == channel).astype(BF16)
            drives.append(jnp.dot(stim, chosen, preferred_element_type=F32))
        gain[rows] = z.pack(jnp.concatenate(gains, axis=1))
        for step in range(z.steps):
            part = [d[step * z.batch : (step + 1) * z.batch] for d in drives]
            drive[step, rows] = z.pack(jnp.concatenate(part, axis=1))
        rates[rows] = own[...] if k == 0 else message[0 : z.piece]
    pad[...] = jnp.zeros_like(pad)
    for step in range(z.steps):
        pad[:, 0 : z.local] = cots[step]
        cot_out[step] = z.pack(pad[...])


def multiply_forward(z, c, ids, weights, x, total, own, parts):
    total[...] = jnp.zeros_like(total)
    for s in range(z.slots):
        total[ids[0, s]] += jnp.dot(x[ids[0, z.slots + s]], weights[s], preferred_element_type=F32)
    for k in range(z.cols):
        both = jnp.concatenate(
            [z.take_blocks(total, 0, c ^ k), z.take_blocks(total, z.post, c ^ k)], axis=0
        )
        if k == 0:
            own[...] = both
        else:
            parted(parts, "col", z.cols, c, k)[...] = both.astype(BF16)


def first_kernel(z, count, *refs):
    near_ids, weights, mine = refs[:3]
    got = refs[3 : 3 + count]
    x, own = refs[3 + count : 5 + count]
    parts, (sums, total, ids, sem) = refs[5 + count : -4], refs[-4:]
    bring = pltpu.make_async_copy(near_ids, ids, sem)
    bring.start()
    p, c = place()
    sums[...] = jnp.zeros_like(sums)
    for k in range(z.rows):
        ref = mine if k == 0 else away(got, "row", z.rows, p, k)
        z.add_blocks(sums, 0, p ^ k, ref[...].astype(F32)[0 : z.piece])
    x[...] = sums[...].astype(BF16)
    bring.wait()
    multiply_forward(z, c, ids, weights, x, total, own, parts)


def forward_kernel(z, step, count, *refs):
    near_ids, weights, kept, rates, gain, drive = refs[:6]
    got = refs[6 : 6 + count]
    new, act_pair, cur_pair, x, own = refs[6 + count : 11 + count]
    parts, (sums, total, ids, sem) = refs[11 + count : -4], refs[-4:]
    bring = pltpu.make_async_copy(near_ids, ids, sem)
    bring.start()
    p, c = place()
    sums[...] = jnp.zeros_like(sums)

    def sent(k, side):
        ref = kept if k == 0 else away(got, "row", z.rows, p, k)
        return ref[side * z.piece : (side + 1) * z.piece].astype(F32)

    for k in range(z.rows):
        rows = slice(k * z.piece, (k + 1) * z.piece)
        current = sent(k, 0) + sent(k ^ z.half, 1) + drive[step, rows]
        activity = jnp.tanh(gain[rows] * current)
        fresh = 0.5 * rates[rows] + 0.5 * activity
        new[rows] = fresh
        if k % z.half == 0:
            at = k // z.half * z.piece
            act_pair[at : at + z.piece] = activity
            cur_pair[at : at + z.piece] = current
        z.add_blocks(sums, 0, p ^ k, fresh)
    x[...] = sums[...].astype(BF16)
    bring.wait()
    multiply_forward(z, c, ids, weights, x, total, own, parts)


def sum_kernel(z, count, with_cot, *refs):
    own, got = refs[0], refs[1 : 1 + count]
    kept, message = refs[-2:]
    _, c = place()
    total = own[...]
    for k in range(1, z.cols):
        total = total + parted(got, "col", z.cols, c, k)[...].astype(F32)
    kept[...] = total
    if with_cot:
        cot = refs[1 + count]
        fill = message.shape[0] - z.pair - z.piece
        parts = [total, cot[z.steps - 1], jnp.zeros((fill, BLOCK), F32)]
        total = jnp.concatenate(parts, axis=0)
    message[...] = total.astype(BF16)


def pair_of(z, ref):
    at = z.half * z.piece
    return jnp.concatenate([ref[0 : z.piece], ref[at : at + z.piece]], axis=0)


def turn_kernel(z, kept, theirs, rates, gain, drive, cots, final, message, gain_pair, tally, base):
    other = theirs[...].astype(F32)
    swapped = jnp.concatenate([other[z.piece : z.pair], other[0 : z.piece]], axis=0)
    gains = pair_of(z, gain)
    current = kept[...] + swapped + pair_of(z, drive.at[z.steps - 1])
    activity = jnp.tanh(gains * current)
    fresh = 0.5 * rates[0 : z.piece] + 0.5 * activity[0 : z.piece]
    final[...] = fresh
    mine = cots[z.steps - 1]
    adjoint = jnp.concatenate([mine, other[z.pair : z.pair + z.piece]], axis=0)
    pressure = adjoint * 0.5 * (1.0 - activity * activity)
    message[...] = (gains * pressure).astype(BF16)
    gain_pair[...] = gains
    tally[...] = pressure * current
    base[...] = cots[z.steps - 2] + 0.5 * mine


def gather_post(z, c, mine, got, sums, d):
    sums[...] = jnp.zeros_like(sums)
    for k in range(z.cols):
        pair = (mine if k == 0 else away(got, "col", z.cols, c, k))[...].astype(F32)
        z.add_blocks(sums, 0, c ^ k, pair[0 : z.piece])
        z.add_blocks(sums, z.post, c ^ k, pair[z.piece : z.pair])
    d[...] = sums[...].astype(BF16)


def back_kernel(z, count, *refs):
    near_ids, weights, base, mine = refs[:4]
    got = refs[4 : 4 + count]
    d, own = refs[4 + count : 6 + count]
    parts, (sums, total, ids, sem) = refs[6 + count : -4], refs[-4:]
    bring = pltpu.make_async_copy(near_ids, ids, sem)
    bring.start()
    p, c = place()
    gather_post(z, c, mine, got, sums, d)
    total[...] = jnp.zeros_like(total)
    bring.wait()
    for s in range(z.slots):
        total[ids[0, z.slots + s]] += jnp.dot(d[ids[0, s]], weights[s], preferred_element_type=F32)
    pieces = [z.take_blocks(total, 0, p ^ k) for k in range(z.rows)]
    for k in range(z.rows):
        other = pieces[k ^ z.half]
        if k == 0:
            own[...] = jnp.concatenate([pieces[0] + base[...], other], axis=0)
        else:
            if k == z.half:
                other = other + base[...]
            both = jnp.concatenate([pieces[k], other], axis=0)
            parted(parts, "row", z.rows, p, k)[...] = both.astype(BF16)


def adjoints(z, own, got):
    p, _ = place()
    total = own[...]
    for k in range(1, z.rows):
        total = total + parted(got, "row", z.rows, p, k)[...].astype(F32)
    return total


def delta_kernel(z, before, count, own, gain, act, cur, tally_in, cots, *refs):
    got, (message, tally, base) = refs[:count], refs[count:]
    adjoint = adjoints(z, own, got)
    activity = act[...]
    pressure = adjoint * 0.5 * (1.0 - activity * activity)
    message[...] = (gain[...] * pressure).astype(BF16)
    tally[...] = tally_in[...] + pressure * cur[...]
    base[...] = cots[before - 1] + 0.5 * adjoint[0 : z.piece]


def last_delta_kernel(z, count, own, gain, act, cur, tally_in, mine, partner, *refs):
    got, message = refs[:count], refs[count]
    adjoint = adjoints(z, own, got)
    activity = act[...]
    pressure = adjoint * 0.5 * (1.0 - activity * activity)
    tally = tally_in[...] + pressure * cur[...]
    rows = [gain[...] * pressure]
    lanes = lax.broadcasted_iota(jnp.int32, (1, BLOCK), 1)
    for side, ref in enumerate((mine, partner)):
        codes = ref[...].astype(F32)[z.piece :]
        begin = side * z.piece
        for f in range(z.frame):
            at = begin + f * z.batch
            if f < z.full:
                g = jnp.sum(tally[at : at + z.batch], axis=0, keepdims=True)
            else:
                packed = jnp.sum(tally[at : at + z.tall], axis=0, keepdims=True)
                g = packed
                for i in range(1, z.groups):
                    g = g + pltpu.roll(packed, BLOCK - i * z.rest, 1)
                g = jnp.where(lanes < z.rest, g, 0.0)
            g1 = g.astype(BF16).astype(F32)
            g2 = (g - g1).astype(BF16).astype(F32)
            rows += [codes[4 * f : 4 * f + 2], g1, g2, g - g1 - g2]
        rows.append(jnp.zeros((CODES - 5 * z.frame, BLOCK), F32))
    message[...] = jnp.concatenate(rows, axis=0).astype(BF16)


def extras_kernel(z, count, right, mine, *refs):
    del right
    got, out = refs[:-1], refs[-1]
    _, c = place()
    for k in range(z.cols):
        ref = mine if k == 0 else away(got, "col", z.cols, c, k)
        out[2 * CODES * k : 2 * CODES * (k + 1)] = ref[z.pair :]


def add_table(z, extras, out):
    highs = z.types // BLOCK
    high_ids = lax.broadcasted_iota(jnp.int32, (highs, BLOCK), 0).astype(F32) + 1.0
    low_ids = lax.broadcasted_iota(jnp.int32, (BLOCK, BLOCK), 1).astype(F32)
    total = jnp.zeros((3 * highs, BLOCK), F32)
    for ref in extras:
        everything = ref[...].astype(F32)
        down = jnp.transpose(everything)
        for side in range(2 * z.cols):
            extra = everything[side * CODES : (side + 1) * CODES]
            for f in range(z.frame):
                at = 5 * f
                low = side * CODES + at + 1
                hit = high_ids == extra[at : at + 1]
                terms = [jnp.where(hit, extra[at + 2 + i : at + 3 + i], 0.0) for i in range(3)]
                left = jnp.concatenate(terms, axis=0).astype(BF16)
                right = (low_ids == down[:, low : low + 1]).astype(BF16)
                total = total + jnp.dot(left, right, preferred_element_type=F32)
    out[...] = total[0:highs] + total[highs : 2 * highs] + total[2 * highs :]


def lay_kernel(z, *refs):
    xs, ds = refs[: z.steps], refs[z.steps : 2 * z.steps - 1]
    last_rates, right, left, final = refs[2 * z.steps - 1 :]
    final[...] = z.unpack(last_rates[...])[:, 0 : z.local]
    n = z.batch
    deep = right.shape[1]
    rest = deep - z.steps * n

    def lay_right(q):
        for t in range(z.steps):
            right[q, t * n : (t + 1) * n] = xs[t][q]
        if rest:
            right[q, z.steps * n :] = jnp.zeros((rest, BLOCK), BF16)

    loop(z.pre, lay_right)

    def lay_left(q):
        parts = [jnp.zeros((n, BLOCK), F32)] + [d[q].astype(F32) for d in ds]
        if rest:
            parts.append(jnp.zeros((rest, BLOCK), F32))
        left[q] = jnp.transpose(jnp.concatenate(parts, axis=0)).astype(BF16)

    loop(2 * z.post, lay_left)


def grad_kernel(z, count, per_step, *refs):
    near_ids, right, later, mine = refs[:4]
    got = refs[4 : 4 + count]
    left, out, sums, d0, ids, sem = refs[4 + count :]
    n = z.batch
    deep = right.shape[1]

    @pl.when(pl.program_id(0) == 0)
    def _():
        bring = pltpu.make_async_copy(near_ids, ids, sem)
        bring.start()
        _, c = place()
        gather_post(z, c, mine, got, sums, d0)
        lanes = lax.broadcasted_iota(jnp.int32, (BLOCK, deep), 1)

        def lay_left(q):
            whole = jnp.concatenate([sums[q], jnp.zeros((deep - n, BLOCK), F32)], axis=0)
            turned = jnp.transpose(whole)
            left[q] = jnp.where(lanes < n, turned, later[q].astype(F32)).astype(BF16)

        loop(2 * z.post, lay_left)
        bring.wait()

    products(z, pl.program_id(0) * per_step, per_step, ids, left, right, out)


def products(z, begin, count, ids, left, right, out):
    for s in range(count):
        product = jnp.dot(
            left[ids[0, begin + s]], right[ids[0, z.slots + begin + s]], preferred_element_type=F32
        )
        out[s] = product.astype(BF16)


def rest_kernel(z, count, begin, per_step, near_ids, left, right, grads, *refs):
    del grads
    extras = refs[:count]
    out, table, ids, sem = refs[count:]
    bring = pltpu.make_async_copy(near_ids, ids, sem)
    bring.start()
    add_table(z, extras, table)
    bring.wait()
    products(z, begin + pl.program_id(0) * per_step, per_step, ids, left, right, out)


def shards(
    initial_rates,
    stimuli,
    cotangent,
    weight_blocks,
    slot_owner,
    slot_post,
    slot_pre,
    cell_type,
    type_gain,
    input_map,
):
    batch, local = initial_rates.shape
    slots = weight_blocks.shape[2]
    steps, _, channels = stimuli.shape
    types = type_gain.shape[0]
    z = Sizes(
        lax.axis_size("row"), lax.axis_size("col"), batch, local, slots, types, channels, steps
    )
    pair = (z.pair, BLOCK)
    product_flops = 2 * slots * batch * BLOCK * BLOCK
    opening = (z.piece + 4 * z.frame + 15) // 16 * 16
    closing = (z.pair + z.piece + 15) // 16 * 16

    fill = jnp.full((z.wide - local,), -BLOCK, jnp.int32)
    blank = jnp.zeros((BLOCK - slots,), jnp.int32)
    lists = [cell_type, fill, input_map, fill]
    for x in (slot_owner, slot_post, slot_pre):
        lists += [x.reshape(slots), blank]
    numbers = jnp.concatenate(lists)
    message, own_rates, ids = call(
        functools.partial(start_kernel, z),
        [
            shape((opening, BLOCK), BF16),
            shape((z.piece, BLOCK)),
            shape((1, 2 * slots), jnp.int32),
        ],
        [pltpu.VMEM((batch, z.wide), F32)],
        [initial_rates, numbers.reshape(numbers.size // BLOCK, BLOCK)],
        flops=4_000_000_000,
    )
    got = share(message, "row")
    weights = weight_blocks.reshape(slots, BLOCK, BLOCK)
    (turned,) = call(
        functools.partial(turn_weights_kernel, z),
        [shape((slots, BLOCK, BLOCK), BF16)],
        [],
        [message, weights],
    )
    held_ids = [pltpu.SMEM((1, 2 * slots), jnp.int32), pltpu.SemaphoreType.DMA]
    if few(z.rows):
        partner_message = away(got, "row", z.rows, None, z.half)
    else:
        partner_message = flip(message, "row", z.half)
    pre_sums = pltpu.VMEM((z.pre, batch, BLOCK), F32)
    post_sums = pltpu.VMEM((2 * z.post, batch, BLOCK), F32)
    x_shape = shape((z.pre, batch, BLOCK), BF16)
    row_parts = parcel(z.rows, pair, BF16)
    col_parts = [shape(pair), *parcel(z.cols, pair, BF16)]
    x, own, *parts = call(
        functools.partial(first_kernel, z, len(got)),
        [x_shape, *col_parts],
        [pre_sums, post_sums, *held_ids],
        [ids, turned, message, *got],
        flops=product_flops,
    )
    every = (z.rows * z.piece, BLOCK)
    rates, gain, drive, cots = call(
        functools.partial(prepare_kernel, z, len(got)),
        [shape(every), shape(every), shape((steps, *every)), shape((steps, z.piece, BLOCK))],
        [pltpu.VMEM((batch, z.wide), F32)],
        [
            message,
            own_rates,
            cotangent,
            type_gain.reshape(types // BLOCK, BLOCK),
            stimuli.reshape(steps * batch, channels),
            *got,
        ],
    )
    xs, acts, curs = [x], [], []
    for t in range(steps):
        last = t == steps - 1
        got = exchange(parts, "col")
        kept, sent = call(
            functools.partial(sum_kernel, z, len(got), last),
            [shape(pair), shape((closing, BLOCK) if last else pair, BF16)],
            [],
            [own, *got] + ([cots] if last else []),
        )
        if last:
            break
        got = share(sent, "row")
        rates, act, cur, x, own, *parts = call(
            functools.partial(forward_kernel, z, t, len(got)),
            [shape(every), shape(pair), shape(pair), x_shape, *col_parts],
            [pre_sums, post_sums, *held_ids],
            [ids, turned, kept, rates, gain, drive, *got],
            flops=product_flops,
        )
        xs.append(x)
        acts.append(act)
        curs.append(cur)
    theirs = flip(sent, "row", z.half)
    last_rates, delta, gain, tally, base = call(
        functools.partial(turn_kernel, z),
        [
            shape((z.piece, BLOCK)),
            shape(pair, BF16),
            shape(pair),
            shape(pair),
            shape((z.piece, BLOCK)),
        ],
        [],
        [kept, theirs, rates, gain, drive, cots],
    )
    ds = []
    for t in reversed(range(1, steps)):
        got = share(delta, "col")
        d, own, *parts = call(
            functools.partial(back_kernel, z, len(got)),
            [shape((2 * z.post, batch, BLOCK), BF16), shape(pair), *row_parts],
            [post_sums, pre_sums, *held_ids],
            [ids, weights, base, delta, *got],
            flops=product_flops,
        )
        ds.insert(0, d)
        got = exchange(parts, "row")
        before = t - 1
        if before > 0:
            delta, tally, base = call(
                functools.partial(delta_kernel, z, before, len(got)),
                [shape(pair, BF16), shape(pair), shape((z.piece, BLOCK))],
                [],
                [own, gain, acts[before], curs[before], tally, cots, *got],
            )
        else:
            (delta,) = call(
                functools.partial(last_delta_kernel, z, len(got)),
                [shape((z.pair + 2 * CODES, BLOCK), BF16)],
                [],
                [own, gain, acts[0], curs[0], tally, message, partner_message, *got],
            )
    got = share(delta, "col")
    grid = 4
    per_step = slots // grid
    deep = (steps * batch + BLOCK - 1) // BLOCK * BLOCK
    left_shape = shape((2 * z.post, BLOCK, deep), BF16)
    right, later, final_rates = call(
        functools.partial(lay_kernel, z),
        [shape((z.pre, deep, BLOCK), BF16), left_shape, shape((batch, local))],
        [],
        [*xs, *ds, last_rates],
    )
    (extras,) = call(
        functools.partial(extras_kernel, z, len(got)),
        [shape((2 * CODES * z.cols, BLOCK), BF16)],
        [],
        [right, delta, *got],
    )
    all_extras = [extras, flip(extras, "row", 1)] if z.half == 2 else [extras]
    ins = [ids, right, later, delta, *got]
    cost = pl.CostEstimate(
        flops=2 * slots * deep * BLOCK * BLOCK, bytes_accessed=4 * 1024 * 1024, transcendentals=0
    )
    grads = shape((slots, BLOCK, BLOCK), BF16)
    limit = pltpu.CompilerParams(vmem_limit_bytes=24 * 1024 * 1024)
    left, weight_grads = pl.pallas_call(
        functools.partial(grad_kernel, z, len(got), per_step),
        grid=(grid - 1,),
        out_shape=[left_shape, grads],
        in_specs=[VMEM] * len(ins),
        out_specs=[VMEM, pl.BlockSpec((per_step, BLOCK, BLOCK), lambda i: (i, 0, 0))],
        scratch_shapes=[post_sums, pltpu.VMEM((2 * z.post, batch, BLOCK), BF16), *held_ids],
        cost_estimate=cost,
        compiler_params=limit,
    )(*ins)
    ins = [ids, left, right, weight_grads, *all_extras]
    weight_grads, table = pl.pallas_call(
        functools.partial(rest_kernel, z, len(all_extras), slots - per_step, per_step),
        grid=(1,),
        out_shape=[grads, shape((types // BLOCK, BLOCK))],
        in_specs=[VMEM] * 3 + [pl.BlockSpec(memory_space=pl.ANY)] + [VMEM] * len(all_extras),
        out_specs=[pl.BlockSpec((per_step, BLOCK, BLOCK), lambda i: (i + grid - 1, 0, 0)), VMEM],
        scratch_shapes=held_ids,
        input_output_aliases={3: 0},
        cost_estimate=cost,
        compiler_params=limit,
    )(*ins)
    if z.half != 2:
        table = 0.5 * lax.psum(table, "row")
    gain_grads = table.reshape(types)
    return (final_rates, weight_grads.reshape(1, 1, slots, BLOCK, BLOCK), gain_grads)


def solution(mesh):
    in_specs = (
        P("groups", ("row", "col")),
        P(None, "groups", None),
        P(None, "groups", ("row", "col")),
        P("row", "col", None, None, None),
        P("row", "col", None),
        P("row", "col", None),
        P("row", "col", None),
        P(("row", "col")),
        P(),
        P(("row", "col")),
    )
    out_specs = (P("groups", ("row", "col")), P("row", "col", "groups", None, None), P("groups"))
    return jax.shard_map(shards, mesh=mesh, in_specs=in_specs, out_specs=out_specs, check_vma=False)
```

```python
import functools

import jax
import jax.numpy as jnp
from jax import lax
from jax.experimental import pallas as pl
from jax.experimental.pallas import tpu as pltpu
from jax.sharding import PartitionSpec as P

BLOCK = 128
CODES = 16
F32 = jnp.float32
BF16 = jnp.bfloat16
VMEM = pl.BlockSpec(memory_space=pltpu.VMEM)


class Sizes:
    def __init__(self, row_count, col_count, batch, local, slots, types, channels, steps):
        self.rows, self.cols = row_count, col_count
        self.batch, self.local, self.slots = batch, local, slots
        self.types, self.channels, self.steps = types, channels, steps
        self.post = col_count * local // BLOCK
        self.pre = row_count * local // BLOCK
        self.half = row_count // 2
        self.full, self.rest = local // BLOCK, local % BLOCK
        self.groups = BLOCK // self.rest
        self.tall = batch // self.groups
        self.piece = self.full * batch + self.tall
        self.pair = 2 * self.piece
        offsets = [local * i % BLOCK for i in range(max(row_count, col_count))]
        self.frame = (max(offsets) + local + BLOCK - 1) // BLOCK
        self.wide = self.frame * BLOCK
        assert 2 * slots == BLOCK and BLOCK % self.rest == 0 and batch % (8 * self.groups) == 0
        assert self.frame == self.full + 1 and self.pair % 16 == 0

    def first(self, i):
        return lax.div(i * self.local, jnp.int32(BLOCK))

    def offset(self, i):
        return lax.rem(i * self.local, jnp.int32(BLOCK))

    def pack(self, whole):
        parts = [whole[:, i * BLOCK : (i + 1) * BLOCK] for i in range(self.full)]
        tail = whole[:, self.full * BLOCK :]
        lanes = lax.broadcasted_iota(jnp.int32, (self.tall, BLOCK), 1)
        joined = tail[0 : self.tall]
        for g in range(1, self.groups):
            moved = pltpu.roll(tail[g * self.tall : (g + 1) * self.tall], g * self.rest, 1)
            joined = jnp.where(lanes < g * self.rest, joined, moved)
        return jnp.concatenate(parts + [joined], axis=0)

    def unpack(self, piece):
        parts = [piece[i * self.batch : (i + 1) * self.batch] for i in range(self.full)]
        joined = piece[self.full * self.batch :]
        lanes = lax.broadcasted_iota(jnp.int32, (self.tall, BLOCK), 1)
        tails = []
        for g in range(self.groups):
            moved = joined if g == 0 else pltpu.roll(joined, BLOCK - g * self.rest, 1)
            tails.append(jnp.where(lanes < self.rest, moved, 0.0))
        return jnp.concatenate(parts + [jnp.concatenate(tails, axis=0)], axis=1)

    def add_blocks(self, target, base, i, piece):
        turned = pltpu.roll(self.unpack(piece), self.offset(i), 1)
        first = base + self.first(i)
        for f in range(self.frame):
            target[first + f] += turned[:, f * BLOCK : (f + 1) * BLOCK]

    def take_blocks(self, source, base, i):
        first = base + self.first(i)
        blocks = [source[0, first + f] + source[1, first + f] for f in range(self.frame)]
        whole = jnp.concatenate(blocks, axis=1)
        back = lax.rem(self.wide - self.offset(i), jnp.int32(self.wide))
        return self.pack(pltpu.roll(whole, back, 1))


def call(body, outs, scratch, ins, places=None, flops=0, out_specs=None, aliases=None):
    specs = [(places or {}).get(i, VMEM) for i in range(len(ins))]
    moved = sum(x.size * x.dtype.itemsize for x in ins) + sum(x.size * x.dtype.itemsize for x in outs)
    return pl.pallas_call(
        body,
        out_shape=outs,
        in_specs=specs,
        out_specs=out_specs or [VMEM] * len(outs),
        scratch_shapes=scratch,
        cost_estimate=pl.CostEstimate(flops=flops, bytes_accessed=moved, transcendentals=0),
        compiler_params=pltpu.CompilerParams(vmem_limit_bytes=24 * 1024 * 1024),
        input_output_aliases=aliases or {},
    )(*ins)


def shape(dims, kind=F32):
    return jax.ShapeDtypeStruct(tuple(dims), kind)


def flip(x, axis, k):
    count = lax.axis_size(axis)
    return lax.ppermute(x, axis, [(i, i ^ k) for i in range(count)])


def few(count):
    return count <= 4


def order(axis, count):
    return (3, 1, 2) if axis == "row" and count == 4 else tuple(range(count - 1, 0, -1))


def share(x, axis):
    count = lax.axis_size(axis)
    if few(count):
        return [flip(x, axis, k) for k in order(axis, count)[::-1]]
    return [lax.all_gather(x, axis)]


def exchange(parts, axis):
    count = lax.axis_size(axis)
    if len(parts) == count - 1:
        return [flip(part, axis, k) for part, k in zip(parts, order(axis, count))]
    return [lax.all_to_all(parts[0], axis, 0, 0, tiled=True)]


def parcel(count, dims, kind):
    if few(count):
        return [shape(dims, kind)] * (count - 1)
    return [shape((count, *dims), kind)]


def away(refs, axis, count, me, k):
    if few(count):
        return refs[order(axis, count)[::-1].index(k)]
    return refs[0].at[me ^ k]


def parted(refs, axis, count, me, k):
    if few(count):
        return refs[order(axis, count).index(k)]
    return refs[0].at[me ^ k]


def place():
    return lax.axis_index("row"), lax.axis_index("col")


def loop(count, body):
    lax.fori_loop(0, count, lambda i, c: (body(i), c)[1], 0, unroll=count <= 18)


def open_kernel(out):
    out[...] = jnp.zeros_like(out)


def start_kernel(z, after, rates, types, inputs, owner, post, pre, message, own, ids, pad, codes):
    pad[...] = jnp.zeros_like(pad)
    pad[:, 0 : z.local] = rates[...]
    packed = z.pack(pad[...])
    own[...] = packed
    del after
    ids[...] = jnp.concatenate([owner[0] * z.post + post[0], pre[0]], axis=1)
    codes[...] = jnp.full(codes.shape, -BLOCK, jnp.int32)
    codes[0:1, 0 : z.local] = types[...].reshape(1, z.local)
    codes[1:2, 0 : z.local] = inputs[...].reshape(1, z.local)
    number = codes[...]
    high = (lax.shift_right_arithmetic(number, 7) + 1).astype(F32)
    low = (number & 127).astype(F32)
    blocks = []
    for f in range(z.frame):
        for r in range(2):
            lanes = slice(f * BLOCK, (f + 1) * BLOCK)
            blocks += [high[r : r + 1, lanes], low[r : r + 1, lanes]]
    fill = message.shape[0] - z.piece - 4 * z.frame
    extra = jnp.concatenate(blocks + [jnp.zeros((fill, BLOCK), F32)], axis=0)
    message[...] = jnp.concatenate([packed, extra], axis=0).astype(BF16)


def turn_weights_kernel(z, after, weights, out):
    del after

    def one(s):
        out[s] = jnp.transpose(weights[s])

    lax.fori_loop(0, z.slots, lambda i, c: (one(i), c)[1], 0, unroll=8)


def prepare_kernel(z, count, *refs):
    mine, own, cots, table, stimuli = refs[:5]
    got = refs[5 : 5 + count]
    rates, gain, drive, cot_out, pad = refs[5 + count :]
    p, _ = place()
    highs = z.types // BLOCK
    t = jnp.transpose(table[...])
    t1 = t.astype(BF16)
    t2 = (t - t1.astype(F32)).astype(BF16)
    t3 = (t - t1.astype(F32) - t2.astype(F32)).astype(BF16)
    high_ids = lax.broadcasted_iota(jnp.int32, (highs, BLOCK), 0).astype(F32) + 1.0
    low_ids = lax.broadcasted_iota(jnp.int32, (BLOCK, BLOCK), 0).astype(F32)
    channel_ids = lax.broadcasted_iota(jnp.int32, (z.channels, BLOCK), 0).astype(F32)
    stim = stimuli[...]
    for k in range(z.rows):
        ref = mine if k == 0 else away(got, "row", z.rows, p, k)
        rows = slice(k * z.piece, (k + 1) * z.piece)
        message = ref[...].astype(F32)
        gains, drives = [], []
        for f in range(z.frame):
            at = z.piece + 4 * f
            codes = message[at : at + 4]
            pick = (high_ids == codes[0:1]).astype(BF16)
            found = sum(jnp.dot(x, pick, preferred_element_type=F32) for x in (t1, t2, t3))
            line = jnp.sum(jnp.where(low_ids == codes[1:2], found, 0.0), axis=0, keepdims=True)
            gains.append(jnp.broadcast_to(line, (z.batch, BLOCK)))
            channel = (codes[2:3] - 1.0) * BLOCK + codes[3:4]
            chosen = (channel_ids == channel).astype(BF16)
            drives.append(jnp.dot(stim, chosen, preferred_element_type=F32))
        gain[rows] = z.pack(jnp.concatenate(gains, axis=1))
        for step in range(z.steps):
            part = [d[step * z.batch : (step + 1) * z.batch] for d in drives]
            drive[step, rows] = z.pack(jnp.concatenate(part, axis=1))
        rates[rows] = own[...] if k == 0 else message[0 : z.piece]
    pad[...] = jnp.zeros_like(pad)
    for step in range(z.steps):
        pad[:, 0 : z.local] = cots[step]
        cot_out[step] = z.pack(pad[...])


def multiply_forward(z, c, ids, weights, x, total, own, parts):
    total[...] = jnp.zeros_like(total)
    for s in range(z.slots):
        product = jnp.dot(x[ids[0, z.slots + s]], weights[s], preferred_element_type=F32)
        total[s % 2, ids[0, s]] += product
    for k in range(z.cols):
        both = jnp.concatenate(
            [z.take_blocks(total, 0, c ^ k), z.take_blocks(total, z.post, c ^ k)], axis=0
        )
        if k == 0:
            own[...] = both
        else:
            parted(parts, "col", z.cols, c, k)[...] = both.astype(BF16)


def first_kernel(z, count, *refs):
    near_ids, weights, mine = refs[:3]
    got = refs[3 : 3 + count]
    x, own = refs[3 + count : 5 + count]
    parts, (sums, total, ids, sem) = refs[5 + count : -4], refs[-4:]
    bring = pltpu.make_async_copy(near_ids, ids, sem)
    bring.start()
    p, c = place()
    sums[...] = jnp.zeros_like(sums)
    for k in range(z.rows):
        ref = mine if k == 0 else away(got, "row", z.rows, p, k)
        z.add_blocks(sums, 0, p ^ k, ref[...].astype(F32)[0 : z.piece])
    x[...] = sums[...].astype(BF16)
    bring.wait()
    multiply_forward(z, c, ids, weights, x, total, own, parts)


def forward_kernel(z, step, count, *refs):
    near_ids, weights, kept, rates, gain, drive = refs[:6]
    got = refs[6 : 6 + count]
    new, act_pair, cur_pair, x, own = refs[6 + count : 11 + count]
    parts, (sums, total, ids, sem) = refs[11 + count : -4], refs[-4:]
    bring = pltpu.make_async_copy(near_ids, ids, sem)
    bring.start()
    p, c = place()
    sums[...] = jnp.zeros_like(sums)

    def sent(k, side):
        ref = kept if k == 0 else away(got, "row", z.rows, p, k)
        return ref[side * z.piece : (side + 1) * z.piece].astype(F32)

    for k in range(z.rows):
        rows = slice(k * z.piece, (k + 1) * z.piece)
        current = sent(k, 0) + sent(k ^ z.half, 1) + drive[step, rows]
        activity = jnp.tanh(gain[rows] * current)
        fresh = 0.5 * rates[rows] + 0.5 * activity
        new[rows] = fresh
        if k % z.half == 0:
            at = k // z.half * z.piece
            act_pair[at : at + z.piece] = activity
            cur_pair[at : at + z.piece] = current
        z.add_blocks(sums, 0, p ^ k, fresh)
    x[...] = sums[...].astype(BF16)
    bring.wait()
    multiply_forward(z, c, ids, weights, x, total, own, parts)


def sum_kernel(z, count, with_cot, *refs):
    own, got = refs[0], refs[1 : 1 + count]
    kept, message = refs[-2:]
    _, c = place()
    total = own[...]
    for k in range(1, z.cols):
        total = total + parted(got, "col", z.cols, c, k)[...].astype(F32)
    kept[...] = total
    if with_cot:
        cot = refs[1 + count]
        fill = message.shape[0] - z.pair - z.piece
        parts = [total, cot[z.steps - 1], jnp.zeros((fill, BLOCK), F32)]
        total = jnp.concatenate(parts, axis=0)
    message[...] = total.astype(BF16)


def pair_of(z, ref):
    at = z.half * z.piece
    return jnp.concatenate([ref[0 : z.piece], ref[at : at + z.piece]], axis=0)


def turn_kernel(z, kept, theirs, rates, gain, drive, cots, final, message, gain_pair, tally, base):
    other = theirs[...].astype(F32)
    swapped = jnp.concatenate([other[z.piece : z.pair], other[0 : z.piece]], axis=0)
    gains = pair_of(z, gain)
    current = kept[...] + swapped + pair_of(z, drive.at[z.steps - 1])
    activity = jnp.tanh(gains * current)
    fresh = 0.5 * rates[0 : z.piece] + 0.5 * activity[0 : z.piece]
    final[...] = fresh
    mine = cots[z.steps - 1]
    adjoint = jnp.concatenate([mine, other[z.pair : z.pair + z.piece]], axis=0)
    pressure = adjoint * 0.5 * (1.0 - activity * activity)
    message[...] = (gains * pressure).astype(BF16)
    gain_pair[...] = gains
    tally[...] = pressure * current
    base[...] = cots[z.steps - 2] + 0.5 * mine


def gather_post(z, c, mine, got, sums, d):
    sums[...] = jnp.zeros_like(sums)
    for k in range(z.cols):
        pair = (mine if k == 0 else away(got, "col", z.cols, c, k))[...].astype(F32)
        z.add_blocks(sums, 0, c ^ k, pair[0 : z.piece])
        z.add_blocks(sums, z.post, c ^ k, pair[z.piece : z.pair])
    d[...] = sums[...].astype(BF16)


def back_kernel(z, count, *refs):
    near_ids, weights, base, mine = refs[:4]
    got = refs[4 : 4 + count]
    d, own = refs[4 + count : 6 + count]
    parts, (sums, total, ids, sem) = refs[6 + count : -4], refs[-4:]
    bring = pltpu.make_async_copy(near_ids, ids, sem)
    bring.start()
    p, c = place()
    gather_post(z, c, mine, got, sums, d)
    total[...] = jnp.zeros_like(total)
    bring.wait()
    for s in range(z.slots):
        product = jnp.dot(d[ids[0, s]], weights[s], preferred_element_type=F32)
        total[s % 2, ids[0, z.slots + s]] += product
    pieces = [z.take_blocks(total, 0, p ^ k) for k in range(z.rows)]
    for k in range(z.rows):
        other = pieces[k ^ z.half]
        if k == 0:
            own[...] = jnp.concatenate([pieces[0] + base[...], other], axis=0)
        else:
            if k == z.half:
                other = other + base[...]
            both = jnp.concatenate([pieces[k], other], axis=0)
            parted(parts, "row", z.rows, p, k)[...] = both.astype(BF16)


def adjoints(z, own, got):
    p, _ = place()
    total = own[...]
    for k in range(1, z.rows):
        total = total + parted(got, "row", z.rows, p, k)[...].astype(F32)
    return total


def delta_kernel(z, before, count, own, gain, act, cur, tally_in, cots, *refs):
    got, (message, tally, base) = refs[:count], refs[count:]
    adjoint = adjoints(z, own, got)
    activity = act[...]
    pressure = adjoint * 0.5 * (1.0 - activity * activity)
    message[...] = (gain[...] * pressure).astype(BF16)
    tally[...] = tally_in[...] + pressure * cur[...]
    base[...] = cots[before - 1] + 0.5 * adjoint[0 : z.piece]


def last_delta_kernel(z, count, own, gain, act, cur, tally_in, mine, partner, *refs):
    got, message = refs[:count], refs[count]
    adjoint = adjoints(z, own, got)
    activity = act[...]
    pressure = adjoint * 0.5 * (1.0 - activity * activity)
    tally = tally_in[...] + pressure * cur[...]
    rows = [gain[...] * pressure]
    lanes = lax.broadcasted_iota(jnp.int32, (1, BLOCK), 1)
    for side, ref in enumerate((mine, partner)):
        codes = ref[...].astype(F32)[z.piece :]
        begin = side * z.piece
        for f in range(z.frame):
            at = begin + f * z.batch
            if f < z.full:
                g = jnp.sum(tally[at : at + z.batch], axis=0, keepdims=True)
            else:
                packed = jnp.sum(tally[at : at + z.tall], axis=0, keepdims=True)
                g = packed
                for i in range(1, z.groups):
                    g = g + pltpu.roll(packed, BLOCK - i * z.rest, 1)
                g = jnp.where(lanes < z.rest, g, 0.0)
            g1 = g.astype(BF16).astype(F32)
            g2 = (g - g1).astype(BF16).astype(F32)
            rows += [codes[4 * f : 4 * f + 2], g1, g2, g - g1 - g2]
        rows.append(jnp.zeros((CODES - 5 * z.frame, BLOCK), F32))
    message[...] = jnp.concatenate(rows, axis=0).astype(BF16)


def extras_kernel(z, count, right, mine, *refs):
    del right
    got, out = refs[:-1], refs[-1]
    _, c = place()
    for k in range(z.cols):
        ref = mine if k == 0 else away(got, "col", z.cols, c, k)
        out[2 * CODES * k : 2 * CODES * (k + 1)] = ref[z.pair :]


def add_table(z, extras, out):
    highs = z.types // BLOCK
    high_ids = lax.broadcasted_iota(jnp.int32, (highs, BLOCK), 0).astype(F32) + 1.0
    low_ids = lax.broadcasted_iota(jnp.int32, (BLOCK, BLOCK), 1).astype(F32)
    total = jnp.zeros((3 * highs, BLOCK), F32)
    for ref in extras:
        everything = ref[...].astype(F32)
        down = jnp.transpose(everything)
        for side in range(2 * z.cols):
            extra = everything[side * CODES : (side + 1) * CODES]
            for f in range(z.frame):
                at = 5 * f
                low = side * CODES + at + 1
                hit = high_ids == extra[at : at + 1]
                terms = [jnp.where(hit, extra[at + 2 + i : at + 3 + i], 0.0) for i in range(3)]
                left = jnp.concatenate(terms, axis=0).astype(BF16)
                right = (low_ids == down[:, low : low + 1]).astype(BF16)
                total = total + jnp.dot(left, right, preferred_element_type=F32)
    out[...] = total[0:highs] + total[highs : 2 * highs] + total[2 * highs :]


def lay_kernel(z, *refs):
    xs, ds = refs[: z.steps], refs[z.steps : 2 * z.steps - 1]
    last_rates, right, left, final = refs[2 * z.steps - 1 :]
    final[...] = z.unpack(last_rates[...])[:, 0 : z.local]
    n = z.batch
    deep = right.shape[1]
    rest = deep - z.steps * n

    def lay_right(q):
        for t in range(z.steps):
            right[q, t * n : (t + 1) * n] = xs[t][q]
        if rest:
            right[q, z.steps * n :] = jnp.zeros((rest, BLOCK), BF16)

    loop(z.pre, lay_right)

    def lay_left(q):
        parts = [jnp.zeros((n, BLOCK), F32)] + [d[q].astype(F32) for d in ds]
        if rest:
            parts.append(jnp.zeros((rest, BLOCK), F32))
        left[q] = jnp.transpose(jnp.concatenate(parts, axis=0)).astype(BF16)

    loop(2 * z.post, lay_left)


def grad_kernel(z, count, per_step, *refs):
    near_ids, right, later, mine = refs[:4]
    got = refs[4 : 4 + count]
    left, out, sums, d0, ids, sem = refs[4 + count :]
    n = z.batch
    deep = right.shape[1]

    @pl.when(pl.program_id(0) == 0)
    def _():
        bring = pltpu.make_async_copy(near_ids, ids, sem)
        bring.start()
        _, c = place()
        gather_post(z, c, mine, got, sums, d0)
        lanes = lax.broadcasted_iota(jnp.int32, (BLOCK, deep), 1)

        def lay_left(q):
            whole = jnp.concatenate([sums[q], jnp.zeros((deep - n, BLOCK), F32)], axis=0)
            turned = jnp.transpose(whole)
            left[q] = jnp.where(lanes < n, turned, later[q].astype(F32)).astype(BF16)

        loop(2 * z.post, lay_left)
        bring.wait()

    paired_products(z, pl.program_id(0) * per_step, per_step, ids, left, right, out)


def products(z, begin, count, ids, left, right, out):
    for s in range(count):
        product = jnp.dot(
            left[ids[0, begin + s]], right[ids[0, z.slots + begin + s]], preferred_element_type=F32
        )
        out[s] = product.astype(BF16)


def paired_products(z, begin, count, ids, left, right, out):
    for s in range(0, count, 2):
        a, b = begin + s, begin + s + 1
        deltas = jnp.concatenate([left[ids[0, a]], left[ids[0, b]]], axis=1)
        one, two = right[ids[0, z.slots + a]], right[ids[0, z.slots + b]]
        none = jnp.zeros_like(one)
        rates = jnp.concatenate(
            [jnp.concatenate([one, none], axis=1), jnp.concatenate([none, two], axis=1)], axis=0
        )
        product = jnp.dot(deltas, rates, preferred_element_type=F32)
        out[s] = product[:, 0:BLOCK].astype(BF16)
        out[s + 1] = product[:, BLOCK:].astype(BF16)


def rest_kernel(z, count, begin, per_step, near_ids, left, right, grads, *refs):
    del grads
    extras = refs[:count]
    out, table, ids, sem = refs[count:]
    bring = pltpu.make_async_copy(near_ids, ids, sem)
    bring.start()
    add_table(z, extras, table)
    bring.wait()
    products(z, begin + pl.program_id(0) * per_step, per_step, ids, left, right, out)


def shards(
    initial_rates,
    stimuli,
    cotangent,
    weight_blocks,
    slot_owner,
    slot_post,
    slot_pre,
    cell_type,
    type_gain,
    input_map,
):
    batch, local = initial_rates.shape
    slots = weight_blocks.shape[2]
    steps, _, channels = stimuli.shape
    types = type_gain.shape[0]
    z = Sizes(
        lax.axis_size("row"), lax.axis_size("col"), batch, local, slots, types, channels, steps
    )
    pair = (z.pair, BLOCK)
    product_flops = 2 * slots * batch * BLOCK * BLOCK
    opening = (z.piece + 4 * z.frame + 15) // 16 * 16
    closing = (z.pair + z.piece + 15) // 16 * 16

    (opened,) = call(open_kernel, [shape((8, BLOCK))], [], [], flops=4_000_000_000)
    message, own_rates, ids = call(
        functools.partial(start_kernel, z),
        [
            shape((opening, BLOCK), BF16),
            shape((z.piece, BLOCK)),
            shape((1, 2 * slots), jnp.int32),
        ],
        [pltpu.VMEM((batch, z.wide), F32), pltpu.VMEM((8, z.wide), jnp.int32)],
        [opened, initial_rates, cell_type, input_map, slot_owner, slot_post, slot_pre],
    )
    got = share(message, "row")
    weights = weight_blocks.reshape(slots, BLOCK, BLOCK)
    (turned,) = call(
        functools.partial(turn_weights_kernel, z),
        [shape((slots, BLOCK, BLOCK), BF16)],
        [],
        [message, weights],
    )
    held_ids = [pltpu.SMEM((1, 2 * slots), jnp.int32), pltpu.SemaphoreType.DMA]
    if few(z.rows):
        partner_message = away(got, "row", z.rows, None, z.half)
    else:
        partner_message = flip(message, "row", z.half)
    pre_sums = pltpu.VMEM((z.pre, batch, BLOCK), F32)
    post_sums = pltpu.VMEM((2 * z.post, batch, BLOCK), F32)
    pre_totals = pltpu.VMEM((2, z.pre, batch, BLOCK), F32)
    post_totals = pltpu.VMEM((2, 2 * z.post, batch, BLOCK), F32)
    x_shape = shape((z.pre, batch, BLOCK), BF16)
    row_parts = parcel(z.rows, pair, BF16)
    col_parts = [shape(pair), *parcel(z.cols, pair, BF16)]
    x, own, *parts = call(
        functools.partial(first_kernel, z, len(got)),
        [x_shape, *col_parts],
        [pre_sums, post_totals, *held_ids],
        [ids, turned, message, *got],
        flops=product_flops,
    )
    every = (z.rows * z.piece, BLOCK)
    rates, gain, drive, cots = call(
        functools.partial(prepare_kernel, z, len(got)),
        [shape(every), shape(every), shape((steps, *every)), shape((steps, z.piece, BLOCK))],
        [pltpu.VMEM((batch, z.wide), F32)],
        [
            message,
            own_rates,
            cotangent,
            type_gain.reshape(types // BLOCK, BLOCK),
            stimuli.reshape(steps * batch, channels),
            *got,
        ],
    )
    xs, acts, curs = [x], [], []
    for t in range(steps):
        last = t == steps - 1
        got = exchange(parts, "col")
        kept, sent = call(
            functools.partial(sum_kernel, z, len(got), last),
            [shape(pair), shape((closing, BLOCK) if last else pair, BF16)],
            [],
            [own, *got] + ([cots] if last else []),
        )
        if last:
            break
        got = share(sent, "row")
        rates, act, cur, x, own, *parts = call(
            functools.partial(forward_kernel, z, t, len(got)),
            [shape(every), shape(pair), shape(pair), x_shape, *col_parts],
            [pre_sums, post_totals, *held_ids],
            [ids, turned, kept, rates, gain, drive, *got],
            flops=product_flops,
        )
        xs.append(x)
        acts.append(act)
        curs.append(cur)
    theirs = flip(sent, "row", z.half)
    last_rates, delta, gain, tally, base = call(
        functools.partial(turn_kernel, z),
        [
            shape((z.piece, BLOCK)),
            shape(pair, BF16),
            shape(pair),
            shape(pair),
            shape((z.piece, BLOCK)),
        ],
        [],
        [kept, theirs, rates, gain, drive, cots],
    )
    ds = []
    for t in reversed(range(1, steps)):
        got = share(delta, "col")
        d, own, *parts = call(
            functools.partial(back_kernel, z, len(got)),
            [shape((2 * z.post, batch, BLOCK), BF16), shape(pair), *row_parts],
            [post_sums, pre_totals, *held_ids],
            [ids, weights, base, delta, *got],
            flops=product_flops,
        )
        ds.insert(0, d)
        got = exchange(parts, "row")
        before = t - 1
        if before > 0:
            delta, tally, base = call(
                functools.partial(delta_kernel, z, before, len(got)),
                [shape(pair, BF16), shape(pair), shape((z.piece, BLOCK))],
                [],
                [own, gain, acts[before], curs[before], tally, cots, *got],
            )
        else:
            (delta,) = call(
                functools.partial(last_delta_kernel, z, len(got)),
                [shape((z.pair + 2 * CODES, BLOCK), BF16)],
                [],
                [own, gain, acts[0], curs[0], tally, message, partner_message, *got],
            )
    got = share(delta, "col")
    grid = 4
    per_step = slots // grid
    deep = (steps * batch + BLOCK - 1) // BLOCK * BLOCK
    left_shape = shape((2 * z.post, BLOCK, deep), BF16)
    right, later, final_rates = call(
        functools.partial(lay_kernel, z),
        [shape((z.pre, deep, BLOCK), BF16), left_shape, shape((batch, local))],
        [],
        [*xs, *ds, last_rates],
    )
    (extras,) = call(
        functools.partial(extras_kernel, z, len(got)),
        [shape((2 * CODES * z.cols, BLOCK), BF16)],
        [],
        [right, delta, *got],
    )
    all_extras = [extras, flip(extras, "row", 1)] if z.half == 2 else [extras]
    ins = [ids, right, later, delta, *got]
    cost = pl.CostEstimate(
        flops=2 * slots * deep * BLOCK * BLOCK, bytes_accessed=4 * 1024 * 1024, transcendentals=0
    )
    grads = shape((slots, BLOCK, BLOCK), BF16)
    limit = pltpu.CompilerParams(vmem_limit_bytes=24 * 1024 * 1024)
    left, weight_grads = pl.pallas_call(
        functools.partial(grad_kernel, z, len(got), per_step),
        grid=(grid - 1,),
        out_shape=[left_shape, grads],
        in_specs=[VMEM] * len(ins),
        out_specs=[VMEM, pl.BlockSpec((per_step, BLOCK, BLOCK), lambda i: (i, 0, 0))],
        scratch_shapes=[post_sums, pltpu.VMEM((2 * z.post, batch, BLOCK), BF16), *held_ids],
        cost_estimate=cost,
        compiler_params=limit,
    )(*ins)
    ins = [ids, left, right, weight_grads, *all_extras]
    weight_grads, table = pl.pallas_call(
        functools.partial(rest_kernel, z, len(all_extras), slots - per_step, per_step),
        grid=(1,),
        out_shape=[grads, shape((types // BLOCK, BLOCK))],
        in_specs=[VMEM] * 3 + [pl.BlockSpec(memory_space=pl.ANY)] + [VMEM] * len(all_extras),
        out_specs=[pl.BlockSpec((per_step, BLOCK, BLOCK), lambda i: (i + grid - 1, 0, 0)), VMEM],
        scratch_shapes=held_ids,
        input_output_aliases={3: 0},
        cost_estimate=cost,
        compiler_params=limit,
    )(*ins)
    if z.half != 2:
        table = 0.5 * lax.psum(table, "row")
    gain_grads = table.reshape(types)
    return (final_rates, weight_grads.reshape(1, 1, slots, BLOCK, BLOCK), gain_grads)


def solution(mesh):
    in_specs = (
        P("groups", ("row", "col")),
        P(None, "groups", None),
        P(None, "groups", ("row", "col")),
        P("row", "col", None, None, None),
        P("row", "col", None),
        P("row", "col", None),
        P("row", "col", None),
        P(("row", "col")),
        P(),
        P(("row", "col")),
    )
    out_specs = (P("groups", ("row", "col")), P("row", "col", "groups", None, None), P("groups"))
    return jax.shard_map(shards, mesh=mesh, in_specs=in_specs, out_specs=out_specs, check_vma=False)
```

```python
import functools

import jax
import jax.numpy as jnp
from jax import lax
from jax.experimental import pallas as pl
from jax.experimental.pallas import tpu as pltpu
from jax.sharding import PartitionSpec as P

BLOCK = 128
CODES = 16
F32 = jnp.float32
BF16 = jnp.bfloat16
VMEM = pl.BlockSpec(memory_space=pltpu.VMEM)


class Sizes:
    def __init__(self, row_count, col_count, batch, local, slots, types, channels, steps):
        self.rows, self.cols = row_count, col_count
        self.batch, self.local, self.slots = batch, local, slots
        self.types, self.channels, self.steps = types, channels, steps
        self.post = col_count * local // BLOCK
        self.pre = row_count * local // BLOCK
        self.half = row_count // 2
        self.full, self.rest = local // BLOCK, local % BLOCK
        self.groups = BLOCK // self.rest
        self.tall = batch // self.groups
        self.piece = self.full * batch + self.tall
        self.pair = 2 * self.piece
        offsets = [local * i % BLOCK for i in range(max(row_count, col_count))]
        self.frame = (max(offsets) + local + BLOCK - 1) // BLOCK
        self.wide = self.frame * BLOCK
        assert 2 * slots == BLOCK and BLOCK % self.rest == 0 and batch % (8 * self.groups) == 0
        assert self.frame == self.full + 1 and self.pair % 16 == 0

    def first(self, i):
        return lax.div(i * self.local, jnp.int32(BLOCK))

    def offset(self, i):
        return lax.rem(i * self.local, jnp.int32(BLOCK))

    def pack(self, whole):
        parts = [whole[:, i * BLOCK : (i + 1) * BLOCK] for i in range(self.full)]
        tail = whole[:, self.full * BLOCK :]
        lanes = lax.broadcasted_iota(jnp.int32, (self.tall, BLOCK), 1)
        joined = tail[0 : self.tall]
        for g in range(1, self.groups):
            moved = pltpu.roll(tail[g * self.tall : (g + 1) * self.tall], g * self.rest, 1)
            joined = jnp.where(lanes < g * self.rest, joined, moved)
        return jnp.concatenate(parts + [joined], axis=0)

    def unpack(self, piece):
        parts = [piece[i * self.batch : (i + 1) * self.batch] for i in range(self.full)]
        joined = piece[self.full * self.batch :]
        lanes = lax.broadcasted_iota(jnp.int32, (self.tall, BLOCK), 1)
        tails = []
        for g in range(self.groups):
            moved = joined if g == 0 else pltpu.roll(joined, BLOCK - g * self.rest, 1)
            tails.append(jnp.where(lanes < self.rest, moved, 0.0))
        return jnp.concatenate(parts + [jnp.concatenate(tails, axis=0)], axis=1)

    def add_blocks(self, target, base, i, piece):
        turned = pltpu.roll(self.unpack(piece), self.offset(i), 1)
        first = base + self.first(i)
        for f in range(self.frame):
            target[first + f] += turned[:, f * BLOCK : (f + 1) * BLOCK]

    def take_blocks(self, source, base, i):
        first = base + self.first(i)
        whole = jnp.concatenate([source[first + f] for f in range(self.frame)], axis=1)
        back = lax.rem(self.wide - self.offset(i), jnp.int32(self.wide))
        return self.pack(pltpu.roll(whole, back, 1))


def call(body, outs, scratch, ins, places=None, flops=0, out_specs=None, aliases=None):
    specs = [(places or {}).get(i, VMEM) for i in range(len(ins))]
    moved = sum(x.size * x.dtype.itemsize for x in ins) + sum(x.size * x.dtype.itemsize for x in outs)
    return pl.pallas_call(
        body,
        out_shape=outs,
        in_specs=specs,
        out_specs=out_specs or [VMEM] * len(outs),
        scratch_shapes=scratch,
        cost_estimate=pl.CostEstimate(flops=flops, bytes_accessed=moved, transcendentals=0),
        compiler_params=pltpu.CompilerParams(vmem_limit_bytes=24 * 1024 * 1024),
        input_output_aliases=aliases or {},
    )(*ins)


def shape(dims, kind=F32):
    return jax.ShapeDtypeStruct(tuple(dims), kind)


def flip(x, axis, k):
    count = lax.axis_size(axis)
    return lax.ppermute(x, axis, [(i, i ^ k) for i in range(count)])


def few(count):
    return count <= 4


def order(axis, count):
    return (3, 1, 2) if axis == "row" and count == 4 else tuple(range(count - 1, 0, -1))


def share(x, axis):
    count = lax.axis_size(axis)
    if few(count):
        return [flip(x, axis, k) for k in order(axis, count)[::-1]]
    return [lax.all_gather(x, axis)]


def exchange(parts, axis):
    count = lax.axis_size(axis)
    if len(parts) == count - 1:
        return [flip(part, axis, k) for part, k in zip(parts, order(axis, count))]
    return [lax.all_to_all(parts[0], axis, 0, 0, tiled=True)]


def parcel(count, dims, kind):
    if few(count):
        return [shape(dims, kind)] * (count - 1)
    return [shape((count, *dims), kind)]


def away(refs, axis, count, me, k):
    if few(count):
        return refs[order(axis, count)[::-1].index(k)]
    return refs[0].at[me ^ k]


def parted(refs, axis, count, me, k):
    if few(count):
        return refs[order(axis, count).index(k)]
    return refs[0].at[me ^ k]


def place():
    return lax.axis_index("row"), lax.axis_index("col")


def loop(count, body):
    lax.fori_loop(0, count, lambda i, c: (body(i), c)[1], 0, unroll=count <= 18)


def open_kernel(out):
    out[...] = jnp.zeros_like(out)


def start_kernel(z, after, rates, types, inputs, owner, post, pre, message, own, ids, pad, codes):
    pad[...] = jnp.zeros_like(pad)
    pad[:, 0 : z.local] = rates[...]
    packed = z.pack(pad[...])
    own[...] = packed
    del after
    ids[...] = jnp.concatenate([owner[0] * z.post + post[0], pre[0]], axis=1)
    codes[...] = jnp.full(codes.shape, -BLOCK, jnp.int32)
    codes[0:1, 0 : z.local] = types[...].reshape(1, z.local)
    codes[1:2, 0 : z.local] = inputs[...].reshape(1, z.local)
    number = codes[...]
    high = (lax.shift_right_arithmetic(number, 7) + 1).astype(F32)
    low = (number & 127).astype(F32)
    blocks = []
    for f in range(z.frame):
        for r in range(2):
            lanes = slice(f * BLOCK, (f + 1) * BLOCK)
            blocks += [high[r : r + 1, lanes], low[r : r + 1, lanes]]
    fill = message.shape[0] - z.piece - 4 * z.frame
    extra = jnp.concatenate(blocks + [jnp.zeros((fill, BLOCK), F32)], axis=0)
    message[...] = jnp.concatenate([packed, extra], axis=0).astype(BF16)


def turn_weights_kernel(z, after, weights, out):
    del after

    def one(s):
        out[s] = jnp.transpose(weights[s])

    lax.fori_loop(0, z.slots, lambda i, c: (one(i), c)[1], 0, unroll=8)


def prepare_kernel(z, count, *refs):
    mine, own, cots, table, stimuli = refs[:5]
    got = refs[5 : 5 + count]
    rates, gain, drive, cot_out, pad = refs[5 + count :]
    p, _ = place()
    highs = z.types // BLOCK
    t = jnp.transpose(table[...])
    t1 = t.astype(BF16)
    t2 = (t - t1.astype(F32)).astype(BF16)
    t3 = (t - t1.astype(F32) - t2.astype(F32)).astype(BF16)
    high_ids = lax.broadcasted_iota(jnp.int32, (highs, BLOCK), 0).astype(F32) + 1.0
    low_ids = lax.broadcasted_iota(jnp.int32, (BLOCK, BLOCK), 0).astype(F32)
    channel_ids = lax.broadcasted_iota(jnp.int32, (z.channels, BLOCK), 0).astype(F32)
    stim = stimuli[...]
    for k in range(z.rows):
        ref = mine if k == 0 else away(got, "row", z.rows, p, k)
        rows = slice(k * z.piece, (k + 1) * z.piece)
        message = ref[...].astype(F32)
        gains, drives = [], []
        for f in range(z.frame):
            at = z.piece + 4 * f
            codes = message[at : at + 4]
            pick = (high_ids == codes[0:1]).astype(BF16)
            found = sum(jnp.dot(x, pick, preferred_element_type=F32) for x in (t1, t2, t3))
            line = jnp.sum(jnp.where(low_ids == codes[1:2], found, 0.0), axis=0, keepdims=True)
            gains.append(jnp.broadcast_to(line, (z.batch, BLOCK)))
            channel = (codes[2:3] - 1.0) * BLOCK + codes[3:4]
            chosen = (channel_ids == channel).astype(BF16)
            drives.append(jnp.dot(stim, chosen, preferred_element_type=F32))
        gain[rows] = z.pack(jnp.concatenate(gains, axis=1))
        for step in range(z.steps):
            part = [d[step * z.batch : (step + 1) * z.batch] for d in drives]
            drive[step, rows] = z.pack(jnp.concatenate(part, axis=1))
        rates[rows] = own[...] if k == 0 else message[0 : z.piece]
    pad[...] = jnp.zeros_like(pad)
    for step in range(z.steps):
        pad[:, 0 : z.local] = cots[step]
        cot_out[step] = z.pack(pad[...])


def multiply_forward(z, c, ids, weights, x, total, own, parts):
    total[...] = jnp.zeros_like(total)
    for s in range(z.slots):
        total[ids[0, s]] += jnp.dot(x[ids[0, z.slots + s]], weights[s], preferred_element_type=F32)
    for k in range(z.cols):
        both = jnp.concatenate(
            [z.take_blocks(total, 0, c ^ k), z.take_blocks(total, z.post, c ^ k)], axis=0
        )
        if k == 0:
            own[...] = both
        else:
            parted(parts, "col", z.cols, c, k)[...] = both.astype(BF16)


def first_kernel(z, count, *refs):
    near_ids, weights, mine = refs[:3]
    got = refs[3 : 3 + count]
    x, own = refs[3 + count : 5 + count]
    parts, (sums, total, ids, sem) = refs[5 + count : -4], refs[-4:]
    bring = pltpu.make_async_copy(near_ids, ids, sem)
    bring.start()
    p, c = place()
    sums[...] = jnp.zeros_like(sums)
    for k in range(z.rows):
        ref = mine if k == 0 else away(got, "row", z.rows, p, k)
        z.add_blocks(sums, 0, p ^ k, ref[...].astype(F32)[0 : z.piece])
    x[...] = sums[...].astype(BF16)
    bring.wait()
    multiply_forward(z, c, ids, weights, x, total, own, parts)


def forward_kernel(z, step, count, *refs):
    near_ids, weights, kept, rates, gain, drive = refs[:6]
    got = refs[6 : 6 + count]
    new, act_pair, cur_pair, x, own = refs[6 + count : 11 + count]
    parts, (sums, total, ids, sem) = refs[11 + count : -4], refs[-4:]
    bring = pltpu.make_async_copy(near_ids, ids, sem)
    bring.start()
    p, c = place()
    sums[...] = jnp.zeros_like(sums)

    def sent(k, side):
        ref = kept if k == 0 else away(got, "row", z.rows, p, k)
        return ref[side * z.piece : (side + 1) * z.piece].astype(F32)

    for k in range(z.rows):
        rows = slice(k * z.piece, (k + 1) * z.piece)
        current = sent(k, 0) + sent(k ^ z.half, 1) + drive[step, rows]
        activity = jnp.tanh(gain[rows] * current)
        fresh = 0.5 * rates[rows] + 0.5 * activity
        new[rows] = fresh
        if k % z.half == 0:
            at = k // z.half * z.piece
            act_pair[at : at + z.piece] = activity
            cur_pair[at : at + z.piece] = current
        z.add_blocks(sums, 0, p ^ k, fresh)
    x[...] = sums[...].astype(BF16)
    bring.wait()
    multiply_forward(z, c, ids, weights, x, total, own, parts)


def sum_kernel(z, count, with_cot, *refs):
    own, got = refs[0], refs[1 : 1 + count]
    kept, message = refs[-2:]
    _, c = place()
    total = own[...]
    for k in range(1, z.cols):
        total = total + parted(got, "col", z.cols, c, k)[...].astype(F32)
    kept[...] = total
    if with_cot:
        cot = refs[1 + count]
        fill = message.shape[0] - z.pair - z.piece
        parts = [total, cot[z.steps - 1], jnp.zeros((fill, BLOCK), F32)]
        total = jnp.concatenate(parts, axis=0)
    message[...] = total.astype(BF16)


def pair_of(z, ref):
    at = z.half * z.piece
    return jnp.concatenate([ref[0 : z.piece], ref[at : at + z.piece]], axis=0)


def turn_kernel(z, kept, theirs, rates, gain, drive, cots, final, message, gain_pair, tally, base):
    other = theirs[...].astype(F32)
    swapped = jnp.concatenate([other[z.piece : z.pair], other[0 : z.piece]], axis=0)
    gains = pair_of(z, gain)
    current = kept[...] + swapped + pair_of(z, drive.at[z.steps - 1])
    activity = jnp.tanh(gains * current)
    fresh = 0.5 * rates[0 : z.piece] + 0.5 * activity[0 : z.piece]
    final[...] = fresh
    mine = cots[z.steps - 1]
    adjoint = jnp.concatenate([mine, other[z.pair : z.pair + z.piece]], axis=0)
    pressure = adjoint * 0.5 * (1.0 - activity * activity)
    message[...] = (gains * pressure).astype(BF16)
    gain_pair[...] = gains
    tally[...] = pressure * current
    base[...] = cots[z.steps - 2] + 0.5 * mine


def gather_post(z, c, mine, got, sums, d):
    sums[...] = jnp.zeros_like(sums)
    for k in range(z.cols):
        pair = (mine if k == 0 else away(got, "col", z.cols, c, k))[...].astype(F32)
        z.add_blocks(sums, 0, c ^ k, pair[0 : z.piece])
        z.add_blocks(sums, z.post, c ^ k, pair[z.piece : z.pair])
    d[...] = sums[...].astype(BF16)


def back_kernel(z, count, *refs):
    near_ids, weights, base, mine = refs[:4]
    got = refs[4 : 4 + count]
    d, own = refs[4 + count : 6 + count]
    parts, (sums, total, ids, sem) = refs[6 + count : -4], refs[-4:]
    bring = pltpu.make_async_copy(near_ids, ids, sem)
    bring.start()
    p, c = place()
    gather_post(z, c, mine, got, sums, d)
    total[...] = jnp.zeros_like(total)
    bring.wait()
    for s in range(z.slots):
        total[ids[0, z.slots + s]] += jnp.dot(d[ids[0, s]], weights[s], preferred_element_type=F32)
    pieces = [z.take_blocks(total, 0, p ^ k) for k in range(z.rows)]
    for k in range(z.rows):
        other = pieces[k ^ z.half]
        if k == 0:
            own[...] = jnp.concatenate([pieces[0] + base[...], other], axis=0)
        else:
            if k == z.half:
                other = other + base[...]
            both = jnp.concatenate([pieces[k], other], axis=0)
            parted(parts, "row", z.rows, p, k)[...] = both.astype(BF16)


def adjoints(z, own, got):
    p, _ = place()
    total = own[...]
    for k in range(1, z.rows):
        total = total + parted(got, "row", z.rows, p, k)[...].astype(F32)
    return total


def delta_kernel(z, before, count, own, gain, act, cur, tally_in, cots, *refs):
    got, (message, tally, base) = refs[:count], refs[count:]
    adjoint = adjoints(z, own, got)
    activity = act[...]
    pressure = adjoint * 0.5 * (1.0 - activity * activity)
    message[...] = (gain[...] * pressure).astype(BF16)
    tally[...] = tally_in[...] + pressure * cur[...]
    base[...] = cots[before - 1] + 0.5 * adjoint[0 : z.piece]


def last_delta_kernel(z, count, own, gain, act, cur, tally_in, mine, partner, *refs):
    got, message = refs[:count], refs[count]
    adjoint = adjoints(z, own, got)
    activity = act[...]
    pressure = adjoint * 0.5 * (1.0 - activity * activity)
    tally = tally_in[...] + pressure * cur[...]
    rows = [gain[...] * pressure]
    lanes = lax.broadcasted_iota(jnp.int32, (1, BLOCK), 1)
    for side, ref in enumerate((mine, partner)):
        codes = ref[...].astype(F32)[z.piece :]
        begin = side * z.piece
        for f in range(z.frame):
            at = begin + f * z.batch
            if f < z.full:
                g = jnp.sum(tally[at : at + z.batch], axis=0, keepdims=True)
            else:
                packed = jnp.sum(tally[at : at + z.tall], axis=0, keepdims=True)
                g = packed
                for i in range(1, z.groups):
                    g = g + pltpu.roll(packed, BLOCK - i * z.rest, 1)
                g = jnp.where(lanes < z.rest, g, 0.0)
            g1 = g.astype(BF16).astype(F32)
            g2 = (g - g1).astype(BF16).astype(F32)
            rows += [codes[4 * f : 4 * f + 2], g1, g2, g - g1 - g2]
        rows.append(jnp.zeros((CODES - 5 * z.frame, BLOCK), F32))
    message[...] = jnp.concatenate(rows, axis=0).astype(BF16)


def extras_kernel(z, count, right, mine, *refs):
    del right
    got, out = refs[:-1], refs[-1]
    _, c = place()
    for k in range(z.cols):
        ref = mine if k == 0 else away(got, "col", z.cols, c, k)
        out[2 * CODES * k : 2 * CODES * (k + 1)] = ref[z.pair :]


def add_table(z, extras, out):
    highs = z.types // BLOCK
    high_ids = lax.broadcasted_iota(jnp.int32, (highs, BLOCK), 0).astype(F32) + 1.0
    low_ids = lax.broadcasted_iota(jnp.int32, (BLOCK, BLOCK), 1).astype(F32)
    total = jnp.zeros((3 * highs, BLOCK), F32)
    everything = extras[...].astype(F32)
    down = jnp.transpose(everything)
    for side in range(2 * z.cols):
        extra = everything[side * CODES : (side + 1) * CODES]
        for f in range(z.frame):
            at = 5 * f
            low = side * CODES + at + 1
            hit = high_ids == extra[at : at + 1]
            terms = [jnp.where(hit, extra[at + 2 + i : at + 3 + i], 0.0) for i in range(3)]
            left = jnp.concatenate(terms, axis=0).astype(BF16)
            right = (low_ids == down[:, low : low + 1]).astype(BF16)
            total = total + jnp.dot(left, right, preferred_element_type=F32)
    out[...] = total[0:highs] + total[highs : 2 * highs] + total[2 * highs :]


def lay_kernel(z, *refs):
    xs, ds = refs[: z.steps], refs[z.steps : 2 * z.steps - 1]
    last_rates, right, left, final = refs[2 * z.steps - 1 :]
    final[...] = z.unpack(last_rates[...])[:, 0 : z.local]
    n = z.batch
    deep = right.shape[1]
    rest = deep - z.steps * n

    def lay_right(q):
        for t in range(z.steps):
            right[q, t * n : (t + 1) * n] = xs[t][q]
        if rest:
            right[q, z.steps * n :] = jnp.zeros((rest, BLOCK), BF16)

    loop(z.pre, lay_right)

    def lay_left(q):
        parts = [jnp.zeros((n, BLOCK), F32)] + [d[q].astype(F32) for d in ds]
        if rest:
            parts.append(jnp.zeros((rest, BLOCK), F32))
        left[q] = jnp.transpose(jnp.concatenate(parts, axis=0)).astype(BF16)

    loop(2 * z.post, lay_left)


def grad_kernel(z, count, per_step, *refs):
    near_ids, right, later, extras, mine = refs[:5]
    got = refs[5 : 5 + count]
    table, out, left, sums, d0, ids, sem = refs[5 + count :]
    n = z.batch
    deep = right.shape[1]

    @pl.when(pl.program_id(0) == 0)
    def _():
        bring = pltpu.make_async_copy(near_ids, ids, sem)
        bring.start()
        _, c = place()
        add_table(z, extras, table)
        gather_post(z, c, mine, got, sums, d0)
        lanes = lax.broadcasted_iota(jnp.int32, (BLOCK, deep), 1)

        def lay_left(q):
            whole = jnp.concatenate([sums[q], jnp.zeros((deep - n, BLOCK), F32)], axis=0)
            turned = jnp.transpose(whole)
            left[q] = jnp.where(lanes < n, turned, later[q].astype(F32)).astype(BF16)

        loop(2 * z.post, lay_left)
        bring.wait()

    products(z, pl.program_id(0) * per_step, per_step, ids, left, right, out)


def products(z, begin, count, ids, left, right, out):
    for s in range(count):
        product = jnp.dot(
            left[ids[0, begin + s]], right[ids[0, z.slots + begin + s]], preferred_element_type=F32
        )
        out[s] = product.astype(BF16)


def finish_kernel(z, own, extras, table):
    add_table(z, extras, table)
    table[...] += own[...]


def shards(
    initial_rates,
    stimuli,
    cotangent,
    weight_blocks,
    slot_owner,
    slot_post,
    slot_pre,
    cell_type,
    type_gain,
    input_map,
):
    batch, local = initial_rates.shape
    slots = weight_blocks.shape[2]
    steps, _, channels = stimuli.shape
    types = type_gain.shape[0]
    z = Sizes(
        lax.axis_size("row"), lax.axis_size("col"), batch, local, slots, types, channels, steps
    )
    pair = (z.pair, BLOCK)
    product_flops = 2 * slots * batch * BLOCK * BLOCK
    opening = (z.piece + 4 * z.frame + 15) // 16 * 16
    closing = (z.pair + z.piece + 15) // 16 * 16

    (opened,) = call(open_kernel, [shape((8, BLOCK))], [], [], flops=4_000_000_000)
    message, own_rates, ids = call(
        functools.partial(start_kernel, z),
        [
            shape((opening, BLOCK), BF16),
            shape((z.piece, BLOCK)),
            shape((1, 2 * slots), jnp.int32),
        ],
        [pltpu.VMEM((batch, z.wide), F32), pltpu.VMEM((8, z.wide), jnp.int32)],
        [opened, initial_rates, cell_type, input_map, slot_owner, slot_post, slot_pre],
    )
    got = share(message, "row")
    weights = weight_blocks.reshape(slots, BLOCK, BLOCK)
    (turned,) = call(
        functools.partial(turn_weights_kernel, z),
        [shape((slots, BLOCK, BLOCK), BF16)],
        [],
        [message, weights],
    )
    held_ids = [pltpu.SMEM((1, 2 * slots), jnp.int32), pltpu.SemaphoreType.DMA]
    if few(z.rows):
        partner_message = away(got, "row", z.rows, None, z.half)
    else:
        partner_message = flip(message, "row", z.half)
    pre_sums = pltpu.VMEM((z.pre, batch, BLOCK), F32)
    post_sums = pltpu.VMEM((2 * z.post, batch, BLOCK), F32)
    x_shape = shape((z.pre, batch, BLOCK), BF16)
    row_parts = parcel(z.rows, pair, BF16)
    col_parts = [shape(pair), *parcel(z.cols, pair, BF16)]
    x, own, *parts = call(
        functools.partial(first_kernel, z, len(got)),
        [x_shape, *col_parts],
        [pre_sums, post_sums, *held_ids],
        [ids, turned, message, *got],
        flops=product_flops,
    )
    every = (z.rows * z.piece, BLOCK)
    rates, gain, drive, cots = call(
        functools.partial(prepare_kernel, z, len(got)),
        [shape(every), shape(every), shape((steps, *every)), shape((steps, z.piece, BLOCK))],
        [pltpu.VMEM((batch, z.wide), F32)],
        [
            message,
            own_rates,
            cotangent,
            type_gain.reshape(types // BLOCK, BLOCK),
            stimuli.reshape(steps * batch, channels),
            *got,
        ],
    )
    xs, acts, curs = [x], [], []
    for t in range(steps):
        last = t == steps - 1
        got = exchange(parts, "col")
        kept, sent = call(
            functools.partial(sum_kernel, z, len(got), last),
            [shape(pair), shape((closing, BLOCK) if last else pair, BF16)],
            [],
            [own, *got] + ([cots] if last else []),
        )
        if last:
            break
        got = share(sent, "row")
        rates, act, cur, x, own, *parts = call(
            functools.partial(forward_kernel, z, t, len(got)),
            [shape(every), shape(pair), shape(pair), x_shape, *col_parts],
            [pre_sums, post_sums, *held_ids],
            [ids, turned, kept, rates, gain, drive, *got],
            flops=product_flops,
        )
        xs.append(x)
        acts.append(act)
        curs.append(cur)
    theirs = flip(sent, "row", z.half)
    last_rates, delta, gain, tally, base = call(
        functools.partial(turn_kernel, z),
        [
            shape((z.piece, BLOCK)),
            shape(pair, BF16),
            shape(pair),
            shape(pair),
            shape((z.piece, BLOCK)),
        ],
        [],
        [kept, theirs, rates, gain, drive, cots],
    )
    ds = []
    for t in reversed(range(1, steps)):
        got = share(delta, "col")
        d, own, *parts = call(
            functools.partial(back_kernel, z, len(got)),
            [shape((2 * z.post, batch, BLOCK), BF16), shape(pair), *row_parts],
            [post_sums, pre_sums, *held_ids],
            [ids, weights, base, delta, *got],
            flops=product_flops,
        )
        ds.insert(0, d)
        got = exchange(parts, "row")
        before = t - 1
        if before > 0:
            delta, tally, base = call(
                functools.partial(delta_kernel, z, before, len(got)),
                [shape(pair, BF16), shape(pair), shape((z.piece, BLOCK))],
                [],
                [own, gain, acts[before], curs[before], tally, cots, *got],
            )
        else:
            (delta,) = call(
                functools.partial(last_delta_kernel, z, len(got)),
                [shape((z.pair + 2 * CODES, BLOCK), BF16)],
                [],
                [own, gain, acts[0], curs[0], tally, message, partner_message, *got],
            )
    got = share(delta, "col")
    grid = 4
    per_step = slots // grid
    deep = (steps * batch + BLOCK - 1) // BLOCK * BLOCK
    left_shape = shape((2 * z.post, BLOCK, deep), BF16)
    right, later, final_rates = call(
        functools.partial(lay_kernel, z),
        [shape((z.pre, deep, BLOCK), BF16), left_shape, shape((batch, local))],
        [],
        [*xs, *ds, last_rates],
    )
    (extras,) = call(
        functools.partial(extras_kernel, z, len(got)),
        [shape((2 * CODES * z.cols, BLOCK), BF16)],
        [],
        [right, delta, *got],
    )
    if z.half == 2:
        their_extras = flip(extras, "row", 1)
    ins = [ids, right, later, extras, delta, *got]
    cost = pl.CostEstimate(
        flops=2 * slots * deep * BLOCK * BLOCK, bytes_accessed=4 * 1024 * 1024, transcendentals=0
    )
    grads = shape((slots, BLOCK, BLOCK), BF16)
    limit = pltpu.CompilerParams(vmem_limit_bytes=24 * 1024 * 1024)
    table_shape = shape((types // BLOCK, BLOCK))
    table, weight_grads = pl.pallas_call(
        functools.partial(grad_kernel, z, len(got), per_step),
        grid=(grid,),
        out_shape=[table_shape, grads],
        in_specs=[VMEM] * len(ins),
        out_specs=[VMEM, pl.BlockSpec((per_step, BLOCK, BLOCK), lambda i: (i, 0, 0))],
        scratch_shapes=[
            pltpu.VMEM(left_shape.shape, BF16),
            post_sums,
            pltpu.VMEM((2 * z.post, batch, BLOCK), BF16),
            *held_ids,
        ],
        cost_estimate=cost,
        compiler_params=limit,
    )(*ins)
    if z.half == 2:
        (table,) = call(functools.partial(finish_kernel, z), [table_shape], [], [table, their_extras])
    else:
        table = 0.5 * lax.psum(table, "row")
    gain_grads = table.reshape(types)
    return (final_rates, weight_grads.reshape(1, 1, slots, BLOCK, BLOCK), gain_grads)


def solution(mesh):
    in_specs = (
        P("groups", ("row", "col")),
        P(None, "groups", None),
        P(None, "groups", ("row", "col")),
        P("row", "col", None, None, None),
        P("row", "col", None),
        P("row", "col", None),
        P("row", "col", None),
        P(("row", "col")),
        P(),
        P(("row", "col")),
    )
    out_specs = (P("groups", ("row", "col")), P("row", "col", "groups", None, None), P("groups"))
    return jax.shard_map(shards, mesh=mesh, in_specs=in_specs, out_specs=out_specs, check_vma=False)
```

```python
import functools

import jax
import jax.numpy as jnp
from jax import lax
from jax.experimental import pallas as pl
from jax.experimental.pallas import tpu as pltpu
from jax.sharding import PartitionSpec as P

BLOCK = 128
CODES = 16
F32 = jnp.float32
BF16 = jnp.bfloat16
VMEM = pl.BlockSpec(memory_space=pltpu.VMEM)


class Sizes:
    def __init__(self, row_count, col_count, batch, local, slots, types, channels, steps):
        self.rows, self.cols = row_count, col_count
        self.batch, self.local, self.slots = batch, local, slots
        self.types, self.channels, self.steps = types, channels, steps
        self.post = col_count * local // BLOCK
        self.pre = row_count * local // BLOCK
        self.half = row_count // 2
        self.full, self.rest = local // BLOCK, local % BLOCK
        self.groups = BLOCK // self.rest
        self.tall = batch // self.groups
        self.piece = self.full * batch + self.tall
        self.pair = 2 * self.piece
        offsets = [local * i % BLOCK for i in range(max(row_count, col_count))]
        self.frame = (max(offsets) + local + BLOCK - 1) // BLOCK
        self.wide = self.frame * BLOCK
        assert 2 * slots == BLOCK and BLOCK % self.rest == 0 and batch % (8 * self.groups) == 0
        assert self.frame == self.full + 1 and self.pair % 16 == 0

    def first(self, i):
        return lax.div(i * self.local, jnp.int32(BLOCK))

    def offset(self, i):
        return lax.rem(i * self.local, jnp.int32(BLOCK))

    def pack(self, whole):
        parts = [whole[:, i * BLOCK : (i + 1) * BLOCK] for i in range(self.full)]
        tail = whole[:, self.full * BLOCK :]
        lanes = lax.broadcasted_iota(jnp.int32, (self.tall, BLOCK), 1)
        joined = tail[0 : self.tall]
        for g in range(1, self.groups):
            moved = pltpu.roll(tail[g * self.tall : (g + 1) * self.tall], g * self.rest, 1)
            joined = jnp.where(lanes < g * self.rest, joined, moved)
        return jnp.concatenate(parts + [joined], axis=0)

    def unpack(self, piece):
        parts = [piece[i * self.batch : (i + 1) * self.batch] for i in range(self.full)]
        joined = piece[self.full * self.batch :]
        lanes = lax.broadcasted_iota(jnp.int32, (self.tall, BLOCK), 1)
        tails = []
        for g in range(self.groups):
            moved = joined if g == 0 else pltpu.roll(joined, BLOCK - g * self.rest, 1)
            tails.append(jnp.where(lanes < self.rest, moved, 0.0))
        return jnp.concatenate(parts + [jnp.concatenate(tails, axis=0)], axis=1)

    def add_blocks(self, target, base, i, piece):
        turned = pltpu.roll(self.unpack(piece), self.offset(i), 1)
        first = base + self.first(i)
        for f in range(self.frame):
            target[first + f] += turned[:, f * BLOCK : (f + 1) * BLOCK]

    def take_blocks(self, source, base, i):
        first = base + self.first(i)
        whole = jnp.concatenate([source[first + f] for f in range(self.frame)], axis=1)
        back = lax.rem(self.wide - self.offset(i), jnp.int32(self.wide))
        return self.pack(pltpu.roll(whole, back, 1))


def call(body, outs, scratch, ins, places=None, flops=0, out_specs=None, aliases=None):
    specs = [(places or {}).get(i, VMEM) for i in range(len(ins))]
    moved = sum(x.size * x.dtype.itemsize for x in ins) + sum(x.size * x.dtype.itemsize for x in outs)
    return pl.pallas_call(
        body,
        out_shape=outs,
        in_specs=specs,
        out_specs=out_specs or [VMEM] * len(outs),
        scratch_shapes=scratch,
        cost_estimate=pl.CostEstimate(flops=flops, bytes_accessed=moved, transcendentals=0),
        compiler_params=pltpu.CompilerParams(vmem_limit_bytes=24 * 1024 * 1024),
        input_output_aliases=aliases or {},
    )(*ins)


def shape(dims, kind=F32):
    return jax.ShapeDtypeStruct(tuple(dims), kind)


def flip(x, axis, k):
    count = lax.axis_size(axis)
    return lax.ppermute(x, axis, [(i, i ^ k) for i in range(count)])


def few(count):
    return count <= 4


def order(axis, count):
    return (3, 1, 2) if axis == "row" and count == 4 else tuple(range(count - 1, 0, -1))


def share(x, axis):
    count = lax.axis_size(axis)
    if few(count):
        return [flip(x, axis, k) for k in order(axis, count)[::-1]]
    return [lax.all_gather(x, axis)]


def exchange(parts, axis):
    count = lax.axis_size(axis)
    if len(parts) == count - 1:
        return [flip(part, axis, k) for part, k in zip(parts, order(axis, count))]
    return [lax.all_to_all(parts[0], axis, 0, 0, tiled=True)]


def parcel(count, dims, kind):
    if few(count):
        return [shape(dims, kind)] * (count - 1)
    return [shape((count, *dims), kind)]


def away(refs, axis, count, me, k):
    if few(count):
        return refs[order(axis, count)[::-1].index(k)]
    return refs[0].at[me ^ k]


def parted(refs, axis, count, me, k):
    if few(count):
        return refs[order(axis, count).index(k)]
    return refs[0].at[me ^ k]


def place():
    return lax.axis_index("row"), lax.axis_index("col")


def loop(count, body):
    lax.fori_loop(0, count, lambda i, c: (body(i), c)[1], 0, unroll=count <= 18)


def open_kernel(out):
    out[...] = jnp.zeros_like(out)


def start_kernel(z, after, rates, types, inputs, owner, post, pre, message, own, ids, pad, codes):
    pad[...] = jnp.zeros_like(pad)
    pad[:, 0 : z.local] = rates[...]
    packed = z.pack(pad[...])
    own[...] = packed
    del after
    ids[...] = jnp.concatenate([owner[0] * z.post + post[0], pre[0]], axis=1)
    codes[...] = jnp.full(codes.shape, -BLOCK, jnp.int32)
    codes[0:1, 0 : z.local] = types[...].reshape(1, z.local)
    codes[1:2, 0 : z.local] = inputs[...].reshape(1, z.local)
    number = codes[...]
    high = (lax.shift_right_arithmetic(number, 7) + 1).astype(F32)
    low = (number & 127).astype(F32)
    blocks = []
    for f in range(z.frame):
        for r in range(2):
            lanes = slice(f * BLOCK, (f + 1) * BLOCK)
            blocks += [high[r : r + 1, lanes], low[r : r + 1, lanes]]
    fill = message.shape[0] - z.piece - 4 * z.frame
    extra = jnp.concatenate(blocks + [jnp.zeros((fill, BLOCK), F32)], axis=0)
    message[...] = jnp.concatenate([packed, extra], axis=0).astype(BF16)


def turn_weights_kernel(z, after, weights, out):
    del after

    def one(s):
        out[s] = jnp.transpose(weights[s])

    lax.fori_loop(0, z.slots, lambda i, c: (one(i), c)[1], 0, unroll=8)


def prepare_kernel(z, count, *refs):
    mine, own, cots, table, stimuli = refs[:5]
    got = refs[5 : 5 + count]
    rates, gain, drive, cot_out, pad = refs[5 + count :]
    p, _ = place()
    highs = z.types // BLOCK
    t = jnp.transpose(table[...])
    t1 = t.astype(BF16)
    t2 = (t - t1.astype(F32)).astype(BF16)
    t3 = (t - t1.astype(F32) - t2.astype(F32)).astype(BF16)
    high_ids = lax.broadcasted_iota(jnp.int32, (highs, BLOCK), 0).astype(F32) + 1.0
    low_ids = lax.broadcasted_iota(jnp.int32, (BLOCK, BLOCK), 0).astype(F32)
    channel_ids = lax.broadcasted_iota(jnp.int32, (z.channels, BLOCK), 0).astype(F32)
    stim = stimuli[...]
    for k in range(z.rows):
        ref = mine if k == 0 else away(got, "row", z.rows, p, k)
        rows = slice(k * z.piece, (k + 1) * z.piece)
        message = ref[...].astype(F32)
        gains, drives = [], []
        for f in range(z.frame):
            at = z.piece + 4 * f
            codes = message[at : at + 4]
            pick = (high_ids == codes[0:1]).astype(BF16)
            found = sum(jnp.dot(x, pick, preferred_element_type=F32) for x in (t1, t2, t3))
            line = jnp.sum(jnp.where(low_ids == codes[1:2], found, 0.0), axis=0, keepdims=True)
            gains.append(jnp.broadcast_to(line, (z.batch, BLOCK)))
            channel = (codes[2:3] - 1.0) * BLOCK + codes[3:4]
            chosen = (channel_ids == channel).astype(BF16)
            drives.append(jnp.dot(stim, chosen, preferred_element_type=F32))
        gain[rows] = z.pack(jnp.concatenate(gains, axis=1))
        for step in range(z.steps):
            part = [d[step * z.batch : (step + 1) * z.batch] for d in drives]
            drive[step, rows] = z.pack(jnp.concatenate(part, axis=1))
        rates[rows] = own[...] if k == 0 else message[0 : z.piece]
    pad[...] = jnp.zeros_like(pad)
    for step in range(z.steps):
        pad[:, 0 : z.local] = cots[step]
        cot_out[step] = z.pack(pad[...])


def multiply_forward(z, c, ids, weights, x, total, own, parts):
    total[...] = jnp.zeros_like(total)
    for s in range(z.slots):
        total[ids[0, s]] += jnp.dot(x[ids[0, z.slots + s]], weights[s], preferred_element_type=F32)
    for k in range(z.cols):
        both = jnp.concatenate(
            [z.take_blocks(total, 0, c ^ k), z.take_blocks(total, z.post, c ^ k)], axis=0
        )
        if k == 0:
            own[...] = both
        else:
            parted(parts, "col", z.cols, c, k)[...] = both.astype(BF16)


def first_kernel(z, count, *refs):
    near_ids, weights, mine = refs[:3]
    got = refs[3 : 3 + count]
    x, own = refs[3 + count : 5 + count]
    parts, (sums, total, ids, sem) = refs[5 + count : -4], refs[-4:]
    bring = pltpu.make_async_copy(near_ids, ids, sem)
    bring.start()
    p, c = place()
    sums[...] = jnp.zeros_like(sums)
    for k in range(z.rows):
        ref = mine if k == 0 else away(got, "row", z.rows, p, k)
        z.add_blocks(sums, 0, p ^ k, ref[...].astype(F32)[0 : z.piece])
    x[...] = sums[...].astype(BF16)
    bring.wait()
    multiply_forward(z, c, ids, weights, x, total, own, parts)


def forward_kernel(z, step, count, *refs):
    near_ids, weights, kept, rates, gain, drive = refs[:6]
    got = refs[6 : 6 + count]
    new, act_pair, cur_pair, x, own = refs[6 + count : 11 + count]
    parts, (sums, total, ids, sem) = refs[11 + count : -4], refs[-4:]
    bring = pltpu.make_async_copy(near_ids, ids, sem)
    bring.start()
    p, c = place()
    sums[...] = jnp.zeros_like(sums)

    def sent(k, side):
        ref = kept if k == 0 else away(got, "row", z.rows, p, k)
        return ref[side * z.piece : (side + 1) * z.piece].astype(F32)

    for k in range(z.rows):
        rows = slice(k * z.piece, (k + 1) * z.piece)
        current = sent(k, 0) + sent(k ^ z.half, 1) + drive[step, rows]
        activity = jnp.tanh(gain[rows] * current)
        fresh = 0.5 * rates[rows] + 0.5 * activity
        new[rows] = fresh
        if k % z.half == 0:
            at = k // z.half * z.piece
            act_pair[at : at + z.piece] = activity
            cur_pair[at : at + z.piece] = current
        z.add_blocks(sums, 0, p ^ k, fresh)
    x[...] = sums[...].astype(BF16)
    bring.wait()
    multiply_forward(z, c, ids, weights, x, total, own, parts)


def sum_kernel(z, count, with_cot, *refs):
    own, got = refs[0], refs[1 : 1 + count]
    kept, message = refs[-2:]
    _, c = place()
    total = own[...]
    for k in range(1, z.cols):
        total = total + parted(got, "col", z.cols, c, k)[...].astype(F32)
    kept[...] = total
    if with_cot:
        cot = refs[1 + count]
        fill = message.shape[0] - z.pair - z.piece
        parts = [total, cot[z.steps - 1], jnp.zeros((fill, BLOCK), F32)]
        total = jnp.concatenate(parts, axis=0)
    message[...] = total.astype(BF16)


def pair_of(z, ref):
    at = z.half * z.piece
    return jnp.concatenate([ref[0 : z.piece], ref[at : at + z.piece]], axis=0)


def turn_kernel(z, kept, theirs, rates, gain, drive, cots, final, message, gain_pair, tally, base):
    other = theirs[...].astype(F32)
    swapped = jnp.concatenate([other[z.piece : z.pair], other[0 : z.piece]], axis=0)
    gains = pair_of(z, gain)
    current = kept[...] + swapped + pair_of(z, drive.at[z.steps - 1])
    activity = jnp.tanh(gains * current)
    fresh = 0.5 * rates[0 : z.piece] + 0.5 * activity[0 : z.piece]
    final[...] = fresh
    mine = cots[z.steps - 1]
    adjoint = jnp.concatenate([mine, other[z.pair : z.pair + z.piece]], axis=0)
    pressure = adjoint * 0.5 * (1.0 - activity * activity)
    message[...] = (gains * pressure).astype(BF16)
    gain_pair[...] = gains
    tally[...] = pressure * current
    base[...] = cots[z.steps - 2] + 0.5 * mine


def gather_post(z, c, mine, got, sums, d):
    sums[...] = jnp.zeros_like(sums)
    for k in range(z.cols):
        pair = (mine if k == 0 else away(got, "col", z.cols, c, k))[...].astype(F32)
        z.add_blocks(sums, 0, c ^ k, pair[0 : z.piece])
        z.add_blocks(sums, z.post, c ^ k, pair[z.piece : z.pair])
    d[...] = sums[...].astype(BF16)


def back_kernel(z, count, *refs):
    near_ids, weights, base, mine = refs[:4]
    got = refs[4 : 4 + count]
    d, own = refs[4 + count : 6 + count]
    parts, (sums, total, ids, sem) = refs[6 + count : -4], refs[-4:]
    bring = pltpu.make_async_copy(near_ids, ids, sem)
    bring.start()
    p, c = place()
    gather_post(z, c, mine, got, sums, d)
    total[...] = jnp.zeros_like(total)
    bring.wait()
    for s in range(z.slots):
        total[ids[0, z.slots + s]] += jnp.dot(d[ids[0, s]], weights[s], preferred_element_type=F32)
    pieces = [z.take_blocks(total, 0, p ^ k) for k in range(z.rows)]
    for k in range(z.rows):
        other = pieces[k ^ z.half]
        if k == 0:
            own[...] = jnp.concatenate([pieces[0] + base[...], other], axis=0)
        else:
            if k == z.half:
                other = other + base[...]
            both = jnp.concatenate([pieces[k], other], axis=0)
            parted(parts, "row", z.rows, p, k)[...] = both.astype(BF16)


def adjoints(z, own, got):
    p, _ = place()
    total = own[...]
    for k in range(1, z.rows):
        total = total + parted(got, "row", z.rows, p, k)[...].astype(F32)
    return total


def delta_kernel(z, before, count, own, gain, act, cur, tally_in, cots, *refs):
    got, (message, tally, base) = refs[:count], refs[count:]
    adjoint = adjoints(z, own, got)
    activity = act[...]
    pressure = adjoint * 0.5 * (1.0 - activity * activity)
    message[...] = (gain[...] * pressure).astype(BF16)
    tally[...] = tally_in[...] + pressure * cur[...]
    base[...] = cots[before - 1] + 0.5 * adjoint[0 : z.piece]


def last_delta_kernel(z, count, own, gain, act, cur, tally_in, mine, partner, *refs):
    got, message = refs[:count], refs[count]
    adjoint = adjoints(z, own, got)
    activity = act[...]
    pressure = adjoint * 0.5 * (1.0 - activity * activity)
    tally = tally_in[...] + pressure * cur[...]
    rows = [gain[...] * pressure]
    lanes = lax.broadcasted_iota(jnp.int32, (1, BLOCK), 1)
    for side, ref in enumerate((mine, partner)):
        codes = ref[...].astype(F32)[z.piece :]
        begin = side * z.piece
        for f in range(z.frame):
            at = begin + f * z.batch
            if f < z.full:
                g = jnp.sum(tally[at : at + z.batch], axis=0, keepdims=True)
            else:
                packed = jnp.sum(tally[at : at + z.tall], axis=0, keepdims=True)
                g = packed
                for i in range(1, z.groups):
                    g = g + pltpu.roll(packed, BLOCK - i * z.rest, 1)
                g = jnp.where(lanes < z.rest, g, 0.0)
            g1 = g.astype(BF16).astype(F32)
            g2 = (g - g1).astype(BF16).astype(F32)
            rows += [codes[4 * f : 4 * f + 2], g1, g2, g - g1 - g2]
        rows.append(jnp.zeros((CODES - 5 * z.frame, BLOCK), F32))
    message[...] = jnp.concatenate(rows, axis=0).astype(BF16)


def table_kernel(z, count, right, mine, *refs):
    del right
    got, out = refs[:-1], refs[-1]
    _, c = place()
    highs = z.types // BLOCK
    high_ids = lax.broadcasted_iota(jnp.int32, (highs, BLOCK), 0).astype(F32) + 1.0
    low_ids = lax.broadcasted_iota(jnp.int32, (BLOCK, BLOCK), 0).astype(F32)
    total = jnp.zeros((3 * highs, BLOCK), F32)
    for k in range(z.cols):
        ref = mine if k == 0 else away(got, "col", z.cols, c, k)
        extra = ref[z.pair :].astype(F32)
        for side in range(2):
            for f in range(z.frame):
                at = side * CODES + 5 * f
                hit = high_ids == extra[at : at + 1]
                terms = [jnp.where(hit, extra[at + 2 + i : at + 3 + i], 0.0) for i in range(3)]
                left = jnp.concatenate(terms, axis=0).astype(BF16)
                right_side = (low_ids == extra[at + 1 : at + 2]).astype(BF16)
                total = total + lax.dot_general(
                    left, right_side, (((1,), (1,)), ((), ())), preferred_element_type=F32
                )
    out[...] = total[0:highs] + total[highs : 2 * highs] + total[2 * highs :]


def lay_kernel(z, *refs):
    xs, ds = refs[: z.steps], refs[z.steps : 2 * z.steps - 1]
    last_rates, right, left, final = refs[2 * z.steps - 1 :]
    final[...] = z.unpack(last_rates[...])[:, 0 : z.local]
    n = z.batch
    deep = right.shape[1]
    rest = deep - z.steps * n

    def lay_right(q):
        for t in range(z.steps):
            right[q, t * n : (t + 1) * n] = xs[t][q]
        if rest:
            right[q, z.steps * n :] = jnp.zeros((rest, BLOCK), BF16)

    loop(z.pre, lay_right)

    def lay_left(q):
        parts = [jnp.zeros((n, BLOCK), F32)] + [d[q].astype(F32) for d in ds]
        if rest:
            parts.append(jnp.zeros((rest, BLOCK), F32))
        left[q] = jnp.transpose(jnp.concatenate(parts, axis=0)).astype(BF16)

    loop(2 * z.post, lay_left)


def grad_kernel(z, count, per_step, *refs):
    near_ids, right, later, mine = refs[:4]
    got = refs[4 : 4 + count]
    out, left, sums, d0, ids, sem = refs[4 + count :]
    n = z.batch
    deep = right.shape[1]

    @pl.when(pl.program_id(0) == 0)
    def _():
        bring = pltpu.make_async_copy(near_ids, ids, sem)
        bring.start()
        _, c = place()
        gather_post(z, c, mine, got, sums, d0)
        lanes = lax.broadcasted_iota(jnp.int32, (BLOCK, deep), 1)

        def lay_left(q):
            whole = jnp.concatenate([sums[q], jnp.zeros((deep - n, BLOCK), F32)], axis=0)
            turned = jnp.transpose(whole)
            left[q] = jnp.where(lanes < n, turned, later[q].astype(F32)).astype(BF16)

        loop(2 * z.post, lay_left)
        bring.wait()

    products(z, pl.program_id(0) * per_step, per_step, ids, left, right, out)


def products(z, begin, count, ids, left, right, out):
    for s in range(count):
        product = jnp.dot(
            left[ids[0, begin + s]], right[ids[0, z.slots + begin + s]], preferred_element_type=F32
        )
        out[s] = product.astype(BF16)


def shards(
    initial_rates,
    stimuli,
    cotangent,
    weight_blocks,
    slot_owner,
    slot_post,
    slot_pre,
    cell_type,
    type_gain,
    input_map,
):
    batch, local = initial_rates.shape
    slots = weight_blocks.shape[2]
    steps, _, channels = stimuli.shape
    types = type_gain.shape[0]
    z = Sizes(
        lax.axis_size("row"), lax.axis_size("col"), batch, local, slots, types, channels, steps
    )
    pair = (z.pair, BLOCK)
    product_flops = 2 * slots * batch * BLOCK * BLOCK
    opening = (z.piece + 4 * z.frame + 15) // 16 * 16
    closing = (z.pair + z.piece + 15) // 16 * 16

    (opened,) = call(open_kernel, [shape((8, BLOCK))], [], [], flops=4_000_000_000)
    message, own_rates, ids = call(
        functools.partial(start_kernel, z),
        [
            shape((opening, BLOCK), BF16),
            shape((z.piece, BLOCK)),
            shape((1, 2 * slots), jnp.int32),
        ],
        [pltpu.VMEM((batch, z.wide), F32), pltpu.VMEM((8, z.wide), jnp.int32)],
        [opened, initial_rates, cell_type, input_map, slot_owner, slot_post, slot_pre],
    )
    got = share(message, "row")
    weights = weight_blocks.reshape(slots, BLOCK, BLOCK)
    (turned,) = call(
        functools.partial(turn_weights_kernel, z),
        [shape((slots, BLOCK, BLOCK), BF16)],
        [],
        [message, weights],
    )
    held_ids = [pltpu.SMEM((1, 2 * slots), jnp.int32), pltpu.SemaphoreType.DMA]
    if few(z.rows):
        partner_message = away(got, "row", z.rows, None, z.half)
    else:
        partner_message = flip(message, "row", z.half)
    pre_sums = pltpu.VMEM((z.pre, batch, BLOCK), F32)
    post_sums = pltpu.VMEM((2 * z.post, batch, BLOCK), F32)
    x_shape = shape((z.pre, batch, BLOCK), BF16)
    row_parts = parcel(z.rows, pair, BF16)
    col_parts = [shape(pair), *parcel(z.cols, pair, BF16)]
    x, own, *parts = call(
        functools.partial(first_kernel, z, len(got)),
        [x_shape, *col_parts],
        [pre_sums, post_sums, *held_ids],
        [ids, turned, message, *got],
        flops=product_flops,
    )
    every = (z.rows * z.piece, BLOCK)
    rates, gain, drive, cots = call(
        functools.partial(prepare_kernel, z, len(got)),
        [shape(every), shape(every), shape((steps, *every)), shape((steps, z.piece, BLOCK))],
        [pltpu.VMEM((batch, z.wide), F32)],
        [
            message,
            own_rates,
            cotangent,
            type_gain.reshape(types // BLOCK, BLOCK),
            stimuli.reshape(steps * batch, channels),
            *got,
        ],
    )
    xs, acts, curs = [x], [], []
    for t in range(steps):
        last = t == steps - 1
        got = exchange(parts, "col")
        kept, sent = call(
            functools.partial(sum_kernel, z, len(got), last),
            [shape(pair), shape((closing, BLOCK) if last else pair, BF16)],
            [],
            [own, *got] + ([cots] if last else []),
        )
        if last:
            break
        got = share(sent, "row")
        rates, act, cur, x, own, *parts = call(
            functools.partial(forward_kernel, z, t, len(got)),
            [shape(every), shape(pair), shape(pair), x_shape, *col_parts],
            [pre_sums, post_sums, *held_ids],
            [ids, turned, kept, rates, gain, drive, *got],
            flops=product_flops,
        )
        xs.append(x)
        acts.append(act)
        curs.append(cur)
    theirs = flip(sent, "row", z.half)
    last_rates, delta, gain, tally, base = call(
        functools.partial(turn_kernel, z),
        [
            shape((z.piece, BLOCK)),
            shape(pair, BF16),
            shape(pair),
            shape(pair),
            shape((z.piece, BLOCK)),
        ],
        [],
        [kept, theirs, rates, gain, drive, cots],
    )
    ds = []
    for t in reversed(range(1, steps)):
        got = share(delta, "col")
        d, own, *parts = call(
            functools.partial(back_kernel, z, len(got)),
            [shape((2 * z.post, batch, BLOCK), BF16), shape(pair), *row_parts],
            [post_sums, pre_sums, *held_ids],
            [ids, weights, base, delta, *got],
            flops=product_flops,
        )
        ds.insert(0, d)
        got = exchange(parts, "row")
        before = t - 1
        if before > 0:
            delta, tally, base = call(
                functools.partial(delta_kernel, z, before, len(got)),
                [shape(pair, BF16), shape(pair), shape((z.piece, BLOCK))],
                [],
                [own, gain, acts[before], curs[before], tally, cots, *got],
            )
        else:
            (delta,) = call(
                functools.partial(last_delta_kernel, z, len(got)),
                [shape((z.pair + 2 * CODES, BLOCK), BF16)],
                [],
                [own, gain, acts[0], curs[0], tally, message, partner_message, *got],
            )
    got = share(delta, "col")
    grid = 4
    per_step = slots // grid
    deep = (steps * batch + BLOCK - 1) // BLOCK * BLOCK
    left_shape = shape((2 * z.post, BLOCK, deep), BF16)
    right, later, final_rates = call(
        functools.partial(lay_kernel, z),
        [shape((z.pre, deep, BLOCK), BF16), left_shape, shape((batch, local))],
        [],
        [*xs, *ds, last_rates],
    )
    (table,) = call(
        functools.partial(table_kernel, z, len(got)),
        [shape((types // BLOCK, BLOCK))],
        [],
        [right, delta, *got],
    )
    if z.half == 2:
        table = table + flip(table, "row", 1)
    else:
        table = 0.5 * lax.psum(table, "row")
    ins = [ids, right, later, delta, *got]
    cost = pl.CostEstimate(
        flops=2 * slots * deep * BLOCK * BLOCK, bytes_accessed=4 * 1024 * 1024, transcendentals=0
    )
    grads = shape((slots, BLOCK, BLOCK), BF16)
    limit = pltpu.CompilerParams(vmem_limit_bytes=24 * 1024 * 1024)
    weight_grads = pl.pallas_call(
        functools.partial(grad_kernel, z, len(got), per_step),
        grid=(grid,),
        out_shape=grads,
        in_specs=[VMEM] * len(ins),
        out_specs=pl.BlockSpec((per_step, BLOCK, BLOCK), lambda i: (i, 0, 0)),
        scratch_shapes=[
            pltpu.VMEM(left_shape.shape, BF16),
            post_sums,
            pltpu.VMEM((2 * z.post, batch, BLOCK), BF16),
            *held_ids,
        ],
        cost_estimate=cost,
        compiler_params=limit,
    )(*ins)
    gain_grads = table.reshape(types)
    return (final_rates, weight_grads.reshape(1, 1, slots, BLOCK, BLOCK), gain_grads)


def solution(mesh):
    in_specs = (
        P("groups", ("row", "col")),
        P(None, "groups", None),
        P(None, "groups", ("row", "col")),
        P("row", "col", None, None, None),
        P("row", "col", None),
        P("row", "col", None),
        P("row", "col", None),
        P(("row", "col")),
        P(),
        P(("row", "col")),
    )
    out_specs = (P("groups", ("row", "col")), P("row", "col", "groups", None, None), P("groups"))
    return jax.shard_map(shards, mesh=mesh, in_specs=in_specs, out_specs=out_specs, check_vma=False)
```

```python
import functools

import jax
import jax.numpy as jnp
from jax import lax
from jax.experimental import pallas as pl
from jax.experimental.pallas import tpu as pltpu
from jax.sharding import PartitionSpec as P

BLOCK = 128
CODES = 16
F32 = jnp.float32
BF16 = jnp.bfloat16
VMEM = pl.BlockSpec(memory_space=pltpu.VMEM)


class Sizes:
    def __init__(self, row_count, col_count, batch, local, slots, types, channels, steps):
        self.rows, self.cols = row_count, col_count
        self.batch, self.local, self.slots = batch, local, slots
        self.types, self.channels, self.steps = types, channels, steps
        self.post = col_count * local // BLOCK
        self.pre = row_count * local // BLOCK
        self.half = row_count // 2
        self.full, self.rest = local // BLOCK, local % BLOCK
        self.groups = BLOCK // self.rest
        self.tall = batch // self.groups
        self.piece = self.full * batch + self.tall
        self.pair = 2 * self.piece
        offsets = [local * i % BLOCK for i in range(max(row_count, col_count))]
        self.frame = (max(offsets) + local + BLOCK - 1) // BLOCK
        self.wide = self.frame * BLOCK
        assert 2 * slots == BLOCK and BLOCK % self.rest == 0 and batch % (8 * self.groups) == 0
        assert self.frame == self.full + 1 and self.pair % 16 == 0

    def first(self, i):
        return lax.div(i * self.local, jnp.int32(BLOCK))

    def offset(self, i):
        return lax.rem(i * self.local, jnp.int32(BLOCK))

    def pack(self, whole):
        parts = [whole[:, i * BLOCK : (i + 1) * BLOCK] for i in range(self.full)]
        tail = whole[:, self.full * BLOCK :]
        lanes = lax.broadcasted_iota(jnp.int32, (self.tall, BLOCK), 1)
        joined = tail[0 : self.tall]
        for g in range(1, self.groups):
            moved = pltpu.roll(tail[g * self.tall : (g + 1) * self.tall], g * self.rest, 1)
            joined = jnp.where(lanes < g * self.rest, joined, moved)
        return jnp.concatenate(parts + [joined], axis=0)

    def unpack(self, piece):
        parts = [piece[i * self.batch : (i + 1) * self.batch] for i in range(self.full)]
        joined = piece[self.full * self.batch :]
        lanes = lax.broadcasted_iota(jnp.int32, (self.tall, BLOCK), 1)
        tails = []
        for g in range(self.groups):
            moved = joined if g == 0 else pltpu.roll(joined, BLOCK - g * self.rest, 1)
            tails.append(jnp.where(lanes < self.rest, moved, 0.0))
        return jnp.concatenate(parts + [jnp.concatenate(tails, axis=0)], axis=1)

    def add_blocks(self, target, base, i, piece):
        turned = pltpu.roll(self.unpack(piece), self.offset(i), 1)
        first = base + self.first(i)
        for f in range(self.frame):
            target[first + f] += turned[:, f * BLOCK : (f + 1) * BLOCK]

    def take_blocks(self, source, base, i):
        first = base + self.first(i)
        whole = jnp.concatenate([source[first + f] for f in range(self.frame)], axis=1)
        back = lax.rem(self.wide - self.offset(i), jnp.int32(self.wide))
        return self.pack(pltpu.roll(whole, back, 1))


def call(body, outs, scratch, ins, places=None, flops=0, out_specs=None, aliases=None):
    specs = [(places or {}).get(i, VMEM) for i in range(len(ins))]
    moved = sum(x.size * x.dtype.itemsize for x in ins) + sum(x.size * x.dtype.itemsize for x in outs)
    return pl.pallas_call(
        body,
        out_shape=outs,
        in_specs=specs,
        out_specs=out_specs or [VMEM] * len(outs),
        scratch_shapes=scratch,
        cost_estimate=pl.CostEstimate(flops=flops, bytes_accessed=moved, transcendentals=0),
        compiler_params=pltpu.CompilerParams(vmem_limit_bytes=24 * 1024 * 1024),
        input_output_aliases=aliases or {},
    )(*ins)


def shape(dims, kind=F32):
    return jax.ShapeDtypeStruct(tuple(dims), kind)


def flip(x, axis, k):
    count = lax.axis_size(axis)
    return lax.ppermute(x, axis, [(i, i ^ k) for i in range(count)])


def few(count):
    return count <= 4


def order(axis, count):
    return (3, 1, 2) if axis == "row" and count == 4 else tuple(range(count - 1, 0, -1))


def share(x, axis):
    count = lax.axis_size(axis)
    if few(count):
        return [flip(x, axis, k) for k in order(axis, count)[::-1]]
    return [lax.all_gather(x, axis)]


def exchange(parts, axis):
    count = lax.axis_size(axis)
    if len(parts) == count - 1:
        return [flip(part, axis, k) for part, k in zip(parts, order(axis, count))]
    return [lax.all_to_all(parts[0], axis, 0, 0, tiled=True)]


def parcel(count, dims, kind):
    if few(count):
        return [shape(dims, kind)] * (count - 1)
    return [shape((count, *dims), kind)]


def away(refs, axis, count, me, k):
    if few(count):
        return refs[order(axis, count)[::-1].index(k)]
    return refs[0].at[me ^ k]


def parted(refs, axis, count, me, k):
    if few(count):
        return refs[order(axis, count).index(k)]
    return refs[0].at[me ^ k]


def place():
    return lax.axis_index("row"), lax.axis_index("col")


def loop(count, body):
    lax.fori_loop(0, count, lambda i, c: (body(i), c)[1], 0, unroll=count <= 18)


def open_kernel(out):
    out[...] = jnp.zeros_like(out)


def start_kernel(z, after, rates, types, inputs, owner, post, pre, message, own, ids, pad, codes):
    pad[...] = jnp.zeros_like(pad)
    pad[:, 0 : z.local] = rates[...]
    packed = z.pack(pad[...])
    own[...] = packed
    del after
    ids[...] = jnp.concatenate([owner[0] * z.post + post[0], pre[0]], axis=1)
    codes[...] = jnp.full(codes.shape, -BLOCK, jnp.int32)
    codes[0:1, 0 : z.local] = types[...].reshape(1, z.local)
    codes[1:2, 0 : z.local] = inputs[...].reshape(1, z.local)
    number = codes[...]
    high = (lax.shift_right_arithmetic(number, 7) + 1).astype(F32)
    low = (number & 127).astype(F32)
    blocks = []
    for f in range(z.frame):
        for r in range(2):
            lanes = slice(f * BLOCK, (f + 1) * BLOCK)
            blocks += [high[r : r + 1, lanes], low[r : r + 1, lanes]]
    fill = message.shape[0] - z.piece - 4 * z.frame
    extra = jnp.concatenate(blocks + [jnp.zeros((fill, BLOCK), F32)], axis=0)
    message[...] = jnp.concatenate([packed, extra], axis=0).astype(BF16)


def turn_weights_kernel(z, after, weights, out):
    del after

    def one(s):
        out[s] = jnp.transpose(weights[s])

    lax.fori_loop(0, z.slots, lambda i, c: (one(i), c)[1], 0, unroll=8)


def prepare_kernel(z, count, *refs):
    mine, own, cots, table, stimuli = refs[:5]
    got = refs[5 : 5 + count]
    rates, gain, drive, cot_out, pad = refs[5 + count :]
    p, _ = place()
    highs = z.types // BLOCK
    t = jnp.transpose(table[...])
    t1 = t.astype(BF16)
    t2 = (t - t1.astype(F32)).astype(BF16)
    t3 = (t - t1.astype(F32) - t2.astype(F32)).astype(BF16)
    high_ids = lax.broadcasted_iota(jnp.int32, (highs, BLOCK), 0).astype(F32) + 1.0
    low_ids = lax.broadcasted_iota(jnp.int32, (BLOCK, BLOCK), 0).astype(F32)
    channel_ids = lax.broadcasted_iota(jnp.int32, (z.channels, BLOCK), 0).astype(F32)
    stim = stimuli[...]
    for k in range(z.rows):
        ref = mine if k == 0 else away(got, "row", z.rows, p, k)
        rows = slice(k * z.piece, (k + 1) * z.piece)
        message = ref[...].astype(F32)
        gains, drives = [], []
        for f in range(z.frame):
            at = z.piece + 4 * f
            codes = message[at : at + 4]
            pick = (high_ids == codes[0:1]).astype(BF16)
            found = sum(jnp.dot(x, pick, preferred_element_type=F32) for x in (t1, t2, t3))
            line = jnp.sum(jnp.where(low_ids == codes[1:2], found, 0.0), axis=0, keepdims=True)
            gains.append(jnp.broadcast_to(line, (z.batch, BLOCK)))
            channel = (codes[2:3] - 1.0) * BLOCK + codes[3:4]
            chosen = (channel_ids == channel).astype(BF16)
            drives.append(jnp.dot(stim, chosen, preferred_element_type=F32))
        gain[rows] = z.pack(jnp.concatenate(gains, axis=1))
        for step in range(z.steps):
            part = [d[step * z.batch : (step + 1) * z.batch] for d in drives]
            drive[step, rows] = z.pack(jnp.concatenate(part, axis=1))
        rates[rows] = own[...] if k == 0 else message[0 : z.piece]
    pad[...] = jnp.zeros_like(pad)
    for step in range(z.steps):
        pad[:, 0 : z.local] = cots[step]
        cot_out[step] = z.pack(pad[...])


def multiply_forward(z, c, ids, weights, x, total, own, parts):
    total[...] = jnp.zeros_like(total)
    for s in range(z.slots):
        total[ids[0, s]] += jnp.dot(x[ids[0, z.slots + s]], weights[s], preferred_element_type=F32)
    for k in range(z.cols):
        both = jnp.concatenate(
            [z.take_blocks(total, 0, c ^ k), z.take_blocks(total, z.post, c ^ k)], axis=0
        )
        if k == 0:
            own[...] = both
        else:
            parted(parts, "col", z.cols, c, k)[...] = both.astype(BF16)


def first_kernel(z, count, *refs):
    near_ids, weights, mine = refs[:3]
    got = refs[3 : 3 + count]
    x, own = refs[3 + count : 5 + count]
    parts, (sums, total) = refs[5 + count : -2], refs[-2:]
    ids = near_ids[...]
    p, c = place()
    sums[...] = jnp.zeros_like(sums)
    for k in range(z.rows):
        ref = mine if k == 0 else away(got, "row", z.rows, p, k)
        z.add_blocks(sums, 0, p ^ k, ref[...].astype(F32)[0 : z.piece])
    x[...] = sums[...].astype(BF16)
    multiply_forward(z, c, ids, weights, x, total, own, parts)


def forward_kernel(z, step, count, *refs):
    near_ids, weights, kept, rates, gain, drive = refs[:6]
    got = refs[6 : 6 + count]
    new, act_pair, cur_pair, x, own = refs[6 + count : 11 + count]
    parts, (sums, total) = refs[11 + count : -2], refs[-2:]
    ids = near_ids[...]
    p, c = place()
    sums[...] = jnp.zeros_like(sums)

    def sent(k, side):
        ref = kept if k == 0 else away(got, "row", z.rows, p, k)
        return ref[side * z.piece : (side + 1) * z.piece].astype(F32)

    for k in range(z.rows):
        rows = slice(k * z.piece, (k + 1) * z.piece)
        current = sent(k, 0) + sent(k ^ z.half, 1) + drive[step, rows]
        activity = jnp.tanh(gain[rows] * current)
        fresh = 0.5 * rates[rows] + 0.5 * activity
        new[rows] = fresh
        if k % z.half == 0:
            at = k // z.half * z.piece
            act_pair[at : at + z.piece] = activity
            cur_pair[at : at + z.piece] = current
        z.add_blocks(sums, 0, p ^ k, fresh)
    x[...] = sums[...].astype(BF16)
    multiply_forward(z, c, ids, weights, x, total, own, parts)


def sum_kernel(z, count, with_cot, *refs):
    own, got = refs[0], refs[1 : 1 + count]
    kept, message = refs[-2:]
    _, c = place()
    total = own[...]
    for k in range(1, z.cols):
        total = total + parted(got, "col", z.cols, c, k)[...].astype(F32)
    kept[...] = total
    if with_cot:
        cot = refs[1 + count]
        fill = message.shape[0] - z.pair - z.piece
        parts = [total, cot[z.steps - 1], jnp.zeros((fill, BLOCK), F32)]
        total = jnp.concatenate(parts, axis=0)
    message[...] = total.astype(BF16)


def pair_of(z, ref):
    at = z.half * z.piece
    return jnp.concatenate([ref[0 : z.piece], ref[at : at + z.piece]], axis=0)


def turn_kernel(z, kept, theirs, rates, gain, drive, cots, final, message, gain_pair, tally, base):
    other = theirs[...].astype(F32)
    swapped = jnp.concatenate([other[z.piece : z.pair], other[0 : z.piece]], axis=0)
    gains = pair_of(z, gain)
    current = kept[...] + swapped + pair_of(z, drive.at[z.steps - 1])
    activity = jnp.tanh(gains * current)
    fresh = 0.5 * rates[0 : z.piece] + 0.5 * activity[0 : z.piece]
    final[...] = fresh
    mine = cots[z.steps - 1]
    adjoint = jnp.concatenate([mine, other[z.pair : z.pair + z.piece]], axis=0)
    pressure = adjoint * 0.5 * (1.0 - activity * activity)
    message[...] = (gains * pressure).astype(BF16)
    gain_pair[...] = gains
    tally[...] = pressure * current
    base[...] = cots[z.steps - 2] + 0.5 * mine


def gather_post(z, c, mine, got, sums, d):
    sums[...] = jnp.zeros_like(sums)
    for k in range(z.cols):
        pair = (mine if k == 0 else away(got, "col", z.cols, c, k))[...].astype(F32)
        z.add_blocks(sums, 0, c ^ k, pair[0 : z.piece])
        z.add_blocks(sums, z.post, c ^ k, pair[z.piece : z.pair])
    d[...] = sums[...].astype(BF16)


def back_kernel(z, count, *refs):
    near_ids, weights, base, mine = refs[:4]
    got = refs[4 : 4 + count]
    d, own = refs[4 + count : 6 + count]
    parts, (sums, total) = refs[6 + count : -2], refs[-2:]
    ids = near_ids[...]
    p, c = place()
    gather_post(z, c, mine, got, sums, d)
    total[...] = jnp.zeros_like(total)
    for s in range(z.slots):
        total[ids[0, z.slots + s]] += jnp.dot(d[ids[0, s]], weights[s], preferred_element_type=F32)
    pieces = [z.take_blocks(total, 0, p ^ k) for k in range(z.rows)]
    for k in range(z.rows):
        other = pieces[k ^ z.half]
        if k == 0:
            own[...] = jnp.concatenate([pieces[0] + base[...], other], axis=0)
        else:
            if k == z.half:
                other = other + base[...]
            both = jnp.concatenate([pieces[k], other], axis=0)
            parted(parts, "row", z.rows, p, k)[...] = both.astype(BF16)


def adjoints(z, own, got):
    p, _ = place()
    total = own[...]
    for k in range(1, z.rows):
        total = total + parted(got, "row", z.rows, p, k)[...].astype(F32)
    return total


def delta_kernel(z, before, count, own, gain, act, cur, tally_in, cots, *refs):
    got, (message, tally, base) = refs[:count], refs[count:]
    adjoint = adjoints(z, own, got)
    activity = act[...]
    pressure = adjoint * 0.5 * (1.0 - activity * activity)
    message[...] = (gain[...] * pressure).astype(BF16)
    tally[...] = tally_in[...] + pressure * cur[...]
    base[...] = cots[before - 1] + 0.5 * adjoint[0 : z.piece]


def last_delta_kernel(z, count, own, gain, act, cur, tally_in, mine, partner, *refs):
    got, message = refs[:count], refs[count]
    adjoint = adjoints(z, own, got)
    activity = act[...]
    pressure = adjoint * 0.5 * (1.0 - activity * activity)
    tally = tally_in[...] + pressure * cur[...]
    rows = [gain[...] * pressure]
    lanes = lax.broadcasted_iota(jnp.int32, (1, BLOCK), 1)
    for side, ref in enumerate((mine, partner)):
        codes = ref[...].astype(F32)[z.piece :]
        begin = side * z.piece
        for f in range(z.frame):
            at = begin + f * z.batch
            if f < z.full:
                g = jnp.sum(tally[at : at + z.batch], axis=0, keepdims=True)
            else:
                packed = jnp.sum(tally[at : at + z.tall], axis=0, keepdims=True)
                g = packed
                for i in range(1, z.groups):
                    g = g + pltpu.roll(packed, BLOCK - i * z.rest, 1)
                g = jnp.where(lanes < z.rest, g, 0.0)
            g1 = g.astype(BF16).astype(F32)
            g2 = (g - g1).astype(BF16).astype(F32)
            rows += [codes[4 * f : 4 * f + 2], g1, g2, g - g1 - g2]
        rows.append(jnp.zeros((CODES - 5 * z.frame, BLOCK), F32))
    message[...] = jnp.concatenate(rows, axis=0).astype(BF16)


def table_kernel(z, count, right, mine, *refs):
    del right
    got, out = refs[:-1], refs[-1]
    _, c = place()
    highs = z.types // BLOCK
    high_ids = lax.broadcasted_iota(jnp.int32, (highs, BLOCK), 0).astype(F32) + 1.0
    low_ids = lax.broadcasted_iota(jnp.int32, (BLOCK, BLOCK), 0).astype(F32)
    total = jnp.zeros((3 * highs, BLOCK), F32)
    for k in range(z.cols):
        ref = mine if k == 0 else away(got, "col", z.cols, c, k)
        extra = ref[z.pair :].astype(F32)
        for side in range(2):
            for f in range(z.frame):
                at = side * CODES + 5 * f
                hit = high_ids == extra[at : at + 1]
                terms = [jnp.where(hit, extra[at + 2 + i : at + 3 + i], 0.0) for i in range(3)]
                left = jnp.concatenate(terms, axis=0).astype(BF16)
                right_side = (low_ids == extra[at + 1 : at + 2]).astype(BF16)
                total = total + lax.dot_general(
                    left, right_side, (((1,), (1,)), ((), ())), preferred_element_type=F32
                )
    out[...] = total[0:highs] + total[highs : 2 * highs] + total[2 * highs :]


def lay_kernel(z, *refs):
    xs, ds = refs[: z.steps], refs[z.steps : 2 * z.steps - 1]
    last_rates, right, left, final = refs[2 * z.steps - 1 :]
    final[...] = z.unpack(last_rates[...])[:, 0 : z.local]
    n = z.batch
    deep = right.shape[1]
    rest = deep - z.steps * n

    def lay_right(q):
        for t in range(z.steps):
            right[q, t * n : (t + 1) * n] = xs[t][q]
        if rest:
            right[q, z.steps * n :] = jnp.zeros((rest, BLOCK), BF16)

    loop(z.pre, lay_right)

    def lay_left(q):
        parts = [jnp.zeros((n, BLOCK), F32)] + [d[q].astype(F32) for d in ds]
        if rest:
            parts.append(jnp.zeros((rest, BLOCK), F32))
        left[q] = jnp.transpose(jnp.concatenate(parts, axis=0)).astype(BF16)

    loop(2 * z.post, lay_left)


def grad_kernel(z, count, per_step, *refs):
    near_ids, right, later, mine = refs[:4]
    got = refs[4 : 4 + count]
    out, left, sums, d0, ids, sem = refs[4 + count :]
    n = z.batch
    deep = right.shape[1]

    @pl.when(pl.program_id(0) == 0)
    def _():
        bring = pltpu.make_async_copy(near_ids, ids, sem)
        bring.start()
        _, c = place()
        gather_post(z, c, mine, got, sums, d0)
        lanes = lax.broadcasted_iota(jnp.int32, (BLOCK, deep), 1)

        def lay_left(q):
            whole = jnp.concatenate([sums[q], jnp.zeros((deep - n, BLOCK), F32)], axis=0)
            turned = jnp.transpose(whole)
            left[q] = jnp.where(lanes < n, turned, later[q].astype(F32)).astype(BF16)

        loop(2 * z.post, lay_left)
        bring.wait()

    products(z, pl.program_id(0) * per_step, per_step, ids, left, right, out)


def products(z, begin, count, ids, left, right, out):
    for s in range(count):
        product = jnp.dot(
            left[ids[0, begin + s]], right[ids[0, z.slots + begin + s]], preferred_element_type=F32
        )
        out[s] = product.astype(BF16)


def shards(
    initial_rates,
    stimuli,
    cotangent,
    weight_blocks,
    slot_owner,
    slot_post,
    slot_pre,
    cell_type,
    type_gain,
    input_map,
):
    batch, local = initial_rates.shape
    slots = weight_blocks.shape[2]
    steps, _, channels = stimuli.shape
    types = type_gain.shape[0]
    z = Sizes(
        lax.axis_size("row"), lax.axis_size("col"), batch, local, slots, types, channels, steps
    )
    pair = (z.pair, BLOCK)
    product_flops = 2 * slots * batch * BLOCK * BLOCK
    opening = (z.piece + 4 * z.frame + 15) // 16 * 16
    closing = (z.pair + z.piece + 15) // 16 * 16

    (opened,) = call(open_kernel, [shape((8, BLOCK))], [], [], flops=4_000_000_000)
    message, own_rates, ids = call(
        functools.partial(start_kernel, z),
        [
            shape((opening, BLOCK), BF16),
            shape((z.piece, BLOCK)),
            shape((1, 2 * slots), jnp.int32),
        ],
        [pltpu.VMEM((batch, z.wide), F32), pltpu.VMEM((8, z.wide), jnp.int32)],
        [opened, initial_rates, cell_type, input_map, slot_owner, slot_post, slot_pre],
    )
    got = share(message, "row")
    weights = weight_blocks.reshape(slots, BLOCK, BLOCK)
    (turned,) = call(
        functools.partial(turn_weights_kernel, z),
        [shape((slots, BLOCK, BLOCK), BF16)],
        [],
        [message, weights],
    )
    held_ids = [pltpu.SMEM((1, 2 * slots), jnp.int32), pltpu.SemaphoreType.DMA]
    if few(z.rows):
        partner_message = away(got, "row", z.rows, None, z.half)
    else:
        partner_message = flip(message, "row", z.half)
    pre_sums = pltpu.VMEM((z.pre, batch, BLOCK), F32)
    post_sums = pltpu.VMEM((2 * z.post, batch, BLOCK), F32)
    x_shape = shape((z.pre, batch, BLOCK), BF16)
    row_parts = parcel(z.rows, pair, BF16)
    col_parts = [shape(pair), *parcel(z.cols, pair, BF16)]
    x, own, *parts = call(
        functools.partial(first_kernel, z, len(got)),
        [x_shape, *col_parts],
        [pre_sums, post_sums],
        [ids, turned, message, *got],
        flops=product_flops,
    )
    every = (z.rows * z.piece, BLOCK)
    rates, gain, drive, cots = call(
        functools.partial(prepare_kernel, z, len(got)),
        [shape(every), shape(every), shape((steps, *every)), shape((steps, z.piece, BLOCK))],
        [pltpu.VMEM((batch, z.wide), F32)],
        [
            message,
            own_rates,
            cotangent,
            type_gain.reshape(types // BLOCK, BLOCK),
            stimuli.reshape(steps * batch, channels),
            *got,
        ],
    )
    xs, acts, curs = [x], [], []
    for t in range(steps):
        last = t == steps - 1
        got = exchange(parts, "col")
        kept, sent = call(
            functools.partial(sum_kernel, z, len(got), last),
            [shape(pair), shape((closing, BLOCK) if last else pair, BF16)],
            [],
            [own, *got] + ([cots] if last else []),
        )
        if last:
            break
        got = share(sent, "row")
        rates, act, cur, x, own, *parts = call(
            functools.partial(forward_kernel, z, t, len(got)),
            [shape(every), shape(pair), shape(pair), x_shape, *col_parts],
            [pre_sums, post_sums],
            [ids, turned, kept, rates, gain, drive, *got],
            flops=product_flops,
        )
        xs.append(x)
        acts.append(act)
        curs.append(cur)
    theirs = flip(sent, "row", z.half)
    last_rates, delta, gain, tally, base = call(
        functools.partial(turn_kernel, z),
        [
            shape((z.piece, BLOCK)),
            shape(pair, BF16),
            shape(pair),
            shape(pair),
            shape((z.piece, BLOCK)),
        ],
        [],
        [kept, theirs, rates, gain, drive, cots],
    )
    ds = []
    for t in reversed(range(1, steps)):
        got = share(delta, "col")
        d, own, *parts = call(
            functools.partial(back_kernel, z, len(got)),
            [shape((2 * z.post, batch, BLOCK), BF16), shape(pair), *row_parts],
            [post_sums, pre_sums],
            [ids, weights, base, delta, *got],
            flops=product_flops,
        )
        ds.insert(0, d)
        got = exchange(parts, "row")
        before = t - 1
        if before > 0:
            delta, tally, base = call(
                functools.partial(delta_kernel, z, before, len(got)),
                [shape(pair, BF16), shape(pair), shape((z.piece, BLOCK))],
                [],
                [own, gain, acts[before], curs[before], tally, cots, *got],
            )
        else:
            (delta,) = call(
                functools.partial(last_delta_kernel, z, len(got)),
                [shape((z.pair + 2 * CODES, BLOCK), BF16)],
                [],
                [own, gain, acts[0], curs[0], tally, message, partner_message, *got],
            )
    got = share(delta, "col")
    grid = 4
    per_step = slots // grid
    deep = (steps * batch + BLOCK - 1) // BLOCK * BLOCK
    left_shape = shape((2 * z.post, BLOCK, deep), BF16)
    right, later, final_rates = call(
        functools.partial(lay_kernel, z),
        [shape((z.pre, deep, BLOCK), BF16), left_shape, shape((batch, local))],
        [],
        [*xs, *ds, last_rates],
    )
    (table,) = call(
        functools.partial(table_kernel, z, len(got)),
        [shape((types // BLOCK, BLOCK))],
        [],
        [right, delta, *got],
    )
    if z.half == 2:
        table = table + flip(table, "row", 1)
    else:
        table = 0.5 * lax.psum(table, "row")
    ins = [ids, right, later, delta, *got]
    cost = pl.CostEstimate(
        flops=2 * slots * deep * BLOCK * BLOCK, bytes_accessed=4 * 1024 * 1024, transcendentals=0
    )
    grads = shape((slots, BLOCK, BLOCK), BF16)
    limit = pltpu.CompilerParams(vmem_limit_bytes=24 * 1024 * 1024)
    weight_grads = pl.pallas_call(
        functools.partial(grad_kernel, z, len(got), per_step),
        grid=(grid,),
        out_shape=grads,
        in_specs=[VMEM] * len(ins),
        out_specs=pl.BlockSpec((per_step, BLOCK, BLOCK), lambda i: (i, 0, 0)),
        scratch_shapes=[
            pltpu.VMEM(left_shape.shape, BF16),
            post_sums,
            pltpu.VMEM((2 * z.post, batch, BLOCK), BF16),
            *held_ids,
        ],
        cost_estimate=cost,
        compiler_params=limit,
    )(*ins)
    gain_grads = table.reshape(types)
    return (final_rates, weight_grads.reshape(1, 1, slots, BLOCK, BLOCK), gain_grads)


def solution(mesh):
    in_specs = (
        P("groups", ("row", "col")),
        P(None, "groups", None),
        P(None, "groups", ("row", "col")),
        P("row", "col", None, None, None),
        P("row", "col", None),
        P("row", "col", None),
        P("row", "col", None),
        P(("row", "col")),
        P(),
        P(("row", "col")),
    )
    out_specs = (P("groups", ("row", "col")), P("row", "col", "groups", None, None), P("groups"))
    return jax.shard_map(shards, mesh=mesh, in_specs=in_specs, out_specs=out_specs, check_vma=False)
```

```python
import functools

import jax
import jax.numpy as jnp
from jax import lax
from jax.experimental import pallas as pl
from jax.experimental.pallas import tpu as pltpu
from jax.sharding import PartitionSpec as P

BLOCK = 128
CODES = 16
F32 = jnp.float32
BF16 = jnp.bfloat16
VMEM = pl.BlockSpec(memory_space=pltpu.VMEM)


class Sizes:
    def __init__(self, row_count, col_count, batch, local, slots, types, channels, steps):
        self.rows, self.cols = row_count, col_count
        self.batch, self.local, self.slots = batch, local, slots
        self.types, self.channels, self.steps = types, channels, steps
        self.post = col_count * local // BLOCK
        self.pre = row_count * local // BLOCK
        self.half = row_count // 2
        self.full, self.rest = local // BLOCK, local % BLOCK
        self.groups = BLOCK // self.rest
        self.tall = batch // self.groups
        self.piece = self.full * batch + self.tall
        self.pair = 2 * self.piece
        offsets = [local * i % BLOCK for i in range(max(row_count, col_count))]
        self.frame = (max(offsets) + local + BLOCK - 1) // BLOCK
        self.wide = self.frame * BLOCK
        assert 2 * slots == BLOCK and BLOCK % self.rest == 0 and batch % (8 * self.groups) == 0
        assert self.frame == self.full + 1 and self.pair % 16 == 0

    def first(self, i):
        return lax.div(i * self.local, jnp.int32(BLOCK))

    def offset(self, i):
        return lax.rem(i * self.local, jnp.int32(BLOCK))

    def pack(self, whole):
        parts = [whole[:, i * BLOCK : (i + 1) * BLOCK] for i in range(self.full)]
        tail = whole[:, self.full * BLOCK :]
        lanes = lax.broadcasted_iota(jnp.int32, (self.tall, BLOCK), 1)
        joined = tail[0 : self.tall]
        for g in range(1, self.groups):
            moved = pltpu.roll(tail[g * self.tall : (g + 1) * self.tall], g * self.rest, 1)
            joined = jnp.where(lanes < g * self.rest, joined, moved)
        return jnp.concatenate(parts + [joined], axis=0)

    def unpack(self, piece):
        parts = [piece[i * self.batch : (i + 1) * self.batch] for i in range(self.full)]
        joined = piece[self.full * self.batch :]
        lanes = lax.broadcasted_iota(jnp.int32, (self.tall, BLOCK), 1)
        tails = []
        for g in range(self.groups):
            moved = joined if g == 0 else pltpu.roll(joined, BLOCK - g * self.rest, 1)
            tails.append(jnp.where(lanes < self.rest, moved, 0.0))
        return jnp.concatenate(parts + [jnp.concatenate(tails, axis=0)], axis=1)

    def add_blocks(self, target, base, i, piece):
        turned = pltpu.roll(self.unpack(piece), self.offset(i), 1)
        first = base + self.first(i)
        for f in range(self.frame):
            target[first + f] += turned[:, f * BLOCK : (f + 1) * BLOCK]

    def take_blocks(self, source, base, i):
        first = base + self.first(i)
        whole = jnp.concatenate([source[first + f] for f in range(self.frame)], axis=1)
        back = lax.rem(self.wide - self.offset(i), jnp.int32(self.wide))
        return self.pack(pltpu.roll(whole, back, 1))


def call(body, outs, scratch, ins, places=None, flops=0, out_specs=None, aliases=None):
    specs = [(places or {}).get(i, VMEM) for i in range(len(ins))]
    moved = sum(x.size * x.dtype.itemsize for x in ins) + sum(x.size * x.dtype.itemsize for x in outs)
    return pl.pallas_call(
        body,
        out_shape=outs,
        in_specs=specs,
        out_specs=out_specs or [VMEM] * len(outs),
        scratch_shapes=scratch,
        cost_estimate=pl.CostEstimate(flops=flops, bytes_accessed=moved, transcendentals=0),
        compiler_params=pltpu.CompilerParams(vmem_limit_bytes=24 * 1024 * 1024),
        input_output_aliases=aliases or {},
    )(*ins)


def shape(dims, kind=F32):
    return jax.ShapeDtypeStruct(tuple(dims), kind)


def flip(x, axis, k):
    count = lax.axis_size(axis)
    return lax.ppermute(x, axis, [(i, i ^ k) for i in range(count)])


def few(count):
    return count <= 4


def order(axis, count):
    return (3, 1, 2) if axis == "row" and count == 4 else tuple(range(count - 1, 0, -1))


def share(x, axis):
    count = lax.axis_size(axis)
    if few(count):
        return [flip(x, axis, k) for k in order(axis, count)[::-1]]
    return [lax.all_gather(x, axis)]


def exchange(parts, axis):
    count = lax.axis_size(axis)
    if len(parts) == count - 1:
        return [flip(part, axis, k) for part, k in zip(parts, order(axis, count))]
    return [lax.all_to_all(parts[0], axis, 0, 0, tiled=True)]


def parcel(count, dims, kind):
    if few(count):
        return [shape(dims, kind)] * (count - 1)
    return [shape((count, *dims), kind)]


def away(refs, axis, count, me, k):
    if few(count):
        return refs[order(axis, count)[::-1].index(k)]
    return refs[0].at[me ^ k]


def parted(refs, axis, count, me, k):
    if few(count):
        return refs[order(axis, count).index(k)]
    return refs[0].at[me ^ k]


def place():
    return lax.axis_index("row"), lax.axis_index("col")


def loop(count, body):
    lax.fori_loop(0, count, lambda i, c: (body(i), c)[1], 0, unroll=count <= 18)


def open_kernel(out):
    out[...] = jnp.zeros_like(out)


def start_kernel(z, after, rates, types, inputs, owner, post, pre, message, own, ids, pad, codes):
    pad[...] = jnp.zeros_like(pad)
    pad[:, 0 : z.local] = rates[...]
    packed = z.pack(pad[...])
    own[...] = packed
    del after
    ids[...] = jnp.concatenate([owner[0] * z.post + post[0], pre[0]], axis=1)
    codes[...] = jnp.full(codes.shape, -BLOCK, jnp.int32)
    codes[0:1, 0 : z.local] = types[...].reshape(1, z.local)
    codes[1:2, 0 : z.local] = inputs[...].reshape(1, z.local)
    number = codes[...]
    high = (lax.shift_right_arithmetic(number, 7) + 1).astype(F32)
    low = (number & 127).astype(F32)
    blocks = []
    for f in range(z.frame):
        for r in range(2):
            lanes = slice(f * BLOCK, (f + 1) * BLOCK)
            blocks += [high[r : r + 1, lanes], low[r : r + 1, lanes]]
    fill = message.shape[0] - z.piece - 4 * z.frame
    extra = jnp.concatenate(blocks + [jnp.zeros((fill, BLOCK), F32)], axis=0)
    message[...] = jnp.concatenate([packed, extra], axis=0).astype(BF16)


def turn_weights_kernel(z, after, weights, out):
    del after

    def one(s):
        out[s] = jnp.transpose(weights[s])

    lax.fori_loop(0, z.slots, lambda i, c: (one(i), c)[1], 0, unroll=8)


def prepare_kernel(z, count, *refs):
    mine, own, cots, table, stimuli = refs[:5]
    got = refs[5 : 5 + count]
    rates, gain, drive, cot_out, pad = refs[5 + count :]
    p, _ = place()
    highs = z.types // BLOCK
    t = jnp.transpose(table[...])
    t1 = t.astype(BF16)
    t2 = (t - t1.astype(F32)).astype(BF16)
    t3 = (t - t1.astype(F32) - t2.astype(F32)).astype(BF16)
    high_ids = lax.broadcasted_iota(jnp.int32, (highs, BLOCK), 0).astype(F32) + 1.0
    low_ids = lax.broadcasted_iota(jnp.int32, (BLOCK, BLOCK), 0).astype(F32)
    channel_ids = lax.broadcasted_iota(jnp.int32, (z.channels, BLOCK), 0).astype(F32)
    stim = stimuli[...]
    for k in range(z.rows):
        ref = mine if k == 0 else away(got, "row", z.rows, p, k)
        rows = slice(k * z.piece, (k + 1) * z.piece)
        message = ref[...].astype(F32)
        gains, drives = [], []
        for f in range(z.frame):
            at = z.piece + 4 * f
            codes = message[at : at + 4]
            pick = (high_ids == codes[0:1]).astype(BF16)
            found = sum(jnp.dot(x, pick, preferred_element_type=F32) for x in (t1, t2, t3))
            line = jnp.sum(jnp.where(low_ids == codes[1:2], found, 0.0), axis=0, keepdims=True)
            gains.append(jnp.broadcast_to(line, (z.batch, BLOCK)))
            channel = (codes[2:3] - 1.0) * BLOCK + codes[3:4]
            chosen = (channel_ids == channel).astype(BF16)
            drives.append(jnp.dot(stim, chosen, preferred_element_type=F32))
        gain[rows] = z.pack(jnp.concatenate(gains, axis=1))
        for step in range(z.steps):
            part = [d[step * z.batch : (step + 1) * z.batch] for d in drives]
            drive[step, rows] = z.pack(jnp.concatenate(part, axis=1))
        rates[rows] = own[...] if k == 0 else message[0 : z.piece]
    pad[...] = jnp.zeros_like(pad)
    for step in range(z.steps):
        pad[:, 0 : z.local] = cots[step]
        cot_out[step] = z.pack(pad[...])


def multiply_forward(z, c, ids, weights, x, total, own, parts):
    total[...] = jnp.zeros_like(total)
    for s in range(z.slots):
        total[ids[0, s]] += jnp.dot(x[ids[0, z.slots + s]], weights[s], preferred_element_type=F32)
    for k in range(z.cols):
        both = jnp.concatenate(
            [z.take_blocks(total, 0, c ^ k), z.take_blocks(total, z.post, c ^ k)], axis=0
        )
        if k == 0:
            own[...] = both
        else:
            parted(parts, "col", z.cols, c, k)[...] = both.astype(BF16)


def first_kernel(z, count, *refs):
    near_ids, weights, mine = refs[:3]
    got = refs[3 : 3 + count]
    x, own = refs[3 + count : 5 + count]
    parts, (sums, total) = refs[5 + count : -2], refs[-2:]
    ids = near_ids[...]
    p, c = place()
    sums[...] = jnp.zeros_like(sums)
    for k in range(z.rows):
        ref = mine if k == 0 else away(got, "row", z.rows, p, k)
        z.add_blocks(sums, 0, p ^ k, ref[...].astype(F32)[0 : z.piece])
    x[...] = sums[...].astype(BF16)
    multiply_forward(z, c, ids, weights, x, total, own, parts)


def forward_kernel(z, step, count, *refs):
    near_ids, weights, kept, rates, gain, drive = refs[:6]
    got = refs[6 : 6 + count]
    new, act_pair, cur_pair, x, own = refs[6 + count : 11 + count]
    parts, (sums, total) = refs[11 + count : -2], refs[-2:]
    ids = near_ids[...]
    p, c = place()
    sums[...] = jnp.zeros_like(sums)

    def sent(k, side):
        ref = kept if k == 0 else away(got, "row", z.rows, p, k)
        return ref[side * z.piece : (side + 1) * z.piece].astype(F32)

    for k in range(z.rows):
        rows = slice(k * z.piece, (k + 1) * z.piece)
        current = sent(k, 0) + sent(k ^ z.half, 1) + drive[step, rows]
        activity = jnp.tanh(gain[rows] * current)
        fresh = 0.5 * rates[rows] + 0.5 * activity
        new[rows] = fresh
        if k % z.half == 0:
            at = k // z.half * z.piece
            act_pair[at : at + z.piece] = activity
            cur_pair[at : at + z.piece] = current
        z.add_blocks(sums, 0, p ^ k, fresh)
    x[...] = sums[...].astype(BF16)
    multiply_forward(z, c, ids, weights, x, total, own, parts)


def sum_kernel(z, count, with_cot, *refs):
    own, got = refs[0], refs[1 : 1 + count]
    kept, message = refs[-2:]
    _, c = place()
    total = own[...]
    for k in range(1, z.cols):
        total = total + parted(got, "col", z.cols, c, k)[...].astype(F32)
    kept[...] = total
    if with_cot:
        cot = refs[1 + count]
        fill = message.shape[0] - z.pair - z.piece
        parts = [total, cot[z.steps - 1], jnp.zeros((fill, BLOCK), F32)]
        total = jnp.concatenate(parts, axis=0)
    message[...] = total.astype(BF16)


def pair_of(z, ref):
    at = z.half * z.piece
    return jnp.concatenate([ref[0 : z.piece], ref[at : at + z.piece]], axis=0)


def turn_kernel(z, kept, theirs, rates, gain, drive, cots, final, message, gain_pair, tally, base):
    other = theirs[...].astype(F32)
    swapped = jnp.concatenate([other[z.piece : z.pair], other[0 : z.piece]], axis=0)
    gains = pair_of(z, gain)
    current = kept[...] + swapped + pair_of(z, drive.at[z.steps - 1])
    activity = jnp.tanh(gains * current)
    fresh = 0.5 * rates[0 : z.piece] + 0.5 * activity[0 : z.piece]
    final[...] = fresh
    mine = cots[z.steps - 1]
    adjoint = jnp.concatenate([mine, other[z.pair : z.pair + z.piece]], axis=0)
    pressure = adjoint * 0.5 * (1.0 - activity * activity)
    message[...] = (gains * pressure).astype(BF16)
    gain_pair[...] = gains
    tally[...] = pressure * current
    base[...] = cots[z.steps - 2] + 0.5 * mine


def gather_post(z, c, mine, got, sums, d):
    sums[...] = jnp.zeros_like(sums)
    for k in range(z.cols):
        pair = (mine if k == 0 else away(got, "col", z.cols, c, k))[...].astype(F32)
        z.add_blocks(sums, 0, c ^ k, pair[0 : z.piece])
        z.add_blocks(sums, z.post, c ^ k, pair[z.piece : z.pair])
    d[...] = sums[...].astype(BF16)


def back_kernel(z, count, *refs):
    near_ids, weights, base, mine = refs[:4]
    got = refs[4 : 4 + count]
    d, own = refs[4 + count : 6 + count]
    parts, (sums, total) = refs[6 + count : -2], refs[-2:]
    ids = near_ids[...]
    p, c = place()
    gather_post(z, c, mine, got, sums, d)
    total[...] = jnp.zeros_like(total)
    for s in range(z.slots):
        total[ids[0, z.slots + s]] += jnp.dot(d[ids[0, s]], weights[s], preferred_element_type=F32)
    pieces = [z.take_blocks(total, 0, p ^ k) for k in range(z.rows)]
    for k in range(z.rows):
        other = pieces[k ^ z.half]
        if k == 0:
            own[...] = jnp.concatenate([pieces[0] + base[...], other], axis=0)
        else:
            if k == z.half:
                other = other + base[...]
            both = jnp.concatenate([pieces[k], other], axis=0)
            parted(parts, "row", z.rows, p, k)[...] = both.astype(BF16)


def adjoints(z, own, got):
    p, _ = place()
    total = own[...]
    for k in range(1, z.rows):
        total = total + parted(got, "row", z.rows, p, k)[...].astype(F32)
    return total


def delta_kernel(z, before, count, own, gain, act, cur, tally_in, cots, *refs):
    got, (message, tally, base) = refs[:count], refs[count:]
    adjoint = adjoints(z, own, got)
    activity = act[...]
    pressure = adjoint * 0.5 * (1.0 - activity * activity)
    message[...] = (gain[...] * pressure).astype(BF16)
    tally[...] = tally_in[...] + pressure * cur[...]
    base[...] = cots[before - 1] + 0.5 * adjoint[0 : z.piece]


def last_delta_kernel(z, count, own, gain, act, cur, tally_in, mine, partner, *refs):
    got, message = refs[:count], refs[count]
    adjoint = adjoints(z, own, got)
    activity = act[...]
    pressure = adjoint * 0.5 * (1.0 - activity * activity)
    tally = tally_in[...] + pressure * cur[...]
    rows = [gain[...] * pressure]
    lanes = lax.broadcasted_iota(jnp.int32, (1, BLOCK), 1)
    for side, ref in enumerate((mine, partner)):
        codes = ref[...].astype(F32)[z.piece :]
        begin = side * z.piece
        for f in range(z.frame):
            at = begin + f * z.batch
            if f < z.full:
                g = jnp.sum(tally[at : at + z.batch], axis=0, keepdims=True)
            else:
                packed = jnp.sum(tally[at : at + z.tall], axis=0, keepdims=True)
                g = packed
                for i in range(1, z.groups):
                    g = g + pltpu.roll(packed, BLOCK - i * z.rest, 1)
                g = jnp.where(lanes < z.rest, g, 0.0)
            g1 = g.astype(BF16).astype(F32)
            g2 = (g - g1).astype(BF16).astype(F32)
            rows += [codes[4 * f : 4 * f + 2], g1, g2, g - g1 - g2]
        rows.append(jnp.zeros((CODES - 5 * z.frame, BLOCK), F32))
    message[...] = jnp.concatenate(rows, axis=0).astype(BF16)


def table_kernel(z, count, right, mine, *refs):
    del right
    got, out = refs[:-1], refs[-1]
    _, c = place()
    highs = z.types // BLOCK
    high_ids = lax.broadcasted_iota(jnp.int32, (highs, BLOCK), 0).astype(F32) + 1.0
    low_ids = lax.broadcasted_iota(jnp.int32, (BLOCK, BLOCK), 0).astype(F32)
    total = jnp.zeros((3 * highs, BLOCK), F32)
    for k in range(z.cols):
        ref = mine if k == 0 else away(got, "col", z.cols, c, k)
        extra = ref[z.pair :].astype(F32)
        for side in range(2):
            for f in range(z.frame):
                at = side * CODES + 5 * f
                hit = high_ids == extra[at : at + 1]
                terms = [jnp.where(hit, extra[at + 2 + i : at + 3 + i], 0.0) for i in range(3)]
                left = jnp.concatenate(terms, axis=0).astype(BF16)
                right_side = (low_ids == extra[at + 1 : at + 2]).astype(BF16)
                total = total + lax.dot_general(
                    left, right_side, (((1,), (1,)), ((), ())), preferred_element_type=F32
                )
    out[...] = total[0:highs] + total[highs : 2 * highs] + total[2 * highs :]


def lay_kernel(z, *refs):
    xs, ds = refs[: z.steps], refs[z.steps : 2 * z.steps - 1]
    last_rates, right, left, final = refs[2 * z.steps - 1 :]
    final[...] = z.unpack(last_rates[...])[:, 0 : z.local]
    n = z.batch
    deep = right.shape[1]
    rest = deep - z.steps * n

    def lay_right(q):
        for t in range(z.steps):
            right[q, t * n : (t + 1) * n] = xs[t][q]
        if rest:
            right[q, z.steps * n :] = jnp.zeros((rest, BLOCK), BF16)

    loop(z.pre, lay_right)

    def lay_left(q):
        parts = [jnp.zeros((n, BLOCK), F32)] + [d[q].astype(F32) for d in ds]
        if rest:
            parts.append(jnp.zeros((rest, BLOCK), F32))
        left[q] = jnp.transpose(jnp.concatenate(parts, axis=0)).astype(BF16)

    loop(2 * z.post, lay_left)


def grad_kernel(z, count, per_step, *refs):
    near_ids, right, later, mine = refs[:4]
    got = refs[4 : 4 + count]
    out, left, sums, d0 = refs[4 + count :]
    n = z.batch
    deep = right.shape[1]

    @pl.when(pl.program_id(0) == 0)
    def _():
        _, c = place()
        gather_post(z, c, mine, got, sums, d0)
        lanes = lax.broadcasted_iota(jnp.int32, (BLOCK, deep), 1)

        def lay_left(q):
            whole = jnp.concatenate([sums[q], jnp.zeros((deep - n, BLOCK), F32)], axis=0)
            turned = jnp.transpose(whole)
            left[q] = jnp.where(lanes < n, turned, later[q].astype(F32)).astype(BF16)

        loop(2 * z.post, lay_left)

    for begin in range(0, z.slots, per_step):

        @pl.when(pl.program_id(0) == begin // per_step)
        def _(begin=begin):
            products(z, begin, per_step, near_ids[...], left, right, out)


def products(z, begin, count, ids, left, right, out):
    for s in range(count):
        product = jnp.dot(
            left[ids[0, begin + s]], right[ids[0, z.slots + begin + s]], preferred_element_type=F32
        )
        out[s] = product.astype(BF16)


def shards(
    initial_rates,
    stimuli,
    cotangent,
    weight_blocks,
    slot_owner,
    slot_post,
    slot_pre,
    cell_type,
    type_gain,
    input_map,
):
    batch, local = initial_rates.shape
    slots = weight_blocks.shape[2]
    steps, _, channels = stimuli.shape
    types = type_gain.shape[0]
    z = Sizes(
        lax.axis_size("row"), lax.axis_size("col"), batch, local, slots, types, channels, steps
    )
    pair = (z.pair, BLOCK)
    product_flops = 2 * slots * batch * BLOCK * BLOCK
    opening = (z.piece + 4 * z.frame + 15) // 16 * 16
    closing = (z.pair + z.piece + 15) // 16 * 16

    (opened,) = call(open_kernel, [shape((8, BLOCK))], [], [], flops=4_000_000_000)
    message, own_rates, ids = call(
        functools.partial(start_kernel, z),
        [
            shape((opening, BLOCK), BF16),
            shape((z.piece, BLOCK)),
            shape((1, 2 * slots), jnp.int32),
        ],
        [pltpu.VMEM((batch, z.wide), F32), pltpu.VMEM((8, z.wide), jnp.int32)],
        [opened, initial_rates, cell_type, input_map, slot_owner, slot_post, slot_pre],
    )
    got = share(message, "row")
    weights = weight_blocks.reshape(slots, BLOCK, BLOCK)
    (turned,) = call(
        functools.partial(turn_weights_kernel, z),
        [shape((slots, BLOCK, BLOCK), BF16)],
        [],
        [message, weights],
    )
    if few(z.rows):
        partner_message = away(got, "row", z.rows, None, z.half)
    else:
        partner_message = flip(message, "row", z.half)
    pre_sums = pltpu.VMEM((z.pre, batch, BLOCK), F32)
    post_sums = pltpu.VMEM((2 * z.post, batch, BLOCK), F32)
    x_shape = shape((z.pre, batch, BLOCK), BF16)
    row_parts = parcel(z.rows, pair, BF16)
    col_parts = [shape(pair), *parcel(z.cols, pair, BF16)]
    x, own, *parts = call(
        functools.partial(first_kernel, z, len(got)),
        [x_shape, *col_parts],
        [pre_sums, post_sums],
        [ids, turned, message, *got],
        flops=product_flops,
    )
    every = (z.rows * z.piece, BLOCK)
    rates, gain, drive, cots = call(
        functools.partial(prepare_kernel, z, len(got)),
        [shape(every), shape(every), shape((steps, *every)), shape((steps, z.piece, BLOCK))],
        [pltpu.VMEM((batch, z.wide), F32)],
        [
            message,
            own_rates,
            cotangent,
            type_gain.reshape(types // BLOCK, BLOCK),
            stimuli.reshape(steps * batch, channels),
            *got,
        ],
    )
    xs, acts, curs = [x], [], []
    for t in range(steps):
        last = t == steps - 1
        got = exchange(parts, "col")
        kept, sent = call(
            functools.partial(sum_kernel, z, len(got), last),
            [shape(pair), shape((closing, BLOCK) if last else pair, BF16)],
            [],
            [own, *got] + ([cots] if last else []),
        )
        if last:
            break
        got = share(sent, "row")
        rates, act, cur, x, own, *parts = call(
            functools.partial(forward_kernel, z, t, len(got)),
            [shape(every), shape(pair), shape(pair), x_shape, *col_parts],
            [pre_sums, post_sums],
            [ids, turned, kept, rates, gain, drive, *got],
            flops=product_flops,
        )
        xs.append(x)
        acts.append(act)
        curs.append(cur)
    theirs = flip(sent, "row", z.half)
    last_rates, delta, gain, tally, base = call(
        functools.partial(turn_kernel, z),
        [
            shape((z.piece, BLOCK)),
            shape(pair, BF16),
            shape(pair),
            shape(pair),
            shape((z.piece, BLOCK)),
        ],
        [],
        [kept, theirs, rates, gain, drive, cots],
    )
    ds = []
    for t in reversed(range(1, steps)):
        got = share(delta, "col")
        d, own, *parts = call(
            functools.partial(back_kernel, z, len(got)),
            [shape((2 * z.post, batch, BLOCK), BF16), shape(pair), *row_parts],
            [post_sums, pre_sums],
            [ids, weights, base, delta, *got],
            flops=product_flops,
        )
        ds.insert(0, d)
        got = exchange(parts, "row")
        before = t - 1
        if before > 0:
            delta, tally, base = call(
                functools.partial(delta_kernel, z, before, len(got)),
                [shape(pair, BF16), shape(pair), shape((z.piece, BLOCK))],
                [],
                [own, gain, acts[before], curs[before], tally, cots, *got],
            )
        else:
            (delta,) = call(
                functools.partial(last_delta_kernel, z, len(got)),
                [shape((z.pair + 2 * CODES, BLOCK), BF16)],
                [],
                [own, gain, acts[0], curs[0], tally, message, partner_message, *got],
            )
    got = share(delta, "col")
    grid = 4
    per_step = slots // grid
    deep = (steps * batch + BLOCK - 1) // BLOCK * BLOCK
    left_shape = shape((2 * z.post, BLOCK, deep), BF16)
    right, later, final_rates = call(
        functools.partial(lay_kernel, z),
        [shape((z.pre, deep, BLOCK), BF16), left_shape, shape((batch, local))],
        [],
        [*xs, *ds, last_rates],
    )
    (table,) = call(
        functools.partial(table_kernel, z, len(got)),
        [shape((types // BLOCK, BLOCK))],
        [],
        [right, delta, *got],
    )
    if z.half == 2:
        table = table + flip(table, "row", 1)
    else:
        table = 0.5 * lax.psum(table, "row")
    ins = [ids, right, later, delta, *got]
    cost = pl.CostEstimate(
        flops=2 * slots * deep * BLOCK * BLOCK, bytes_accessed=4 * 1024 * 1024, transcendentals=0
    )
    grads = shape((slots, BLOCK, BLOCK), BF16)
    limit = pltpu.CompilerParams(vmem_limit_bytes=24 * 1024 * 1024)
    weight_grads = pl.pallas_call(
        functools.partial(grad_kernel, z, len(got), per_step),
        grid=(grid,),
        out_shape=grads,
        in_specs=[VMEM] * len(ins),
        out_specs=pl.BlockSpec((per_step, BLOCK, BLOCK), lambda i: (i, 0, 0)),
        scratch_shapes=[
            pltpu.VMEM(left_shape.shape, BF16),
            post_sums,
            pltpu.VMEM((2 * z.post, batch, BLOCK), BF16),
        ],
        cost_estimate=cost,
        compiler_params=limit,
    )(*ins)
    gain_grads = table.reshape(types)
    return (final_rates, weight_grads.reshape(1, 1, slots, BLOCK, BLOCK), gain_grads)


def solution(mesh):
    in_specs = (
        P("groups", ("row", "col")),
        P(None, "groups", None),
        P(None, "groups", ("row", "col")),
        P("row", "col", None, None, None),
        P("row", "col", None),
        P("row", "col", None),
        P("row", "col", None),
        P(("row", "col")),
        P(),
        P(("row", "col")),
    )
    out_specs = (P("groups", ("row", "col")), P("row", "col", "groups", None, None), P("groups"))
    return jax.shard_map(shards, mesh=mesh, in_specs=in_specs, out_specs=out_specs, check_vma=False)
```
